128 devices in a mesh: genome: 32 (over z, y, core), indiv: 4 (over x).
Axes of the slice: x: 4, y: 4, z: 4, core: 2. Of those that a mesh axis runs over, the one named last changes fastest.
Arguments:
- indiv_factors: float32 [8192, 256], P('indiv'), may hold values from -1.5 to 1.5
- variant_factors: float32 [32768, 256], P('genome'), may hold values from -1.5 to 1.5
- dosage_tiles: bfloat16 [32, 4, 64, 128, 128], P('genome', 'indiv'), may hold values from -6 to 6
- block_rows: int32 [32, 4, 64], P('genome', 'indiv'), may hold values from 0 to 15, as said below
- block_cols: int32 [32, 4, 64], P('genome', 'indiv'), may hold values from 0 to 7, as said below
- live_blocks: int32 [32, 4], P('genome', 'indiv'), may hold values from 1 to 64, as said below
Outputs:
- variant_new: float32 [32768, 256], P('genome')
- indiv_new: float32 [8192, 256], P('indiv')
The draws below stay inside these ranges and needn't reach their ends.
Inputs may be any that keep to these rules, and one draw needn't show every extreme that they name: `block_rows`: block row of each slot, counted in blocks of 128 individuals inside the slot's row group; the live slots of one slab and group name distinct (row, column) pairs. `block_cols`: block column of each slot, counted in blocks of 128 variants inside the slot's slab. Slots below live_blocks[g, i] are typed and the later ones are ignored; in every draw some slab and group has all 64 slots typed.
All inputs are finite; a program needn't handle non-finite values.
Results may differ from the reference program's by a relative error of at most 0.003.
The reference program's roundings to bfloat16 on the way (of `indiv_round` and `variant_round`) count: a program that leaves them out, or rounds other values in their place, can miss the bound.
Values may be sent and summed in bfloat16 or wider, within the bound.
No kernel may reach another device: no remote copies, remote signals or barrier semaphores. Data moves between devices by JAX's collectives and lax.ppermute only.
A program may use at most 128 MiB of HBM per device.

```python
import jax
import jax.numpy as jnp
from jax import lax

R = 256
BS = 128
CG_STEPS = 2
I_DEV = 2048
V_DEV = 1024
NB = 64
GSLABS = 32
IGROUPS = 4
NI = 8192
NV = 32768


def block_plan(key):
    col_count = V_DEV // BS
    cell_count = I_DEV // BS * col_count
    devices = GSLABS * IGROUPS
    split_keys = jax.random.split(key, 4)
    partial_counts = jax.random.randint(split_keys[0], (devices,), max(1, NB // 8), NB // 2 + 1)
    dense_slab = jax.random.randint(split_keys[1], (GSLABS, 1), 0, 4) == 0
    dense_slab = jnp.broadcast_to(dense_slab, (GSLABS, IGROUPS)).reshape(devices)
    chosen_one = jax.random.randint(split_keys[2], (), 0, devices)
    filled = dense_slab | (jnp.arange(devices, dtype=jnp.int32) == chosen_one)
    live_count = jnp.where(filled, NB, partial_counts).astype(jnp.int32)
    device_keys = jax.random.split(split_keys[3], devices)
    picked = jax.vmap(lambda one_key: jnp.sort(jax.random.permutation(one_key, cell_count)[:NB]))(device_keys)
    picked = picked.reshape(GSLABS, IGROUPS, NB).astype(jnp.int32)
    return (live_count.reshape(GSLABS, IGROUPS), picked, col_count)


def draw_block_rows(key, part):
    live_count, picked, col_count = block_plan(key)
    return (picked // col_count).astype(jnp.int32)


def draw_block_cols(key, part):
    live_count, picked, col_count = block_plan(key)
    return (picked % col_count).astype(jnp.int32)


def draw_live_blocks(key, part):
    live_count, picked, col_count = block_plan(key)
    return live_count.astype(jnp.int32)


def draw_dosage_tiles(key, part):
    key = jax.random.fold_in(key, 7)
    shape = (GSLABS, IGROUPS, NB, BS, BS)
    position = jnp.arange(IGROUPS, dtype=jnp.float32) / max(IGROUPS - 1, 1)
    values = jax.random.normal(key, shape, jnp.float32)
    scales = 0.6 * 3.3 ** position
    values = values * scales[None, :, None, None, None]
    return jnp.clip(values, -6.0, 6.0).astype(jnp.bfloat16)


def steps_of(stream_key, dims, cuts, smallest, high):
    factor_of, own = 1.0, jax.random.fold_in(stream_key, 6)
    for axis_at, shards_of in cuts:
        steps = jnp.exp(jax.random.uniform(jax.random.fold_in(own, axis_at), (shards_of,), jnp.float32, smallest / len(cuts), high / len(cuts)))
        factor_of = factor_of * jnp.repeat(steps, dims[axis_at] // shards_of).reshape([-1 if axis == axis_at else 1 for axis in range(len(dims))])
    return factor_of


def scatter_about(own_key, extent, deviation, reach, cuts=(), held_as=jnp.bfloat16):
    gain = steps_of(own_key, extent, cuts, -0.22, 0.18) if cuts else 1.0
    entries = jax.random.normal(own_key, extent, jnp.float32) * deviation * gain
    return jnp.minimum(jnp.maximum(entries, -reach), reach).astype(held_as)


def setup_inputs(seed: int = 0) -> dict:
    arg_keys = jax.random.split(jax.random.key(seed), 7)
    indiv_factors = scatter_about(arg_keys[0], (NI, R), 0.25, 1.5, ((0, 4),), jnp.float32)
    variant_factors = scatter_about(arg_keys[1], (NV, R), 0.25, 1.5, ((0, 32),), jnp.float32)
    dosage_tiles = draw_dosage_tiles(jax.random.fold_in(arg_keys[6], 71), 0)
    block_rows = draw_block_rows(jax.random.fold_in(arg_keys[6], 71), 0)
    block_cols = draw_block_cols(jax.random.fold_in(arg_keys[6], 71), 0)
    live_blocks = draw_live_blocks(jax.random.fold_in(arg_keys[6], 71), 0)
    return {"indiv_factors": indiv_factors, "variant_factors": variant_factors, "dosage_tiles": dosage_tiles, "block_rows": block_rows, "block_cols": block_cols, "live_blocks": live_blocks}


smooth_weight = 32.0
ridge_weight = 1.0


def device_term(left_blocks, right_blocks, tiles, row_ids, col_ids, live_count, subtract, to_left):
    left_part = left_blocks[row_ids].astype(jnp.float32)
    right_part = right_blocks[col_ids].astype(jnp.float32)
    product = jnp.einsum("sir,sjr->sij", left_part, right_part)
    if subtract:
        product = product - tiles.astype(jnp.float32)
    keeping = jnp.arange(row_ids.shape[0], dtype=jnp.int32) < live_count
    masked = jnp.where(keeping[:, None, None], product, 0.0)
    if to_left:
        contrib = jnp.einsum("sij,sjr->sir", masked, right_part)
        return jnp.zeros(left_blocks.shape, jnp.float32).at[row_ids].add(contrib)
    contrib = jnp.einsum("sij,sir->sjr", masked, left_part)
    return jnp.zeros(right_blocks.shape, jnp.float32).at[col_ids].add(contrib)


def data_term(left_all, right_all, dosage_tiles, block_rows, block_cols, live_blocks, subtract, to_left):
    def single(slab, group):
        return device_term(left_all[group], right_all[slab], dosage_tiles[slab, group],
                           block_rows[slab, group], block_cols[slab, group], live_blocks[slab, group],
                           subtract, to_left)

    if to_left:
        def per_group(group):
            def accumulate(slab, running):
                return running + single(slab, group)
            return lax.fori_loop(0, GSLABS, accumulate, jnp.zeros(left_all.shape[1:], jnp.float32))
        return lax.map(per_group, jnp.arange(IGROUPS, dtype=jnp.int32))

    def per_slab(slab):
        def accumulate(group, running):
            return running + single(slab, group)
        return lax.fori_loop(0, IGROUPS, accumulate, jnp.zeros(right_all.shape[1:], jnp.float32))
    return lax.map(per_slab, jnp.arange(GSLABS, dtype=jnp.int32))


def blocked(values, groups):
    return values.astype(jnp.bfloat16).reshape(groups, -1, BS, R)


def banded(values):
    padded = jnp.pad(values, ((1, 1), (0, 0)))
    return 2.0 * values - padded[:-2] - padded[2:]


def conjugate(start, operator):
    resid = -operator(start, True)
    direction = resid
    solution = start
    norm_now = jnp.sum(resid * resid)
    for turn_index in range(CG_STEPS):
        applied = operator(direction, False)
        step_size = norm_now / jnp.sum(direction * applied)
        solution = solution + step_size * direction
        resid = resid - step_size * applied
        norm_next = jnp.sum(resid * resid)
        direction = resid + (norm_next / norm_now) * direction
        norm_now = norm_next
    return solution


def reference(indiv_factors, variant_factors, dosage_tiles, block_rows, block_cols, live_blocks):
    indiv_round = blocked(indiv_factors, IGROUPS)

    def variant_apply(direction, subtract):
        partial_term = data_term(indiv_round, blocked(direction, GSLABS), dosage_tiles, block_rows,
                                 block_cols, live_blocks, subtract, False).reshape(NV, R)
        return partial_term + smooth_weight * banded(direction) + ridge_weight * direction

    variant_new = conjugate(variant_factors, variant_apply)
    variant_round = blocked(variant_new, GSLABS)

    def indiv_apply(direction, subtract):
        partial_term = data_term(blocked(direction, IGROUPS), variant_round, dosage_tiles, block_rows,
                                 block_cols, live_blocks, subtract, True).reshape(NI, R)
        return partial_term + ridge_weight * direction

    indiv_new = conjugate(indiv_factors, indiv_apply)
    return variant_new, indiv_new
```

```python
import jax
import jax.numpy as jnp
import numpy as np
from jax import lax
from jax.experimental import pallas as pl
from jax.experimental.pallas import tpu as pltpu
from jax.sharding import Mesh
from jax.sharding import PartitionSpec as P

BS = 128
R = 256
ROWS = 16
COLS = 8
smooth_weight = 32.0
ridge_weight = 1.0
f32, bf16, f16 = jnp.float32, jnp.bfloat16, jnp.float16
ALL = ("z", "y", "c", "x")
GEN = ("z", "y", "c")
CHIP = ("z", "y")
PAY_V = 2 * BS + 2 * BS + 16
PAY_I = BS + 8
VMEM_LIMIT = 48 * 1024 * 1024


def params():
    return pltpu.CompilerParams(vmem_limit_bytes=VMEM_LIMIT)


def smem():
    return pl.BlockSpec(memory_space=pltpu.SMEM)


def vmem():
    return pl.BlockSpec(memory_space=pltpu.VMEM)


def row_col():
    rows = lax.broadcasted_iota(jnp.int32, (BS, BS), 0)
    cols = lax.broadcasted_iota(jnp.int32, (BS, BS), 1)
    return rows, cols


def pack(gram):
    rows, cols = row_col()
    upper = gram[:BS, :BS]
    lower = gram[BS:, BS:]
    mixed = jnp.where(rows <= cols, upper, lower)
    diag = jnp.sum(jnp.where(rows == cols, lower, 0.0), axis=0, keepdims=True)
    return mixed, gram[:BS, BS:], diag


def unpack(mixed, cross, diag):
    rows, cols = row_col()
    turned = mixed.T
    upper = jnp.where(rows <= cols, mixed, turned)
    lower = jnp.where(rows > cols, mixed, jnp.where(rows < cols, turned, diag))
    top = jnp.concatenate([upper, cross], axis=1)
    bottom = jnp.concatenate([cross.T, lower], axis=1)
    return jnp.concatenate([top, bottom], axis=0)


def split(matrix):
    high = matrix.astype(bf16)
    return high, (matrix - high.astype(f32)).astype(bf16)


def times(values, high, low):
    rounded = values.astype(bf16)
    return jnp.dot(rounded, high, preferred_element_type=f32) + jnp.dot(
        rounded, low, preferred_element_type=f32
    )


def set_mask(row_ids, col_ids, live, mask):
    def clear(k, carry):
        mask[k] = 0.0
        return carry

    lax.fori_loop(0, ROWS * COLS, clear, 0)

    def mark(s, carry):
        mask[row_ids[s] * COLS + col_ids[s]] = 1.0
        return carry

    lax.fori_loop(0, live, mark, 0)


def variant_sums(row_ids, col_ids, meta, tiles, factors, pay, turned, rounded, grams, diags, mask):
    live, me, odd = meta[0], meta[1], meta[2]
    set_mask(row_ids, col_ids, live, mask)

    def place(part):
        owner = jnp.where(odd == 1, 3 - part, part)
        return lax.rem(owner - me + 4, 4)

    pay[...] = jnp.zeros_like(pay)
    for r in range(ROWS):
        block = factors[r * BS : (r + 1) * BS, :]
        rounded[r] = block.astype(bf16)
        turned[r] = block.T.astype(bf16)
    for r in range(ROWS):
        gram = jnp.dot(turned[r], rounded[r], preferred_element_type=f32)
        mixed, cross, diag = pack(gram)
        grams[r, :, :BS] = mixed
        grams[r, :, BS:] = cross
        diags[r : r + 1, :] = diag

    def slots(step, carry):
        for k in range(4):
            s = step * 4 + k
            r, c = row_ids[s], col_ids[s]
            weight = jnp.where(s < live, 1.0, 0.0)
            product = weight * jnp.dot(turned[r], tiles[s], preferred_element_type=f32)
            at = place(c // 2)
            rows = pl.ds(pl.multiple_of(2 * BS + lax.rem(c, 2) * BS, BS), BS)
            pay[at, rows, :BS] += product[:BS]
            pay[at, rows, BS:] += product[BS:]
        return carry

    lax.fori_loop(0, (live + 3) // 4, slots, 0)

    for c in range(COLS):
        at = place(c // 2)
        weights = [mask[r * COLS + c] for r in range(ROWS)]
        base = (c % 2) * BS
        for half in range(4):
            rows = slice(half * 32, (half + 1) * 32)
            total = weights[0] * grams[0, rows, :]
            for r in range(1, ROWS):
                total += weights[r] * grams[r, rows, :]
            pay[at, base + half * 32 : base + (half + 1) * 32, :] = total
        total = weights[0] * diags[0:1, :]
        for r in range(1, ROWS):
            total += weights[r] * diags[r : r + 1, :]
        pay[at, 4 * BS + c % 2 : 4 * BS + c % 2 + 1, :BS] = total


def band_of(values, before, after, ext):
    n = values.shape[0]
    ext[7:8, :] = before
    ext[8 : 8 + n, :] = values
    ext[8 + n : 9 + n, :] = after
    return 2.0 * values - ext[7 : 7 + n, :] - ext[9 : 9 + n, :]


def variant_start(meta, total, start, low, high, resid, applied, g_high, g_low, edge, ext):
    part = meta[0]
    n = 2 * BS
    first = pl.multiple_of(part * n, n)
    mine = start[pl.ds(first, n), :]
    before8 = start[pl.ds(pl.multiple_of(jnp.maximum(first - 8, 0), 8), 8), :]
    after8 = start[pl.ds(pl.multiple_of(jnp.minimum(first + n, 3 * n + n - 8), 8), 8), :]
    before = jnp.where(part == 0, low[7:8, :], before8[7:8, :])
    after = jnp.where(part == 3, high[0:1, :], after8[0:1, :])
    banded = band_of(mine, before, after, ext)
    for k in range(2):
        gram = unpack(
            total[k * BS : (k + 1) * BS, :BS],
            total[k * BS : (k + 1) * BS, BS:],
            total[4 * BS + k : 4 * BS + k + 1, :BS],
        )
        up, down = split(gram)
        g_high[k] = up
        g_low[k] = down
        rows = slice(k * BS, (k + 1) * BS)
        data = total[(2 + k) * BS : (3 + k) * BS, :]
        data = jnp.concatenate([data[:, :BS].T, data[:, BS:].T], axis=1)
        resid[rows, :] = (
            data
            - times(mine[rows], up, down)
            - ridge_weight * mine[rows]
            - smooth_weight * banded[rows]
        )
    value = resid[...]
    zero = jnp.zeros((1, R), f32)
    banded = band_of(value, zero, zero, ext)
    for k in range(2):
        rows = slice(k * BS, (k + 1) * BS)
        applied[rows, :] = (
            times(value[rows], g_high[k], g_low[k])
            + ridge_weight * value[rows]
            + smooth_weight * banded[rows]
        )
    edge[...] = jnp.zeros_like(edge)
    edge[0:1, :] = resid[0:1, :]
    edge[1:2, :] = applied[0:1, :]
    edge[2:3, :] = resid[n - 1 : n, :]
    edge[3:4, :] = applied[n - 1 : n, :]


def as_row(values):
    lanes = lax.broadcasted_iota(jnp.int32, (8, BS), 1)
    row = jnp.zeros((8, BS), f32)
    for k, value in enumerate(values):
        row = jnp.where(lanes == k, value, row)
    return row


def total_of(values):
    return jnp.sum(jnp.sum(values, axis=0, keepdims=True), axis=1, keepdims=True)


def largest(values):
    return jnp.max(jnp.max(jnp.abs(values), axis=0, keepdims=True), axis=1, keepdims=True)


def variant_moments(meta, resid, applied, g_high, g_low, edge_before, edge_after, again, moments, ext):
    has_before, has_after = meta[1], meta[2]
    n = 2 * BS
    value = resid[...]
    again[...] = applied[...]
    again[0:1, :] = again[0:1, :] - smooth_weight * edge_before[2:3, :]
    again[n - 1 : n, :] = again[n - 1 : n, :] - smooth_weight * edge_after[0:1, :]
    first = again[...]
    zero = jnp.zeros((1, R), f32)
    before = jnp.where(has_before == 1, edge_before[3:4, :] - smooth_weight * value[0:1, :], zero)
    after = jnp.where(has_after == 1, edge_after[1:2, :] - smooth_weight * value[n - 1 : n, :], zero)
    banded = band_of(first, before, after, ext)
    data = jnp.concatenate(
        [times(first[k * BS : (k + 1) * BS], g_high[k], g_low[k]) for k in range(2)], axis=0
    )
    second = data + ridge_weight * first + smooth_weight * banded
    moments[...] = as_row(
        [
            total_of(value * value),
            total_of(value * first),
            total_of(first * first),
            total_of(first * second),
            largest(value),
            largest(first),
        ]
    )


def coefficients(table):
    sums = jnp.sum(table, axis=0, keepdims=True)
    peaks = jnp.max(table, axis=0, keepdims=True)
    rr, ra, aa, aaa = (sums[:, k : k + 1] for k in range(4))
    first = rr / ra
    rr_next = rr - 2.0 * first * ra + first * first * aa
    ratio = rr_next / rr
    curve = (
        (1.0 + ratio) * (1.0 + ratio) * ra
        - 2.0 * (1.0 + ratio) * first * aa
        + first * first * aaa
    )
    second = rr_next / curve
    on_resid = first + second * (1.0 + ratio)
    on_applied = second * first
    bound = jnp.abs(on_resid) * peaks[:, 4:5] + jnp.abs(on_applied) * peaks[:, 5:6]
    return on_resid, on_applied, bound


def indiv_sums(
    row_ids, col_ids, meta, table, start, tiles,
    resid0, resid1, resid2, resid3, again0, again1, again2, again3,
    new, pay, scales, turned, rounded, grams, diags, mask,
):
    live, me, odd, core = meta[0], meta[1], meta[2], meta[3]
    set_mask(row_ids, col_ids, live, mask)
    on_resid, on_applied, bound = coefficients(table[...])
    n = 2 * BS
    resids, agains = (resid0, resid1, resid2, resid3), (again0, again1, again2, again3)
    for k in range(4):
        owner = lax.rem(me - k + 4, 4)
        part = jnp.where(odd == 1, 3 - owner, owner)
        rows = pl.ds(pl.multiple_of(part * n, n), n)
        new[rows, :] = start[rows, :] + on_resid * resids[k][...] - on_applied * agains[k][...]
    top = bound + 1.5
    scale_e = 30000.0 / (2.0 * 6.0 * COLS * BS * top)
    scale_h = 30000.0 / (2.0 * COLS * BS * top * top)
    scales[...] = as_row([1.0 / scale_e, 1.0 / scale_h])
    pay[...] = jnp.zeros_like(pay)
    for c in range(COLS):
        block = new[c * BS : (c + 1) * BS, :]
        rounded[c] = block.astype(bf16)
        turned[c] = block.T.astype(bf16)
    for c in range(COLS):
        gram = jnp.dot(turned[c], rounded[c], preferred_element_type=f32) * scale_h
        mixed, cross, diag = pack(gram)
        grams[c, :, :BS] = mixed
        grams[c, :, BS:] = cross
        diags[c : c + 1, :] = diag

    def slots(step, carry):
        for k in range(4):
            s = step * 4 + k
            r, c = row_ids[s], col_ids[s]
            weight = jnp.where(s < live, scale_e, 0.0)
            product = weight * jnp.dot(tiles[s], rounded[c], preferred_element_type=f32)
            pay[core, r, :BS, :] += product
        return carry

    lax.fori_loop(0, (live + 3) // 4, slots, 0)
    other = 1 - core
    for r in range(ROWS):
        weights = [mask[r * COLS + c] for c in range(COLS)]
        for half in range(4):
            rows = slice(half * 32, (half + 1) * 32)
            total = weights[0] * grams[0, rows, :]
            for c in range(1, COLS):
                total += weights[c] * grams[c, rows, :]
            pay[other, r, rows, :] = total
        total = weights[0] * diags[0:1, :]
        for c in range(1, COLS):
            total += weights[c] * diags[c : c + 1, :]
        pay[other, r, BS : BS + 1, :BS] = total


def indiv_moments(meta, mine, theirs, start, scales, resid, applied, moments):
    core = meta[0]
    own, far = mine[...], theirs[...]
    data = jnp.where(core == 0, own, far) * scales[0:1, 0:1]
    packed = jnp.where(core == 0, far, own) * scales[0:1, 1:2]
    high, low = split(unpack(packed[:BS, :BS], packed[:BS, BS:], packed[BS : BS + 1, :BS]))
    begin = start[...]
    value = data[:BS, :] - times(begin, high, low) - ridge_weight * begin
    first = times(value, high, low) + ridge_weight * value
    second = times(first, high, low) + ridge_weight * first
    resid[...] = value
    applied[...] = first
    moments[...] = as_row(
        [
            total_of(value * value),
            total_of(value * first),
            total_of(first * first),
            total_of(first * second),
            largest(value),
            largest(first),
        ]
    )


def indiv_update(meta, table, resid, applied, update, scales):
    on_resid, on_applied, bound = coefficients(table[...])
    bound = jnp.maximum(bound, 1e-30)
    rows = pl.ds(pl.multiple_of(meta[0] * (BS // 2), BS // 2), BS // 2)
    update[...] = (on_resid * resid[rows, :] - on_applied * applied[rows, :]) * (30000.0 / bound)
    scales[...] = as_row([bound / 30000.0])


def ring(step):
    return [(k, (k + step) % 4) for k in range(4)]


def on_device(indiv_factors, variant_factors, dosage_tiles, block_rows, block_cols, live_blocks):
    tiles = dosage_tiles[0, 0]
    row_ids = block_rows[0, 0]
    col_ids = block_cols[0, 0]
    live = live_blocks[0, 0]
    me = lax.axis_index("x")
    core = lax.axis_index("c")
    chip = lax.axis_index(CHIP)
    slab = lax.axis_index(GEN)
    odd = core
    part = jnp.where(odd == 1, 3 - me, me)

    slabs = 32
    low = lax.ppermute(variant_factors[-8:], GEN, [(k, k + 1) for k in range(slabs - 1)])
    high = lax.ppermute(variant_factors[:8], GEN, [(k + 1, k) for k in range(slabs - 1)])

    meta = jnp.stack([live, me, odd, core]).astype(jnp.int32)
    pay = pl.pallas_call(
        variant_sums,
        out_shape=jax.ShapeDtypeStruct((4, PAY_V, R), f32),
        in_specs=[smem(), smem(), smem(), vmem(), vmem()],
        out_specs=vmem(),
        scratch_shapes=[
            pltpu.VMEM((ROWS, R, BS), bf16),
            pltpu.VMEM((ROWS, BS, R), bf16),
            pltpu.VMEM((ROWS, BS, R), f32),
            pltpu.VMEM((ROWS, BS), f32),
            pltpu.SMEM((ROWS * COLS,), f32),
        ],
        compiler_params=params(),
    )(row_ids, col_ids, meta, tiles, indiv_factors)
    got = [
        lax.ppermute(pay[k].astype(f16), "x", ring(k)) for k in (1, 2, 3)
    ]
    total = pay[0] + got[0].astype(f32) + got[1].astype(f32) + got[2].astype(f32)

    def device(position):
        at, place = divmod(position, 4)
        return at * 4 + (3 - place if at % 2 else place)

    line = [device(k) for k in range(4 * slabs)]
    position = slab * 4 + part
    meta_line = jnp.stack(
        [part, (position > 0).astype(jnp.int32), (position < 4 * slabs - 1).astype(jnp.int32)]
    ).astype(jnp.int32)
    square = jax.ShapeDtypeStruct((2 * BS, R), f32)
    halves = jax.ShapeDtypeStruct((2, R, R), bf16)
    resid, applied, g_high, g_low, edge = pl.pallas_call(
        variant_start,
        out_shape=(square, square, halves, halves, jax.ShapeDtypeStruct((8, R), f32)),
        in_specs=[smem()] + [vmem()] * 4,
        out_specs=(vmem(),) * 5,
        scratch_shapes=[pltpu.VMEM((2 * BS + 16, R), f32)],
        compiler_params=params(),
    )(meta_line, total, variant_factors, low, high)
    edge_before = lax.ppermute(edge, ALL, list(zip(line[:-1], line[1:])))
    edge_after = lax.ppermute(edge, ALL, list(zip(line[1:], line[:-1])))
    resids = [resid] + [lax.ppermute(resid, "x", ring(k)) for k in (1, 2, 3)]
    again, moments = pl.pallas_call(
        variant_moments,
        out_shape=(square, jax.ShapeDtypeStruct((8, BS), f32)),
        in_specs=[smem()] + [vmem()] * 6,
        out_specs=(vmem(),) * 2,
        scratch_shapes=[pltpu.VMEM((2 * BS + 16, R), f32)],
        compiler_params=params(),
    )(meta_line, resid, applied, g_high, g_low, edge_before, edge_after)
    agains = [again] + [lax.ppermute(again, "x", ring(k)) for k in (1, 2, 3)]
    table = lax.all_to_all(
        jnp.broadcast_to(moments[None, :1], (4 * slabs, 1, BS)), ALL, 0, 0
    ).reshape(4 * slabs, BS)

    variant_new, pay, scales = pl.pallas_call(
        indiv_sums,
        out_shape=(
            jax.ShapeDtypeStruct((COLS * BS, R), f32),
            jax.ShapeDtypeStruct((2, ROWS, PAY_I, R), f32),
            jax.ShapeDtypeStruct((8, BS), f32),
        ),
        in_specs=[smem()] * 3 + [vmem()] * 11,
        out_specs=(vmem(),) * 3,
        scratch_shapes=[
            pltpu.VMEM((COLS, R, BS), bf16),
            pltpu.VMEM((COLS, BS, R), bf16),
            pltpu.VMEM((COLS, BS, R), f32),
            pltpu.VMEM((COLS, BS), f32),
            pltpu.SMEM((ROWS * COLS,), f32),
        ],
        compiler_params=params(),
    )(row_ids, col_ids, meta, table, variant_factors, tiles, *resids, *agains)

    swap = [(0, 1), (1, 0)]
    from_other = lax.ppermute(pay[1].astype(f16), "c", swap)
    of_chip = (pay[0] + from_other.astype(f32)).astype(f16)
    arrived = lax.all_to_all(of_chip, CHIP, 0, 0)
    mine = jnp.sum(arrived.astype(f32), axis=0)
    theirs = lax.ppermute(mine, "c", swap)
    begin = lax.dynamic_slice_in_dim(indiv_factors, chip * BS, BS, 0)
    meta_core = core.astype(jnp.int32).reshape(1)
    block = jax.ShapeDtypeStruct((BS, R), f32)
    row = jax.ShapeDtypeStruct((8, BS), f32)
    resid, applied, moments = pl.pallas_call(
        indiv_moments,
        out_shape=(block, block, row),
        in_specs=[smem()] + [vmem()] * 4,
        out_specs=(vmem(),) * 3,
        compiler_params=params(),
    )(meta_core, mine, theirs, begin, scales)
    chips = 64
    table = lax.all_to_all(
        jnp.broadcast_to(moments[None, :1], (chips, 1, BS)), ("z", "y", "x"), 0, 0
    ).reshape(chips, BS)
    update, scales = pl.pallas_call(
        indiv_update,
        out_shape=(jax.ShapeDtypeStruct((BS // 2, R), f32), row),
        in_specs=[smem()] + [vmem()] * 3,
        out_specs=(vmem(),) * 2,
        compiler_params=params(),
    )(meta_core, table, resid, applied)
    sent = jnp.broadcast_to(update.astype(f16)[None], (ROWS, BS // 2, R))
    ours = lax.all_to_all(sent, CHIP, 0, 0)
    far = lax.ppermute(ours, "c", swap)
    first = jnp.where(core == 0, ours, far)
    last = jnp.where(core == 0, far, ours)
    change = jnp.concatenate([first, last], axis=1).reshape(ROWS * BS, R)
    indiv_new = indiv_factors + change.astype(f32) * scales[0, 0]
    return variant_new, indiv_new


def solution(mesh):
    grid = np.asarray(mesh.devices).reshape(4, 4, 2, 4)
    inner = Mesh(grid, ALL)
    return jax.shard_map(
        on_device,
        mesh=inner,
        in_specs=(
            P("x", None),
            P(GEN, None),
            P(GEN, "x", None, None, None),
            P(GEN, "x", None),
            P(GEN, "x", None),
            P(GEN, "x"),
        ),
        out_specs=(P(GEN, None), P("x", None)),
        check_vma=False,
    )
```

```python
import jax
import jax.numpy as jnp
import numpy as np
from jax import lax
from jax.experimental import pallas as pl
from jax.experimental.pallas import tpu as pltpu
from jax.sharding import Mesh
from jax.sharding import PartitionSpec as P

BS = 128
R = 256
NB = 64
ROWS = 16
COLS = 8
smooth_weight = 32.0
ridge_weight = 1.0
f32, bf16, f16 = jnp.float32, jnp.bfloat16, jnp.float16
ALL = ("z", "y", "c", "x")
GEN = ("z", "y", "c")
CHIP = ("z", "y")
PAY_V = 2 * BS + 2 * BS + 16
PAY_I = BS + 8
VMEM_LIMIT = 48 * 1024 * 1024


def row_col():
    rows = lax.broadcasted_iota(jnp.int32, (BS, BS), 0)
    cols = lax.broadcasted_iota(jnp.int32, (BS, BS), 1)
    return rows, cols


def pack(gram):
    rows, cols = row_col()
    upper = gram[:BS, :BS]
    lower = gram[BS:, BS:]
    mixed = jnp.where(rows <= cols, upper, lower)
    diag = jnp.sum(jnp.where(rows == cols, lower, 0.0), axis=0, keepdims=True)
    return mixed, gram[:BS, BS:], diag


def unpack(mixed, cross, diag):
    rows, cols = row_col()
    turned = mixed.T
    upper = jnp.where(rows <= cols, mixed, turned)
    lower = jnp.where(rows > cols, mixed, jnp.where(rows < cols, turned, diag))
    top = jnp.concatenate([upper, cross], axis=1)
    bottom = jnp.concatenate([cross.T, lower], axis=1)
    return jnp.concatenate([top, bottom], axis=0)


def split(matrix):
    high = matrix.astype(bf16)
    return high, (matrix - high.astype(f32)).astype(bf16)


def times(values, high, low):
    rounded = values.astype(bf16)
    return jnp.dot(rounded, high, preferred_element_type=f32) + jnp.dot(
        rounded, low, preferred_element_type=f32
    )


def set_mask(row_ids, col_ids, live, mask):
    def clear(k, carry):
        mask[k] = 0.0
        return carry

    lax.fori_loop(0, ROWS * COLS, clear, 0)

    def mark(s, carry):
        mask[row_ids[0, 0, s] * COLS + col_ids[0, 0, s]] = 1.0
        return carry

    lax.fori_loop(0, live, mark, 0)


def variant_sums(
    row_ids, col_ids, meta, tiles_hbm, factors_hbm, own, far, dense_hbm, mask,
    tiles, factors, dense, turned, rounded, grams, diags, sems,
):
    live, me, odd = meta[0], meta[1], meta[2]
    quarter = ROWS * BS // 4
    loads = [
        pltpu.make_async_copy(
            factors_hbm.at[pl.ds(k * quarter, quarter), :],
            factors.at[pl.ds(k * quarter, quarter), :],
            sems.at[k],
        )
        for k in range(4)
    ]
    load_tiles = pltpu.make_async_copy(tiles_hbm.at[0, 0], tiles, sems.at[4])
    for load in loads:
        load.start()
    load_tiles.start()
    dense[...] = jnp.zeros_like(dense)
    set_mask(row_ids, col_ids, live, mask)
    for r in range(ROWS):
        if r % 4 == 0:
            loads[r // 4].wait()
        block = factors[r * BS : (r + 1) * BS, :]
        rounded[r] = block.astype(bf16)
        turned[:, r * BS : (r + 1) * BS] = block.T.astype(bf16)
        gram = jnp.dot(turned[:, r * BS : (r + 1) * BS], rounded[r], preferred_element_type=f32)
        mixed, cross, diag = pack(gram)
        grams[r, :, :BS] = mixed
        grams[r, :, BS:] = cross
        diags[r : r + 1, :] = diag
    load_tiles.wait()

    def scatter(s, carry):
        rows = pl.ds(pl.multiple_of(row_ids[0, 0, s] * BS, BS), BS)
        cols = pl.ds(pl.multiple_of(col_ids[0, 0, s] * BS, BS), BS)
        dense[rows, cols] = tiles[s]
        return carry

    lax.fori_loop(0, live, scatter, 0)
    keep = pltpu.make_async_copy(dense, dense_hbm, sems.at[5])
    keep.start()
    zero = jnp.zeros((16, R), f32)
    for k in range(4):
        at = lax.rem(me + k, 4)
        part = jnp.where(odd == 1, 3 - at, at)
        out = own if k == 0 else far.at[k - 1]
        cols = pl.ds(pl.multiple_of(part * 2 * BS, 2 * BS), 2 * BS)
        out[2 * BS : 4 * BS, :] = jnp.dot(
            turned[...], dense[:, cols], preferred_element_type=f32
        )
        out[4 * BS :, :] = zero
        for j in range(2):
            weights = [mask[r * COLS + part * 2 + j] for r in range(ROWS)]
            for piece in range(4):
                rows = slice(piece * 32, (piece + 1) * 32)
                total = weights[0] * grams[0, rows, :]
                for r in range(1, ROWS):
                    total += weights[r] * grams[r, rows, :]
                out[j * BS + piece * 32 : j * BS + (piece + 1) * 32, :] = total
            total = weights[0] * diags[0:1, :]
            for r in range(1, ROWS):
                total += weights[r] * diags[r : r + 1, :]
            out[4 * BS + j : 4 * BS + j + 1, :BS] = total
    keep.wait()


def band_of(values, before, after, ext):
    n = values.shape[0]
    ext[7:8, :] = before
    ext[8 : 8 + n, :] = values
    ext[8 + n : 9 + n, :] = after
    return 2.0 * values - ext[7 : 7 + n, :] - ext[9 : 9 + n, :]


def variant_start(meta, total, start, low, high, resid, applied, g_high, g_low, edge, ext):
    part = meta[0]
    n = 2 * BS
    first = pl.multiple_of(part * n, n)
    mine = start[pl.ds(first, n), :]
    before8 = start[pl.ds(pl.multiple_of(jnp.maximum(first - 8, 0), 8), 8), :]
    after8 = start[pl.ds(pl.multiple_of(jnp.minimum(first + n, 3 * n + n - 8), 8), 8), :]
    before = jnp.where(part == 0, low[7:8, :], before8[7:8, :])
    after = jnp.where(part == 3, high[0:1, :], after8[0:1, :])
    banded = band_of(mine, before, after, ext)
    data = total[2 * BS : 4 * BS, :].T
    for k in range(2):
        gram = unpack(
            total[k * BS : (k + 1) * BS, :BS],
            total[k * BS : (k + 1) * BS, BS:],
            total[4 * BS + k : 4 * BS + k + 1, :BS],
        )
        up, down = split(gram)
        g_high[k] = up
        g_low[k] = down
        rows = slice(k * BS, (k + 1) * BS)
        resid[rows, :] = (
            data[rows]
            - times(mine[rows], up, down)
            - ridge_weight * mine[rows]
            - smooth_weight * banded[rows]
        )
    value = resid[...]
    zero = jnp.zeros((1, R), f32)
    banded = band_of(value, zero, zero, ext)
    for k in range(2):
        rows = slice(k * BS, (k + 1) * BS)
        applied[rows, :] = (
            times(value[rows], g_high[k], g_low[k])
            + ridge_weight * value[rows]
            + smooth_weight * banded[rows]
        )
    edge[...] = jnp.zeros_like(edge)
    edge[0:1, :] = resid[0:1, :]
    edge[1:2, :] = applied[0:1, :]
    edge[2:3, :] = resid[n - 1 : n, :]
    edge[3:4, :] = applied[n - 1 : n, :]


def as_row(values):
    lanes = lax.broadcasted_iota(jnp.int32, (8, BS), 1)
    row = jnp.zeros((8, BS), f32)
    for k, value in enumerate(values):
        row = jnp.where(lanes == k, value, row)
    return row


def total_of(values):
    return jnp.sum(jnp.sum(values, axis=0, keepdims=True), axis=1, keepdims=True)


def largest(values):
    return jnp.max(jnp.max(jnp.abs(values), axis=0, keepdims=True), axis=1, keepdims=True)


def curve_of(rr, ra, aa, aaa):
    first = rr / ra
    rr_next = rr - 2.0 * first * ra + first * first * aa
    ratio = rr_next / rr
    curve = (
        (1.0 + ratio) * (1.0 + ratio) * ra
        - 2.0 * (1.0 + ratio) * first * aa
        + first * first * aaa
    )
    second = rr_next / curve
    return first + second * (1.0 + ratio), second * first, rr_next, curve


def variant_moments(
    meta, start, resid, applied, g_high, g_low, edge_before, edge_after, sent, moments, ext
):
    has_before, has_after = meta[1], meta[2]
    n = 2 * BS
    value = resid[...]
    zero = jnp.zeros((1, R), f32)
    low = jnp.concatenate([edge_before[2:3, :], jnp.zeros((n - 1, R), f32)], axis=0)
    high = jnp.concatenate([jnp.zeros((n - 1, R), f32), edge_after[0:1, :]], axis=0)
    first = applied[...] - smooth_weight * (low + high)
    before = jnp.where(has_before == 1, edge_before[3:4, :] - smooth_weight * value[0:1, :], zero)
    after = jnp.where(has_after == 1, edge_after[1:2, :] - smooth_weight * value[n - 1 : n, :], zero)
    banded = band_of(first, before, after, ext)
    data = jnp.concatenate(
        [times(first[k * BS : (k + 1) * BS], g_high[k], g_low[k]) for k in range(2)], axis=0
    )
    second = data + ridge_weight * first + smooth_weight * banded
    rr, ra = total_of(value * value), total_of(value * first)
    aa, aaa = total_of(first * first), total_of(first * second)
    near, far, rr_next, curve = curve_of(rr, ra, aa, aaa)
    good = (ra > 0.0) & (rr_next > 1e-3 * rr) & (curve > 0.0) & (far > 0.0)
    on_start = jnp.where(good, 1.0, 0.0)
    near = jnp.where(good, near, 0.0)
    far = jnp.where(good, far, -1.0)
    mine = start[pl.ds(pl.multiple_of(meta[0] * n, n), n), :]
    guess = on_start * mine + near * value - far * first
    peak_value, peak_guess = largest(value), largest(guess)
    unit_value = jnp.maximum(peak_value, 1e-30) / 16384.0
    unit_guess = jnp.maximum(peak_guess, 1e-30) / 16384.0
    sent[0] = value / unit_value
    sent[1] = guess / unit_guess
    moments[...] = as_row(
        [rr, ra, aa, aaa, peak_value, largest(first), on_start, near, far, unit_value, unit_guess]
    )


def new_variants(meta, table, start, pieces, new, rounded, scales):
    me, odd, slab = meta[1], meta[2], meta[4]
    sums = jnp.sum(table[...], axis=0, keepdims=True)
    peaks = jnp.max(table[...], axis=0, keepdims=True)
    on_resid, on_applied, _, _ = curve_of(*(sums[:, k : k + 1] for k in range(4)))
    n = 2 * BS
    for k in range(4):
        owner = lax.rem(me - k + 4, 4)
        part = jnp.where(odd == 1, 3 - owner, owner)
        rows = pl.ds(pl.multiple_of(part * n, n), n)
        line = table[pl.ds(slab * 4 + owner, 1), :]
        on_start, near, far, unit_value, unit_guess = (line[:, j : j + 1] for j in range(6, 11))
        share = on_applied / far
        value = (
            (1.0 - share * on_start) * start[rows, :]
            + ((on_resid - share * near) * unit_value) * pieces[k, 0]
            + (share * unit_guess) * pieces[k, 1]
        )
        new[rows, :] = value
        rounded[rows, :] = value.astype(bf16)
    top = jnp.abs(on_resid) * peaks[:, 4:5] + jnp.abs(on_applied) * peaks[:, 5:6] + 1.5
    scale_e = 30000.0 / (2.0 * 6.0 * COLS * BS * top)
    scale_h = 30000.0 / (2.0 * COLS * BS * top * top)
    scales[...] = as_row([scale_e, scale_h, 1.0 / scale_e, 1.0 / scale_h])


def indiv_sums(
    meta, mask_own, mask_far, scales, dense_own, dense_far, rounded_own, rounded_far, pay, grams, diags
):
    core = meta[3]

    @pl.when(core == 0)
    def _():
        scale = scales[0:1, 0:1]
        for r in range(ROWS):
            rows = slice(r * BS, (r + 1) * BS)
            product = jnp.dot(dense_own[rows, :], rounded_own[...], preferred_element_type=f32)
            product += jnp.dot(dense_far[rows, :], rounded_far[...], preferred_element_type=f32)
            pay[r, :BS, :] = scale * product
            pay[r, BS:, :] = jnp.zeros((PAY_I - BS, R), f32)

    @pl.when(core == 1)
    def _():
        scale = scales[0:1, 1:2]
        for k, source in enumerate((rounded_own, rounded_far)):
            for c in range(COLS):
                block = source[c * BS : (c + 1) * BS, :]
                turned = block.astype(f32).T.astype(bf16)
                gram = scale * jnp.dot(turned, block, preferred_element_type=f32)
                mixed, cross, diag = pack(gram)
                at = k * COLS + c
                grams[at, :, :BS] = mixed
                grams[at, :, BS:] = cross
                diags[at : at + 1, :] = diag
        for r in range(ROWS):
            weights = [mask_own[r * COLS + c] for c in range(COLS)]
            weights += [mask_far[r * COLS + c] for c in range(COLS)]
            for piece in range(4):
                rows = slice(piece * 32, (piece + 1) * 32)
                total = weights[0] * grams[0, rows, :]
                for c in range(1, 2 * COLS):
                    total += weights[c] * grams[c, rows, :]
                pay[r, rows, :] = total
            total = weights[0] * diags[0:1, :]
            for c in range(1, 2 * COLS):
                total += weights[c] * diags[c : c + 1, :]
            pay[r, BS:, :] = jnp.zeros((PAY_I - BS, R), f32)
            pay[r, BS : BS + 1, :BS] = total


def exponent_of(peak):
    return jnp.clip(jnp.ceil(jnp.log2(jnp.maximum(peak, 1e-30))), -100.0, 100.0)


def pieces_of(value):
    high = value.astype(bf16).astype(f32)
    rest = (value - high) * 256.0
    middle = rest.astype(bf16).astype(f32)
    return [high, middle, (rest - middle) * 256.0]


def indiv_moments(meta, mine, theirs, start, scales, sent):
    core = meta[3]
    own, far = mine[...], theirs[...]
    data = jnp.where(core == 0, own, far) * scales[0:1, 2:3]
    packed = jnp.where(core == 0, far, own) * scales[0:1, 3:4]
    high, low = split(unpack(packed[:BS, :BS], packed[:BS, BS:], packed[BS : BS + 1, :BS]))
    begin = start[...]
    value = data[:BS, :] - times(begin, high, low) - ridge_weight * begin
    first = times(value, high, low) + ridge_weight * value
    second = times(first, high, low) + ridge_weight * first
    powers = [exponent_of(largest(array)) for array in (value, first, second)]
    value, first, second = (
        array * jnp.exp2(-power) for array, power in zip((value, first, second), powers)
    )
    moments = [
        total_of(value * value),
        total_of(value * first),
        total_of(first * first),
        total_of(first * second),
    ]
    sent[:BS, :] = jnp.where(core == 0, value, first) * 16384.0
    row = as_row([part for moment in moments for part in pieces_of(moment)] + powers)
    sent[BS:, :] = jnp.concatenate([row, row], axis=1)


def chip_moments(lines, moments):
    def moment(k, power):
        parts = [lines[:, 3 * k + j : 3 * k + j + 1] for j in range(3)]
        value = parts[0] + parts[1] * (1.0 / 256.0) + parts[2] * (1.0 / 65536.0)
        return jnp.sum(value * power, axis=0, keepdims=True)

    one, two, three = (jnp.exp2(lines[:, j : j + 1]) for j in (12, 13, 14))
    moments[...] = as_row(
        [
            moment(0, one * one),
            moment(1, one * two),
            moment(2, two * two),
            moment(3, two * three),
        ]
    )


def indiv_shares(meta, lines, own, next1, next2, next3, shares):
    sums = own[0:1, :] + next1[0:1, :] + next2[0:1, :] + next3[0:1, :]
    on_resid, on_applied, _, _ = curve_of(*(sums[:, k : k + 1] for k in range(4)))
    of_resid = on_resid * jnp.exp2(lines[:, 12:13]) * (1.0 / 16384.0)
    of_applied = -on_applied * jnp.exp2(lines[:, 13:14]) * (1.0 / 16384.0)
    core = meta[3]
    lanes = lax.broadcasted_iota(jnp.int32, (ROWS, BS), 1)
    here = jnp.where(core == 0, of_resid, of_applied)
    there = jnp.where(core == 0, of_applied, of_resid)
    shares[...] = jnp.where(lanes == 0, here, there)


def ring(step):
    return [(k, (k + step) % 4) for k in range(4)]


def call(kernel, ins, outs, scratch=(), limit=VMEM_LIMIT):
    return pl.pallas_call(
        kernel,
        out_shape=tuple(jax.ShapeDtypeStruct(shape, dtype) for shape, dtype, _ in outs),
        in_specs=[pl.BlockSpec(memory_space=space) for space in ins],
        out_specs=tuple(pl.BlockSpec(memory_space=space) for _, _, space in outs),
        scratch_shapes=list(scratch),
        compiler_params=pltpu.CompilerParams(vmem_limit_bytes=limit),
    )


def on_device(indiv_factors, variant_factors, dosage_tiles, block_rows, block_cols, live_blocks):
    S, V, H = pltpu.SMEM, pltpu.VMEM, pl.ANY
    live = live_blocks[0, 0]
    me = lax.axis_index("x")
    core = lax.axis_index("c")
    chip = lax.axis_index(CHIP)
    slab = lax.axis_index(GEN)
    part = jnp.where(core == 1, 3 - me, me)
    slabs = 32
    swap = [(0, 1), (1, 0)]
    meta = jnp.stack([live, me, core, core, slab]).astype(jnp.int32)

    own, far, dense, mask = call(
        variant_sums,
        [S, S, S, H, H],
        [
            ((PAY_V, R), f32, V),
            ((3, PAY_V, R), f32, V),
            ((ROWS * BS, COLS * BS), bf16, H),
            ((ROWS * COLS,), f32, S),
        ],
        [
            pltpu.VMEM((NB, BS, BS), bf16),
            pltpu.VMEM((ROWS * BS, R), f32),
            pltpu.VMEM((ROWS * BS, COLS * BS), bf16),
            pltpu.VMEM((R, ROWS * BS), bf16),
            pltpu.VMEM((ROWS, BS, R), bf16),
            pltpu.VMEM((ROWS, BS, R), f32),
            pltpu.VMEM((ROWS, BS), f32),
            pltpu.SemaphoreType.DMA((6,)),
        ],
    )(block_rows, block_cols, meta, dosage_tiles, indiv_factors)
    far = far.astype(f16)
    got = [lax.ppermute(far[k - 1], "x", ring(k)) for k in (1, 2, 3)]
    low = lax.ppermute(variant_factors[-8:], GEN, [(k, k + 1) for k in range(slabs - 1)])
    high = lax.ppermute(variant_factors[:8], GEN, [(k + 1, k) for k in range(slabs - 1)])
    dense_far = lax.ppermute(dense, "c", swap)
    mask_far = lax.ppermute(mask, "c", swap)
    total = own + got[0].astype(f32) + got[1].astype(f32) + got[2].astype(f32)

    def device(position):
        at, place = divmod(position, 4)
        return at * 4 + (3 - place if at % 2 else place)

    line = [device(k) for k in range(4 * slabs)]
    position = slab * 4 + part
    meta_line = jnp.stack(
        [part, (position > 0).astype(jnp.int32), (position < 4 * slabs - 1).astype(jnp.int32)]
    ).astype(jnp.int32)
    square = ((2 * BS, R), f32, V)
    halves = ((2, R, R), bf16, V)
    row = ((8, BS), f32, V)
    ext = pltpu.VMEM((2 * BS + 16, R), f32)
    resid, applied, g_high, g_low, edge = call(
        variant_start,
        [S, V, V, V, V],
        [square, square, halves, halves, ((8, R), f32, V)],
        [ext],
    )(meta_line, total, variant_factors, low, high)
    edge_before = lax.ppermute(edge, ALL, list(zip(line[:-1], line[1:])))
    edge_after = lax.ppermute(edge, ALL, list(zip(line[1:], line[:-1])))
    sent, moments = call(
        variant_moments, [S] + [V] * 7, [((2, 2 * BS, R), f32, V), row], [ext]
    )(meta_line, variant_factors, resid, applied, g_high, g_low, edge_before, edge_after)
    sent = sent.astype(f16)
    pieces = jnp.stack([sent] + [lax.ppermute(sent, "x", ring(k)) for k in (1, 2, 3)])
    table = lax.all_to_all(
        jnp.broadcast_to(moments[None, :1], (4 * slabs, 1, BS)), ALL, 0, 0
    ).reshape(4 * slabs, BS)

    variant_new, rounded, scales = call(
        new_variants,
        [S, V, V, V],
        [((COLS * BS, R), f32, V), ((COLS * BS, R), bf16, V), row],
    )(meta, table, variant_factors, pieces.astype(f32))
    rounded_far = lax.ppermute(rounded, "c", swap)
    (pay,) = call(
        indiv_sums,
        [S, S, S, V, V, V, V, V],
        [((ROWS, PAY_I, R), f32, V)],
        [pltpu.VMEM((ROWS, BS, R), f32), pltpu.VMEM((ROWS, BS), f32)],
    )(meta, mask, mask_far, scales, dense, dense_far, rounded, rounded_far)
    arrived = lax.all_to_all(pay.astype(f16), CHIP, 0, 0)
    mine = jnp.sum(arrived.astype(f32), axis=0)
    theirs = lax.ppermute(mine, "c", swap)
    begin = lax.dynamic_slice_in_dim(indiv_factors, chip * BS, BS, 0)
    (sent,) = call(indiv_moments, [S, V, V, V, V], [((PAY_I, R), f32, V)])(
        meta, mine, theirs, begin, scales
    )
    sent = jnp.broadcast_to(sent.astype(f16)[None], (ROWS, PAY_I, R))
    here = lax.all_to_all(sent, CHIP, 0, 0)
    there = lax.ppermute(here, "c", swap)
    lines = here[:, BS, :BS].astype(f32)
    (moments,) = call(chip_moments, [V], [row])(lines)
    nexts = [lax.ppermute(moments, "x", ring(k)) for k in (1, 2, 3)]
    (shares,) = call(indiv_shares, [S] + [V] * 5, [((ROWS, BS), f32, V)])(
        meta, lines, moments, *nexts
    )
    change = (
        shares[:, 0].reshape(ROWS, 1, 1) * here[:, :BS].astype(f32)
        + shares[:, 1].reshape(ROWS, 1, 1) * there[:, :BS].astype(f32)
    )
    return variant_new, indiv_factors + change.reshape(ROWS * BS, R)


def solution(mesh):
    grid = np.asarray(mesh.devices).reshape(4, 4, 2, 4)
    inner = Mesh(grid, ALL)
    return jax.shard_map(
        on_device,
        mesh=inner,
        in_specs=(
            P("x", None),
            P(GEN, None),
            P(GEN, "x", None, None, None),
            P(GEN, "x", None),
            P(GEN, "x", None),
            P(GEN, "x"),
        ),
        out_specs=(P(GEN, None), P("x", None)),
        check_vma=False,
    )
```

```python
import jax
import jax.numpy as jnp
import numpy as np
from jax import lax
from jax.experimental import pallas as pl
from jax.experimental.pallas import tpu as pltpu
from jax.sharding import Mesh
from jax.sharding import PartitionSpec as P

BS = 128
R = 256
NB = 64
ROWS = 16
COLS = 8
smooth_weight = 32.0
ridge_weight = 1.0
f32, bf16, f16 = jnp.float32, jnp.bfloat16, jnp.float16
ALL = ("z", "y", "c", "x")
GEN = ("z", "y", "c")
CHIP = ("z", "y")
PAY_V = 2 * BS + 2 * BS + 16
PAY_I = BS + 8
VMEM_LIMIT = 16 * 1024 * 1024


def row_col():
    rows = lax.broadcasted_iota(jnp.int32, (BS, BS), 0)
    cols = lax.broadcasted_iota(jnp.int32, (BS, BS), 1)
    return rows, cols


def pack(gram):
    rows, cols = row_col()
    upper = gram[:BS, :BS]
    lower = gram[BS:, BS:]
    mixed = jnp.where(rows <= cols, upper, lower)
    diag = jnp.sum(jnp.where(rows == cols, lower, 0.0), axis=0, keepdims=True)
    return mixed, gram[:BS, BS:], diag


def unpack(mixed, cross, diag):
    rows, cols = row_col()
    turned = mixed.T
    upper = jnp.where(rows <= cols, mixed, turned)
    lower = jnp.where(rows > cols, mixed, jnp.where(rows < cols, turned, diag))
    top = jnp.concatenate([upper, cross], axis=1)
    bottom = jnp.concatenate([cross.T, lower], axis=1)
    return jnp.concatenate([top, bottom], axis=0)


def split(matrix):
    high = matrix.astype(bf16)
    return high, (matrix - high.astype(f32)).astype(bf16)


def times(values, high, low):
    rounded = values.astype(bf16)
    return jnp.dot(rounded, high, preferred_element_type=f32) + jnp.dot(
        rounded, low, preferred_element_type=f32
    )


def set_mask(ids, mask):
    def clear(k, carry):
        mask[k] = 0.0
        return carry

    lax.fori_loop(0, ROWS * COLS, clear, 0)

    def mark(s, carry):
        mask[ids[s] * COLS + ids[NB + s]] = 1.0
        return carry

    lax.fori_loop(0, ids[2 * NB], mark, 0)


def fill(ids, tiles, dense):
    def scatter(s, carry):
        rows = pl.ds(pl.multiple_of(ids[s] * BS, BS), BS)
        cols = pl.ds(pl.multiple_of(ids[NB + s] * BS, BS), BS)
        dense[rows, cols] = tiles[s]
        return carry

    lax.fori_loop(0, ids[2 * NB], scatter, 0)


def variant_sums(
    ids, meta, tiles_hbm, factors_hbm, own, far, mask,
    tiles, factors, dense, turned, rounded, grams, diags, sems,
):
    me, odd = meta[0], meta[1]
    quarter = ROWS * BS // 4
    loads = [
        pltpu.make_async_copy(
            factors_hbm.at[pl.ds(k * quarter, quarter), :],
            factors.at[pl.ds(k * quarter, quarter), :],
            sems.at[k],
        )
        for k in range(4)
    ]
    load_tiles = pltpu.make_async_copy(tiles_hbm.at[0, 0], tiles, sems.at[4])
    for load in loads:
        load.start()
    load_tiles.start()
    dense[...] = jnp.zeros_like(dense)
    set_mask(ids, mask)
    for r in range(ROWS):
        if r % 4 == 0:
            loads[r // 4].wait()
        block = factors[r * BS : (r + 1) * BS, :]
        rounded[r] = block.astype(bf16)
        turned[:, r * BS : (r + 1) * BS] = block.T.astype(bf16)
        gram = jnp.dot(turned[:, r * BS : (r + 1) * BS], rounded[r], preferred_element_type=f32)
        mixed, cross, diag = pack(gram)
        grams[r, :, :BS] = mixed
        grams[r, :, BS:] = cross
        diags[r : r + 1, :] = diag
    load_tiles.wait()
    fill(ids, tiles, dense)
    zero = jnp.zeros((16, R), f32)
    for k in range(4):
        at = lax.rem(me + k, 4)
        part = jnp.where(odd == 1, 3 - at, at)
        out = own if k == 0 else far.at[k - 1]
        cols = pl.ds(pl.multiple_of(part * 2 * BS, 2 * BS), 2 * BS)
        out[2 * BS : 4 * BS, :] = jnp.dot(
            turned[...], dense[:, cols], preferred_element_type=f32
        )
        out[4 * BS :, :] = zero
        for j in range(2):
            weights = [mask[r * COLS + part * 2 + j] for r in range(ROWS)]
            for piece in range(4):
                rows = slice(piece * 32, (piece + 1) * 32)
                total = weights[0] * grams[0, rows, :]
                for r in range(1, ROWS):
                    total += weights[r] * grams[r, rows, :]
                out[j * BS + piece * 32 : j * BS + (piece + 1) * 32, :] = total
            total = weights[0] * diags[0:1, :]
            for r in range(1, ROWS):
                total += weights[r] * diags[r : r + 1, :]
            out[4 * BS + j : 4 * BS + j + 1, :BS] = total


def band_of(values, before, after, ext):
    n = values.shape[0]
    ext[7:8, :] = before
    ext[8 : 8 + n, :] = values
    ext[8 + n : 9 + n, :] = after
    return 2.0 * values - ext[7 : 7 + n, :] - ext[9 : 9 + n, :]


def variant_start(meta, total, start, low, high, resid, applied, g_high, g_low, edge, ext):
    part = meta[0]
    n = 2 * BS
    first = pl.multiple_of(part * n, n)
    mine = start[pl.ds(first, n), :]
    before8 = start[pl.ds(pl.multiple_of(jnp.maximum(first - 8, 0), 8), 8), :]
    after8 = start[pl.ds(pl.multiple_of(jnp.minimum(first + n, 3 * n + n - 8), 8), 8), :]
    before = jnp.where(part == 0, low[7:8, :], before8[7:8, :])
    after = jnp.where(part == 3, high[0:1, :], after8[0:1, :])
    banded = band_of(mine, before, after, ext)
    data = total[2 * BS : 4 * BS, :].T
    for k in range(2):
        gram = unpack(
            total[k * BS : (k + 1) * BS, :BS],
            total[k * BS : (k + 1) * BS, BS:],
            total[4 * BS + k : 4 * BS + k + 1, :BS],
        )
        up, down = split(gram)
        g_high[k] = up
        g_low[k] = down
        rows = slice(k * BS, (k + 1) * BS)
        resid[rows, :] = (
            data[rows]
            - times(mine[rows], up, down)
            - ridge_weight * mine[rows]
            - smooth_weight * banded[rows]
        )
    value = resid[...]
    zero = jnp.zeros((1, R), f32)
    banded = band_of(value, zero, zero, ext)
    for k in range(2):
        rows = slice(k * BS, (k + 1) * BS)
        applied[rows, :] = (
            times(value[rows], g_high[k], g_low[k])
            + ridge_weight * value[rows]
            + smooth_weight * banded[rows]
        )
    edge[...] = jnp.zeros_like(edge)
    edge[0:1, :] = resid[0:1, :]
    edge[1:2, :] = applied[0:1, :]
    edge[2:3, :] = resid[n - 1 : n, :]
    edge[3:4, :] = applied[n - 1 : n, :]


def as_row(values):
    lanes = lax.broadcasted_iota(jnp.int32, (8, BS), 1)
    row = jnp.zeros((8, BS), f32)
    for k, value in enumerate(values):
        row = jnp.where(lanes == k, value, row)
    return row


def total_of(values):
    return jnp.sum(jnp.sum(values, axis=0, keepdims=True), axis=1, keepdims=True)


def largest(values):
    return jnp.max(jnp.max(jnp.abs(values), axis=0, keepdims=True), axis=1, keepdims=True)


def curve_of(rr, ra, aa, aaa):
    first = rr / ra
    rr_next = rr - 2.0 * first * ra + first * first * aa
    ratio = rr_next / rr
    curve = (
        (1.0 + ratio) * (1.0 + ratio) * ra
        - 2.0 * (1.0 + ratio) * first * aa
        + first * first * aaa
    )
    second = rr_next / curve
    return first + second * (1.0 + ratio), second * first, rr_next, curve


def variant_moments(
    meta, start, resid, applied, g_high, g_low, edge_before, edge_after, sent, moments, ext
):
    has_before, has_after = meta[1], meta[2]
    n = 2 * BS
    value = resid[...]
    zero = jnp.zeros((1, R), f32)
    low = jnp.concatenate([edge_before[2:3, :], jnp.zeros((n - 1, R), f32)], axis=0)
    high = jnp.concatenate([jnp.zeros((n - 1, R), f32), edge_after[0:1, :]], axis=0)
    first = applied[...] - smooth_weight * (low + high)
    before = jnp.where(has_before == 1, edge_before[3:4, :] - smooth_weight * value[0:1, :], zero)
    after = jnp.where(has_after == 1, edge_after[1:2, :] - smooth_weight * value[n - 1 : n, :], zero)
    banded = band_of(first, before, after, ext)
    data = jnp.concatenate(
        [times(first[k * BS : (k + 1) * BS], g_high[k], g_low[k]) for k in range(2)], axis=0
    )
    second = data + ridge_weight * first + smooth_weight * banded
    rr, ra = total_of(value * value), total_of(value * first)
    aa, aaa = total_of(first * first), total_of(first * second)
    near, far, rr_next, curve = curve_of(rr, ra, aa, aaa)
    good = (ra > 0.0) & (rr_next > 1e-3 * rr) & (curve > 0.0) & (far > 0.0)
    on_start = jnp.where(good, 1.0, 0.0)
    near = jnp.where(good, near, 0.0)
    far = jnp.where(good, far, -1.0)
    mine = start[pl.ds(pl.multiple_of(meta[0] * n, n), n), :]
    guess = on_start * mine + near * value - far * first
    peak_value, peak_guess = largest(value), largest(guess)
    unit_value = jnp.maximum(peak_value, 1e-30) / 16384.0
    unit_guess = jnp.maximum(peak_guess, 1e-30) / 16384.0
    sent[0] = value / unit_value
    sent[1] = guess / unit_guess
    moments[...] = as_row(
        [rr, ra, aa, aaa, peak_value, largest(first), on_start, near, far, unit_value, unit_guess]
    )


def new_variants(
    meta, ids, table, start, pieces, tiles_hbm, new_hbm, rounded, scales, dense, new, tiles, sems
):
    me, core, slab = meta[0], meta[1], meta[2]
    load = pltpu.make_async_copy(tiles_hbm.at[0, 0], tiles, sems.at[4])
    load.start()

    @pl.when(core == 1)
    def _():
        dense[...] = jnp.zeros_like(dense)

    sums = jnp.sum(table[...], axis=0, keepdims=True)
    peaks = jnp.max(table[...], axis=0, keepdims=True)
    on_resid, on_applied, _, _ = curve_of(*(sums[:, k : k + 1] for k in range(4)))
    n = 2 * BS
    keeps = []
    for k in range(4):
        owner = lax.rem(me - k + 4, 4)
        part = jnp.where(core == 1, 3 - owner, owner)
        rows = pl.ds(pl.multiple_of(part * n, n), n)
        line = table[pl.ds(slab * 4 + owner, 1), :]
        on_start, near, far, unit_value, unit_guess = (line[:, j : j + 1] for j in range(6, 11))
        share = on_applied / far
        value = (
            (1.0 - share * on_start) * start[rows, :]
            + ((on_resid - share * near) * unit_value) * pieces[k, 0]
            + (share * unit_guess) * pieces[k, 1]
        )
        new[rows, :] = value
        rounded[rows, :] = value.astype(bf16)
        keep = pltpu.make_async_copy(new.at[rows, :], new_hbm.at[rows, :], sems.at[k])
        keep.start()
        keeps.append(keep)
    top = jnp.abs(on_resid) * peaks[:, 4:5] + jnp.abs(on_applied) * peaks[:, 5:6] + 1.5
    scale_e = 30000.0 / (2.0 * 6.0 * COLS * BS * top)
    scale_h = 30000.0 / (2.0 * COLS * BS * top * top)
    scales[...] = as_row([scale_e, scale_h, 1.0 / scale_e, 1.0 / scale_h])
    load.wait()

    @pl.when(core == 1)
    def _():
        fill(ids, tiles, dense)

    for keep in keeps:
        keep.wait()


def tile_sums(scale, dense, rounded, pay):
    for r in range(ROWS):
        product = jnp.dot(
            dense[r * BS : (r + 1) * BS, :], rounded[...], preferred_element_type=f32
        )
        pay[r, :BS, :] = scale * product
        pay[r, BS:, :] = jnp.zeros((PAY_I - BS, R), f32)


def gram_sums(scale, mask, rounded, pay, grams, diags):
    for c in range(COLS):
        block = rounded[c * BS : (c + 1) * BS, :]
        turned = block.astype(f32).T.astype(bf16)
        gram = scale * jnp.dot(turned, block, preferred_element_type=f32)
        mixed, cross, diag = pack(gram)
        grams[c, :, :BS] = mixed
        grams[c, :, BS:] = cross
        diags[c : c + 1, :] = diag
    lines = lax.broadcasted_iota(jnp.int32, (PAY_I - BS, R), 0)
    for r in range(ROWS):
        weights = [mask[r * COLS + c] for c in range(COLS)]
        for piece in range(4):
            rows = slice(piece * 32, (piece + 1) * 32)
            total = weights[0] * grams[0, rows, :]
            for c in range(1, COLS):
                total += weights[c] * grams[c, rows, :]
            pay[r, rows, :] = total
        total = weights[0] * diags[0:1, :]
        for c in range(1, COLS):
            total += weights[c] * diags[c : c + 1, :]
        row = jnp.concatenate([total, jnp.zeros((1, BS), f32)], axis=1)
        pay[r, BS:, :] = jnp.where(lines == 0, row, 0.0)


def sums_to_send(meta, mask, scales, dense, rounded, pay, grams, diags):
    @pl.when(meta[1] == 1)
    def _():
        tile_sums(scales[0:1, 0:1], dense, rounded, pay)

    @pl.when(meta[1] == 0)
    def _():
        gram_sums(scales[0:1, 1:2], mask, rounded, pay, grams, diags)


def sums_to_keep(meta, ids, mask, scales, rounded, tiles_hbm, pay, dense, tiles, grams, diags, sem):
    load = pltpu.make_async_copy(tiles_hbm.at[0, 0], tiles, sem)
    load.start()

    @pl.when(meta[1] == 0)
    def _():
        dense[...] = jnp.zeros_like(dense)

    load.wait()

    @pl.when(meta[1] == 0)
    def _():
        fill(ids, tiles, dense)
        tile_sums(scales[0:1, 0:1], dense, rounded, pay)

    @pl.when(meta[1] == 1)
    def _():
        gram_sums(scales[0:1, 1:2], mask, rounded, pay, grams, diags)


def exponent_of(peak):
    return jnp.clip(jnp.ceil(jnp.log2(jnp.maximum(peak, 1e-30))), -100.0, 100.0)


def pieces_of(value):
    high = value.astype(bf16).astype(f32)
    rest = (value - high) * 256.0
    middle = rest.astype(bf16).astype(f32)
    return [high, middle, (rest - middle) * 256.0]


def indiv_moments(meta, mine, theirs, start, scales, sent):
    core = meta[1]
    own, far = mine[...], theirs[...]
    data = jnp.where(core == 0, own, far) * scales[0:1, 2:3]
    packed = jnp.where(core == 0, far, own) * scales[0:1, 3:4]
    high, low = split(unpack(packed[:BS, :BS], packed[:BS, BS:], packed[BS : BS + 1, :BS]))
    begin = start[...]
    value = data[:BS, :] - times(begin, high, low) - ridge_weight * begin
    first = times(value, high, low) + ridge_weight * value
    second = times(first, high, low) + ridge_weight * first
    powers = [exponent_of(largest(array)) for array in (value, first, second)]
    value, first, second = (
        array * jnp.exp2(-power) for array, power in zip((value, first, second), powers)
    )
    moments = [
        total_of(value * value),
        total_of(value * first),
        total_of(first * first),
        total_of(first * second),
    ]
    sent[:BS, :] = jnp.where(core == 0, value, first) * 16384.0
    row = as_row([part for moment in moments for part in pieces_of(moment)] + powers)
    sent[BS:, :] = jnp.concatenate([row, row], axis=1)


def chip_moments(lines, moments):
    def moment(k, power):
        parts = [lines[:, 3 * k + j : 3 * k + j + 1] for j in range(3)]
        value = parts[0] + parts[1] * (1.0 / 256.0) + parts[2] * (1.0 / 65536.0)
        return jnp.sum(value * power, axis=0, keepdims=True)

    one, two, three = (jnp.exp2(lines[:, j : j + 1]) for j in (12, 13, 14))
    moments[...] = as_row(
        [
            moment(0, one * one),
            moment(1, one * two),
            moment(2, two * two),
            moment(3, two * three),
        ]
    )


def indiv_shares(meta, lines, own, next1, next2, next3, shares):
    sums = own[0:1, :] + next1[0:1, :] + next2[0:1, :] + next3[0:1, :]
    on_resid, on_applied, _, _ = curve_of(*(sums[:, k : k + 1] for k in range(4)))
    of_resid = on_resid * jnp.exp2(lines[:, 12:13]) * (1.0 / 16384.0)
    of_applied = -on_applied * jnp.exp2(lines[:, 13:14]) * (1.0 / 16384.0)
    core = meta[1]
    lanes = lax.broadcasted_iota(jnp.int32, (ROWS, BS), 1)
    here = jnp.where(core == 0, of_resid, of_applied)
    there = jnp.where(core == 0, of_applied, of_resid)
    shares[...] = jnp.where(lanes == 0, here, there)


def ring(step):
    return [(k, (k + step) % 4) for k in range(4)]


def call(kernel, ins, outs, scratch=(), nbytes=1 << 20):
    def placed(shape, dtype, space):
        if space == pltpu.SMEM:
            return jax.ShapeDtypeStruct(shape, dtype)
        return space(shape, dtype)

    def run(*operands):
        operands = [
            pltpu.with_memory_space_constraint(x, pltpu.HBM) if space == pltpu.HBM else x
            for x, space in zip(operands, ins)
        ]
        return pl.pallas_call(
            kernel,
            out_shape=tuple(placed(*out) for out in outs),
            in_specs=[pl.BlockSpec(memory_space=space) for space in ins],
            out_specs=tuple(pl.BlockSpec(memory_space=out[2]) for out in outs),
            scratch_shapes=list(scratch),
            compiler_params=pltpu.CompilerParams(vmem_limit_bytes=VMEM_LIMIT),
            cost_estimate=pl.CostEstimate(flops=0, bytes_accessed=nbytes, transcendentals=0),
        )(*operands)

    return run


def on_device(indiv_factors, variant_factors, dosage_tiles, block_rows, block_cols, live_blocks):
    S, V, H = pltpu.SMEM, pltpu.VMEM, pltpu.HBM
    me = lax.axis_index("x")
    core = lax.axis_index("c")
    chip = lax.axis_index(CHIP)
    slab = lax.axis_index(GEN)
    part = jnp.where(core == 1, 3 - me, me)
    slabs = 32
    swap = [(0, 1), (1, 0)]
    meta = jnp.stack([me, core, slab]).astype(jnp.int32)
    ids = jnp.concatenate([block_rows[0, 0], block_cols[0, 0], live_blocks[0]])

    big = pltpu.VMEM((NB, BS, BS), bf16)
    flags = ((ROWS * COLS,), f32, S)
    own, far, mask = call(
        variant_sums,
        [S, S, H, H],
        [((PAY_V, R), f32, V), ((3, PAY_V, R), f32, V), flags],
        [
            big,
            pltpu.VMEM((ROWS * BS, R), f32),
            pltpu.VMEM((ROWS * BS, COLS * BS), bf16),
            pltpu.VMEM((R, ROWS * BS), bf16),
            pltpu.VMEM((ROWS, BS, R), bf16),
            pltpu.VMEM((ROWS, BS, R), f32),
            pltpu.VMEM((ROWS, BS), f32),
            pltpu.SemaphoreType.DMA((5,)),
        ],
        20 << 20,
    )(ids, meta, dosage_tiles, indiv_factors)
    far = far.astype(f16)
    got = [lax.ppermute(far[k - 1], "x", ring(k)) for k in (1, 2, 3)]
    low = lax.ppermute(variant_factors[-8:], GEN, [(k, k + 1) for k in range(slabs - 1)])
    high = lax.ppermute(variant_factors[:8], GEN, [(k + 1, k) for k in range(slabs - 1)])
    total = own + got[0].astype(f32) + got[1].astype(f32) + got[2].astype(f32)
    def device(position):
        at, place = divmod(position, 4)
        return at * 4 + (3 - place if at % 2 else place)

    line = [device(k) for k in range(4 * slabs)]
    position = slab * 4 + part
    meta_line = jnp.stack(
        [part, (position > 0).astype(jnp.int32), (position < 4 * slabs - 1).astype(jnp.int32)]
    ).astype(jnp.int32)
    square = ((2 * BS, R), f32, V)
    halves = ((2, R, R), bf16, V)
    row = ((8, BS), f32, V)
    ext = pltpu.VMEM((2 * BS + 16, R), f32)
    resid, applied, g_high, g_low, edge = call(
        variant_start,
        [S, V, V, V, V],
        [square, square, halves, halves, ((8, R), f32, V)],
        [ext],
    )(meta_line, total, variant_factors, low, high)
    edge_before = lax.ppermute(edge, ALL, list(zip(line[:-1], line[1:])))
    edge_after = lax.ppermute(edge, ALL, list(zip(line[1:], line[:-1])))
    sent, moments = call(variant_moments, [S] + [V] * 7, [((2, 2 * BS, R), f32, V), row], [ext])(
        meta_line, variant_factors, resid, applied, g_high, g_low, edge_before, edge_after
    )
    sent = sent.astype(f16)
    pieces = jnp.stack([sent] + [lax.ppermute(sent, "x", ring(k)) for k in (1, 2, 3)])
    pieces = pieces.astype(f32)
    table = lax.all_to_all(
        jnp.broadcast_to(moments[None, :1], (4 * slabs, 1, BS)), ALL, 0, 0
    ).reshape(4 * slabs, BS)

    whole = ((ROWS * BS, COLS * BS), bf16, V)
    variant_new, rounded, scales, dense = call(
        new_variants,
        [S, S, V, V, V, H],
        [((COLS * BS, R), f32, H), ((COLS * BS, R), bf16, V), row, whole],
        [pltpu.VMEM((COLS * BS, R), f32), big, pltpu.SemaphoreType.DMA((5,))],
    )(meta, ids, table, variant_factors, pieces, dosage_tiles)
    sums = ((ROWS, PAY_I, R), f32, V)
    scratch = [pltpu.VMEM((COLS, BS, R), f32), pltpu.VMEM((COLS, BS), f32)]
    (pay,) = call(sums_to_send, [S, S, V, V, V], [sums], scratch)(
        meta, mask, scales, dense, rounded
    )
    from_other = lax.ppermute(pay.astype(f16), "c", swap)
    (pay,) = call(
        sums_to_keep,
        [S, S, S, V, V, H],
        [sums],
        [pltpu.VMEM((ROWS * BS, COLS * BS), bf16), big, *scratch, pltpu.SemaphoreType.DMA],
        8 << 20,
    )(meta, ids, mask, scales, rounded, dosage_tiles)
    of_chip = (pay + from_other.astype(f32)).astype(f16)
    arrived = lax.all_to_all(of_chip, CHIP, 0, 0)
    mine = jnp.sum(arrived.astype(f32), axis=0)
    theirs = lax.ppermute(mine, "c", swap)
    begin = lax.dynamic_slice_in_dim(indiv_factors, chip * BS, BS, 0)
    (sent,) = call(indiv_moments, [S, V, V, V, V], [((PAY_I, R), f32, V)])(
        meta, mine, theirs, begin, scales
    )
    sent = jnp.broadcast_to(sent.astype(f16)[None], (ROWS, PAY_I, R))
    here = lax.all_to_all(sent, CHIP, 0, 0)
    there = lax.ppermute(here, "c", swap)
    lines = here[:, BS, :BS].astype(f32)
    (moments,) = call(chip_moments, [V], [row])(lines)
    nexts = [lax.ppermute(moments, "x", ring(k)) for k in (1, 2, 3)]
    (shares,) = call(indiv_shares, [S] + [V] * 5, [((ROWS, BS), f32, V)])(
        meta, lines, moments, *nexts
    )
    change = (
        shares[:, 0].reshape(ROWS, 1, 1) * here[:, :BS].astype(f32)
        + shares[:, 1].reshape(ROWS, 1, 1) * there[:, :BS].astype(f32)
    )
    return variant_new, indiv_factors + change.reshape(ROWS * BS, R)


def solution(mesh):
    grid = np.asarray(mesh.devices).reshape(4, 4, 2, 4)
    inner = Mesh(grid, ALL)
    return jax.shard_map(
        on_device,
        mesh=inner,
        in_specs=(
            P("x", None),
            P(GEN, None),
            P(GEN, "x", None, None, None),
            P(GEN, "x", None),
            P(GEN, "x", None),
            P(GEN, "x"),
        ),
        out_specs=(P(GEN, None), P("x", None)),
        check_vma=False,
    )
```

```python
import jax
import jax.numpy as jnp
import numpy as np
from jax import lax
from jax.experimental import pallas as pl
from jax.experimental.pallas import tpu as pltpu
from jax.sharding import Mesh
from jax.sharding import PartitionSpec as P

BS = 128
R = 256
NB = 64
ROWS = 16
COLS = 8
smooth_weight = 32.0
ridge_weight = 1.0
f32, bf16, f16 = jnp.float32, jnp.bfloat16, jnp.float16
ALL = ("z", "y", "c", "x")
GEN = ("z", "y", "c")
CHIP = ("z", "y")
PAY_V = 2 * BS + 2 * BS + 8
PAY_I = BS + 8
VMEM_LIMIT = 16 * 1024 * 1024


def row_col():
    rows = lax.broadcasted_iota(jnp.int32, (BS, BS), 0)
    cols = lax.broadcasted_iota(jnp.int32, (BS, BS), 1)
    return rows, cols


def pack(gram):
    rows, cols = row_col()
    upper = gram[:BS, :BS]
    lower = gram[BS:, BS:]
    mixed = jnp.where(rows <= cols, upper, lower)
    diag = jnp.sum(jnp.where(rows == cols, lower, 0.0), axis=0, keepdims=True)
    return mixed, gram[:BS, BS:], diag


def unpack(mixed, cross, diag):
    rows, cols = row_col()
    turned = mixed.T
    upper = jnp.where(rows <= cols, mixed, turned)
    lower = jnp.where(rows > cols, mixed, jnp.where(rows < cols, turned, diag))
    top = jnp.concatenate([upper, cross], axis=1)
    bottom = jnp.concatenate([cross.T, lower], axis=1)
    return jnp.concatenate([top, bottom], axis=0)


def split(matrix):
    high = matrix.astype(bf16)
    return high, (matrix - high.astype(f32)).astype(bf16)


def times(values, high, low):
    rounded = values.astype(bf16)
    return jnp.dot(rounded, high, preferred_element_type=f32) + jnp.dot(
        rounded, low, preferred_element_type=f32
    )


def scatter(row_of, col_of, live, tiles, dense, mask=None):
    def four(step, carry):
        for k in range(4):
            s = jnp.minimum(step * 4 + k, live - 1)
            row, col = row_of(s), col_of(s)
            rows = pl.ds(pl.multiple_of(row * BS, BS), BS)
            cols = pl.ds(pl.multiple_of(col * BS, BS), BS)
            dense[rows, cols] = tiles[s]
            if mask is not None:
                mask[row * COLS + col] = 1.0
        return carry

    lax.fori_loop(0, (live + 3) // 4, four, 0)


def fill(ids, tiles, dense):
    scatter(lambda s: ids[s], lambda s: ids[NB + s], ids[2 * NB], tiles, dense)


def variant_sums(
    meta, live, rows_hbm, cols_hbm, tiles_hbm, factors_hbm, own, far, mask,
    tiles, factors, dense, turned, rounded, grams, diags, ids, sems,
):
    me, odd = meta[0], meta[1]
    plan = [
        pltpu.make_async_copy(rows_hbm.at[0], ids.at[0], sems.at[5]),
        pltpu.make_async_copy(cols_hbm.at[0], ids.at[1], sems.at[6]),
    ]
    for load in plan:
        load.start()
    quarter = ROWS * BS // 4
    loads = [
        pltpu.make_async_copy(
            factors_hbm.at[pl.ds(k * quarter, quarter), :],
            factors.at[pl.ds(k * quarter, quarter), :],
            sems.at[k],
        )
        for k in range(4)
    ]
    load_tiles = pltpu.make_async_copy(tiles_hbm.at[0, 0], tiles, sems.at[4])
    for load in loads:
        load.start()
    load_tiles.start()
    dense[...] = jnp.zeros_like(dense)
    for cell in range(ROWS * COLS):
        mask[cell] = 0.0
    for r in range(ROWS):
        if r % 4 == 0:
            loads[r // 4].wait()
        block = factors[r * BS : (r + 1) * BS, :]
        rounded[r] = block.astype(bf16)
        turned[:, r * BS : (r + 1) * BS] = block.T.astype(bf16)
        gram = jnp.dot(turned[:, r * BS : (r + 1) * BS], rounded[r], preferred_element_type=f32)
        mixed, cross, diag = pack(gram)
        grams[r, :, :BS] = mixed
        grams[r, :, BS:] = cross
        diags[r : r + 1, :] = diag
    for load in plan:
        load.wait()
    load_tiles.wait()
    scatter(lambda s: ids[0, 0, s], lambda s: ids[1, 0, s], live[0, 0], tiles, dense, mask)
    zero = jnp.zeros((8, R), f32)
    for k in range(4):
        at = lax.rem(me + k, 4)
        part = jnp.where(odd == 1, 3 - at, at)
        out = own if k == 0 else far.at[k - 1]
        cols = pl.ds(pl.multiple_of(part * 2 * BS, 2 * BS), 2 * BS)
        out[2 * BS : 4 * BS, :] = jnp.dot(
            turned[...], dense[:, cols], preferred_element_type=f32
        )
        out[4 * BS :, :] = zero
        for j in range(2):
            weights = [mask[r * COLS + part * 2 + j] for r in range(ROWS)]
            for piece in range(4):
                rows = slice(piece * 32, (piece + 1) * 32)
                total = weights[0] * grams[0, rows, :]
                for r in range(1, ROWS):
                    total += weights[r] * grams[r, rows, :]
                out[j * BS + piece * 32 : j * BS + (piece + 1) * 32, :] = total
            total = weights[0] * diags[0:1, :]
            for r in range(1, ROWS):
                total += weights[r] * diags[r : r + 1, :]
            out[4 * BS + j : 4 * BS + j + 1, :BS] = total


def band_of(values, before, after, ext):
    n = values.shape[0]
    ext[7:8, :] = before
    ext[8 : 8 + n, :] = values
    ext[8 + n : 9 + n, :] = after
    return 2.0 * values - ext[7 : 7 + n, :] - ext[9 : 9 + n, :]


def variant_start(meta, total, start, low, high, resid, applied, g_high, g_low, edge, ext):
    part = meta[0]
    n = 2 * BS
    first = pl.multiple_of(part * n, n)
    mine = start[pl.ds(first, n), :]
    before8 = start[pl.ds(pl.multiple_of(jnp.maximum(first - 8, 0), 8), 8), :]
    after8 = start[pl.ds(pl.multiple_of(jnp.minimum(first + n, 3 * n + n - 8), 8), 8), :]
    before = jnp.where(part == 0, low[7:8, :], before8[7:8, :])
    after = jnp.where(part == 3, high[0:1, :], after8[0:1, :])
    banded = band_of(mine, before, after, ext)
    data = total[2 * BS : 4 * BS, :].T
    for k in range(2):
        gram = unpack(
            total[k * BS : (k + 1) * BS, :BS],
            total[k * BS : (k + 1) * BS, BS:],
            total[4 * BS + k : 4 * BS + k + 1, :BS],
        )
        up, down = split(gram)
        g_high[k] = up
        g_low[k] = down
        rows = slice(k * BS, (k + 1) * BS)
        resid[rows, :] = (
            data[rows]
            - times(mine[rows], up, down)
            - ridge_weight * mine[rows]
            - smooth_weight * banded[rows]
        )
    value = resid[...]
    zero = jnp.zeros((1, R), f32)
    banded = band_of(value, zero, zero, ext)
    for k in range(2):
        rows = slice(k * BS, (k + 1) * BS)
        applied[rows, :] = (
            times(value[rows], g_high[k], g_low[k])
            + ridge_weight * value[rows]
            + smooth_weight * banded[rows]
        )
    edge[...] = jnp.zeros_like(edge)
    edge[0:1, :] = resid[0:1, :]
    edge[1:2, :] = applied[0:1, :]
    edge[2:3, :] = resid[n - 1 : n, :]
    edge[3:4, :] = applied[n - 1 : n, :]


def as_row(values):
    lanes = lax.broadcasted_iota(jnp.int32, (8, BS), 1)
    row = jnp.zeros((8, BS), f32)
    for k, value in enumerate(values):
        row = jnp.where(lanes == k, value, row)
    return row


def total_of(values):
    return jnp.sum(jnp.sum(values, axis=0, keepdims=True), axis=1, keepdims=True)


def largest(values):
    return jnp.max(jnp.max(jnp.abs(values), axis=0, keepdims=True), axis=1, keepdims=True)


def curve_of(rr, ra, aa, aaa):
    first = rr / ra
    rr_next = rr - 2.0 * first * ra + first * first * aa
    ratio = rr_next / rr
    curve = (
        (1.0 + ratio) * (1.0 + ratio) * ra
        - 2.0 * (1.0 + ratio) * first * aa
        + first * first * aaa
    )
    second = rr_next / curve
    return first + second * (1.0 + ratio), second * first, rr_next, curve


def variant_moments(
    meta, start, resid, applied, g_high, g_low, edge_before, edge_after, sent, moments, ext
):
    has_before, has_after = meta[1], meta[2]
    n = 2 * BS
    value = resid[...]
    zero = jnp.zeros((1, R), f32)
    low = jnp.concatenate([edge_before[2:3, :], jnp.zeros((n - 1, R), f32)], axis=0)
    high = jnp.concatenate([jnp.zeros((n - 1, R), f32), edge_after[0:1, :]], axis=0)
    first = applied[...] - smooth_weight * (low + high)
    before = jnp.where(has_before == 1, edge_before[3:4, :] - smooth_weight * value[0:1, :], zero)
    after = jnp.where(has_after == 1, edge_after[1:2, :] - smooth_weight * value[n - 1 : n, :], zero)
    banded = band_of(first, before, after, ext)
    data = jnp.concatenate(
        [times(first[k * BS : (k + 1) * BS], g_high[k], g_low[k]) for k in range(2)], axis=0
    )
    second = data + ridge_weight * first + smooth_weight * banded
    rr, ra = total_of(value * value), total_of(value * first)
    aa, aaa = total_of(first * first), total_of(first * second)
    near, far, rr_next, curve = curve_of(rr, ra, aa, aaa)
    good = (ra > 0.0) & (rr_next > 1e-3 * rr) & (curve > 0.0) & (far > 0.0)
    on_start = jnp.where(good, 1.0, 0.0)
    near = jnp.where(good, near, 0.0)
    far = jnp.where(good, far, -1.0)
    mine = start[pl.ds(pl.multiple_of(meta[0] * n, n), n), :]
    guess = on_start * mine + near * value - far * first
    peak_value, peak_guess = largest(value), largest(guess)
    unit_value = jnp.maximum(peak_value, 1e-30) / 16384.0
    unit_guess = jnp.maximum(peak_guess, 1e-30) / 16384.0
    sent[0] = value / unit_value
    sent[1] = guess / unit_guess
    line = as_row(
        [rr, ra, aa, aaa, peak_value, largest(first), on_start, near, far, unit_value, unit_guess]
    )
    moments[...] = jnp.concatenate([line] * (moments.shape[0] // 8), axis=0)


def new_variants(
    meta, ids, table, start, pieces, tiles_hbm, new_hbm, rounded, scales, dense, new, tiles, sems
):
    me, core, slab = meta[0], meta[1], meta[2]
    load = pltpu.make_async_copy(tiles_hbm.at[0, 0], tiles, sems.at[4])
    load.start()

    @pl.when(core == 1)
    def _():
        dense[...] = jnp.zeros_like(dense)

    sums = jnp.sum(table[...], axis=0, keepdims=True)
    peaks = jnp.max(table[...], axis=0, keepdims=True)
    on_resid, on_applied, _, _ = curve_of(*(sums[:, k : k + 1] for k in range(4)))
    n = 2 * BS
    keeps = []
    for k in range(4):
        owner = lax.rem(me - k + 4, 4)
        part = jnp.where(core == 1, 3 - owner, owner)
        rows = pl.ds(pl.multiple_of(part * n, n), n)
        line = table[pl.ds(slab * 4 + owner, 1), :]
        on_start, near, far, unit_value, unit_guess = (line[:, j : j + 1] for j in range(6, 11))
        share = on_applied / far
        value = (
            (1.0 - share * on_start) * start[rows, :]
            + ((on_resid - share * near) * unit_value) * pieces[k, 0]
            + (share * unit_guess) * pieces[k, 1]
        )
        new[rows, :] = value
        rounded[rows, :] = value.astype(bf16)
        keep = pltpu.make_async_copy(new.at[rows, :], new_hbm.at[rows, :], sems.at[k])
        keep.start()
        keeps.append(keep)
    top = jnp.abs(on_resid) * peaks[:, 4:5] + jnp.abs(on_applied) * peaks[:, 5:6] + 1.5
    scale_e = 30000.0 / (2.0 * 6.0 * COLS * BS * top)
    scale_h = 30000.0 / (2.0 * COLS * BS * top * top)
    scales[...] = as_row([scale_e, scale_h, 1.0 / scale_e, 1.0 / scale_h])
    load.wait()

    @pl.when(core == 1)
    def _():
        fill(ids, tiles, dense)

    for keep in keeps:
        keep.wait()


def tile_sums(scale, dense, rounded, pay):
    for r in range(ROWS):
        product = jnp.dot(
            dense[r * BS : (r + 1) * BS, :], rounded[...], preferred_element_type=f32
        )
        pay[r, :BS, :] = scale * product
        pay[r, BS:, :] = jnp.zeros((PAY_I - BS, R), f32)


def gram_sums(scale, mask, rounded, pay, grams, diags):
    for c in range(COLS):
        block = rounded[c * BS : (c + 1) * BS, :]
        turned = block.astype(f32).T.astype(bf16)
        gram = scale * jnp.dot(turned, block, preferred_element_type=f32)
        mixed, cross, diag = pack(gram)
        grams[c, :, :BS] = mixed
        grams[c, :, BS:] = cross
        diags[c : c + 1, :] = diag
    lines = lax.broadcasted_iota(jnp.int32, (PAY_I - BS, R), 0)
    for r in range(ROWS):
        weights = [mask[r * COLS + c] for c in range(COLS)]
        for piece in range(4):
            rows = slice(piece * 32, (piece + 1) * 32)
            total = weights[0] * grams[0, rows, :]
            for c in range(1, COLS):
                total += weights[c] * grams[c, rows, :]
            pay[r, rows, :] = total
        total = weights[0] * diags[0:1, :]
        for c in range(1, COLS):
            total += weights[c] * diags[c : c + 1, :]
        row = jnp.concatenate([total, jnp.zeros((1, BS), f32)], axis=1)
        pay[r, BS:, :] = jnp.where(lines == 0, row, 0.0)


def sums_to_send(meta, mask, scales, dense, rounded, pay, grams, diags):
    @pl.when(meta[1] == 1)
    def _():
        tile_sums(scales[0:1, 0:1], dense, rounded, pay)

    @pl.when(meta[1] == 0)
    def _():
        gram_sums(scales[0:1, 1:2], mask, rounded, pay, grams, diags)


def sums_to_keep(meta, ids, mask, scales, rounded, tiles, pay, dense, grams, diags):
    @pl.when(meta[1] == 0)
    def _():
        dense[...] = jnp.zeros_like(dense)
        fill(ids, tiles.at[0, 0], dense)
        tile_sums(scales[0:1, 0:1], dense, rounded, pay)

    @pl.when(meta[1] == 1)
    def _():
        gram_sums(scales[0:1, 1:2], mask, rounded, pay, grams, diags)


def exponent_of(peak):
    return jnp.clip(jnp.ceil(jnp.log2(jnp.maximum(peak, 1e-30))), -100.0, 100.0)


def pieces_of(value):
    high = value.astype(bf16).astype(f32)
    rest = (value - high) * 256.0
    middle = rest.astype(bf16).astype(f32)
    return [high, middle, (rest - middle) * 256.0]


def indiv_moments(meta, mine, theirs, start, scales, sent):
    core = meta[1]
    own, far = mine[...], theirs[...]
    data = jnp.where(core == 0, own, far) * scales[0:1, 2:3]
    packed = jnp.where(core == 0, far, own) * scales[0:1, 3:4]
    high, low = split(unpack(packed[:BS, :BS], packed[:BS, BS:], packed[BS : BS + 1, :BS]))
    begin = start[...]
    value = data[:BS, :] - times(begin, high, low) - ridge_weight * begin
    first = times(value, high, low) + ridge_weight * value
    second = times(first, high, low) + ridge_weight * first
    powers = [exponent_of(largest(array)) for array in (value, first, second)]
    value, first, second = (
        array * jnp.exp2(-power) for array, power in zip((value, first, second), powers)
    )
    moments = [
        total_of(value * value),
        total_of(value * first),
        total_of(first * first),
        total_of(first * second),
    ]
    sent[:BS, :] = jnp.where(core == 0, value, first) * 16384.0
    row = as_row([part for moment in moments for part in pieces_of(moment)] + powers)
    sent[BS:, :] = jnp.concatenate([row, row], axis=1)


def chip_moments(lines, moments):
    def moment(k, power):
        parts = [lines[:, 3 * k + j : 3 * k + j + 1] for j in range(3)]
        value = parts[0] + parts[1] * (1.0 / 256.0) + parts[2] * (1.0 / 65536.0)
        return jnp.sum(value * power, axis=0, keepdims=True)

    one, two, three = (jnp.exp2(lines[:, j : j + 1]) for j in (12, 13, 14))
    moments[...] = as_row(
        [
            moment(0, one * one),
            moment(1, one * two),
            moment(2, two * two),
            moment(3, two * three),
        ]
    )


def indiv_shares(meta, lines, own, next1, next2, next3, shares):
    sums = own[0:1, :] + next1[0:1, :] + next2[0:1, :] + next3[0:1, :]
    on_resid, on_applied, _, _ = curve_of(*(sums[:, k : k + 1] for k in range(4)))
    of_resid = on_resid * jnp.exp2(lines[:, 12:13]) * (1.0 / 16384.0)
    of_applied = -on_applied * jnp.exp2(lines[:, 13:14]) * (1.0 / 16384.0)
    core = meta[1]
    lanes = lax.broadcasted_iota(jnp.int32, (ROWS, BS), 1)
    here = jnp.where(core == 0, of_resid, of_applied)
    there = jnp.where(core == 0, of_applied, of_resid)
    shares[...] = jnp.where(lanes == 0, here, there)


def ring(step):
    return [(k, (k + step) % 4) for k in range(4)]


def call(kernel, ins, outs, scratch=(), nbytes=1 << 20):
    def placed(shape, dtype, space):
        if space == pltpu.SMEM:
            return jax.ShapeDtypeStruct(shape, dtype)
        return space(shape, dtype)

    def run(*operands):
        operands = [
            pltpu.with_memory_space_constraint(x, pltpu.HBM) if space == pltpu.HBM else x
            for x, space in zip(operands, ins)
        ]
        return pl.pallas_call(
            kernel,
            out_shape=tuple(placed(*out) for out in outs),
            in_specs=[pl.BlockSpec(memory_space=space) for space in ins],
            out_specs=tuple(pl.BlockSpec(memory_space=out[2]) for out in outs),
            scratch_shapes=list(scratch),
            compiler_params=pltpu.CompilerParams(vmem_limit_bytes=VMEM_LIMIT),
            cost_estimate=pl.CostEstimate(flops=0, bytes_accessed=nbytes, transcendentals=0),
        )(*operands)

    return run


def on_device(indiv_factors, variant_factors, dosage_tiles, block_rows, block_cols, live_blocks):
    S, V, H = pltpu.SMEM, pltpu.VMEM, pltpu.HBM
    me = lax.axis_index("x")
    core = lax.axis_index("c")
    chip = lax.axis_index(CHIP)
    slab = lax.axis_index(GEN)
    part = jnp.where(core == 1, 3 - me, me)
    slabs = 32
    swap = [(0, 1), (1, 0)]
    meta = jnp.stack([me, core, slab]).astype(jnp.int32)
    ids = jnp.concatenate([block_rows[0, 0], block_cols[0, 0], live_blocks[0]])

    big = pltpu.VMEM((NB, BS, BS), bf16)
    flags = ((ROWS * COLS,), f32, S)
    own, far, mask = call(
        variant_sums,
        [S, S, H, H, H, H],
        [((PAY_V, R), f32, V), ((3, PAY_V, R), f32, V), flags],
        [
            big,
            pltpu.VMEM((ROWS * BS, R), f32),
            pltpu.VMEM((ROWS * BS, COLS * BS), bf16),
            pltpu.VMEM((R, ROWS * BS), bf16),
            pltpu.VMEM((ROWS, BS, R), bf16),
            pltpu.VMEM((ROWS, BS, R), f32),
            pltpu.VMEM((ROWS, BS), f32),
            pltpu.SMEM((2, 1, NB), jnp.int32),
            pltpu.SemaphoreType.DMA((7,)),
        ],
        20 << 20,
    )(meta, live_blocks, block_rows, block_cols, dosage_tiles, indiv_factors)
    far = far.astype(f16)
    got = [lax.ppermute(far[k - 1], "x", ring(k)) for k in (1, 2, 3)]
    low = lax.ppermute(variant_factors[-8:], GEN, [(k, k + 1) for k in range(slabs - 1)])
    high = lax.ppermute(variant_factors[:8], GEN, [(k + 1, k) for k in range(slabs - 1)])
    total = own + got[0].astype(f32) + got[1].astype(f32) + got[2].astype(f32)
    def device(position):
        at, place = divmod(position, 4)
        return at * 4 + (3 - place if at % 2 else place)

    line = [device(k) for k in range(4 * slabs)]
    position = slab * 4 + part
    meta_line = jnp.stack(
        [part, (position > 0).astype(jnp.int32), (position < 4 * slabs - 1).astype(jnp.int32)]
    ).astype(jnp.int32)
    square = ((2 * BS, R), f32, V)
    halves = ((2, R, R), bf16, V)
    row = ((8, BS), f32, V)
    ext = pltpu.VMEM((2 * BS + 16, R), f32)
    resid, applied, g_high, g_low, edge = call(
        variant_start,
        [S, V, V, V, V],
        [square, square, halves, halves, ((8, R), f32, V)],
        [ext],
    )(meta_line, total, variant_factors, low, high)
    edge_before = lax.ppermute(edge, ALL, list(zip(line[:-1], line[1:])))
    edge_after = lax.ppermute(edge, ALL, list(zip(line[1:], line[:-1])))
    sent, moments = call(variant_moments, [S] + [V] * 7, [((2, 2 * BS, R), f32, V), ((4 * slabs, BS), f32, V)], [ext])(
        meta_line, variant_factors, resid, applied, g_high, g_low, edge_before, edge_after
    )
    sent = sent.astype(f16)
    pieces = jnp.stack([sent] + [lax.ppermute(sent, "x", ring(k)) for k in (1, 2, 3)])
    pieces = pieces.astype(f32)
    table = lax.all_to_all(
        moments.reshape(4 * slabs, 1, BS), ALL, 0, 0
    ).reshape(4 * slabs, BS)

    whole = ((ROWS * BS, COLS * BS), bf16, V)
    variant_new, rounded, scales, dense = call(
        new_variants,
        [S, S, V, V, V, H],
        [((COLS * BS, R), f32, H), ((COLS * BS, R), bf16, V), row, whole],
        [pltpu.VMEM((COLS * BS, R), f32), big, pltpu.SemaphoreType.DMA((5,))],
    )(meta, ids, table, variant_factors, pieces, dosage_tiles)
    sums = ((ROWS, PAY_I, R), f32, V)
    scratch = [pltpu.VMEM((COLS, BS, R), f32), pltpu.VMEM((COLS, BS), f32)]
    (pay,) = call(sums_to_send, [S, S, V, V, V], [sums], scratch)(
        meta, mask, scales, dense, rounded
    )
    from_other = lax.ppermute(pay.astype(f16), "c", swap)
    (pay,) = call(
        sums_to_keep,
        [S, S, S, V, V, V],
        [sums],
        [pltpu.VMEM((ROWS * BS, COLS * BS), bf16), *scratch],
        8 << 20,
    )(meta, ids, mask, scales, rounded, dosage_tiles)
    of_chip = (pay + from_other.astype(f32)).astype(f16)
    arrived = lax.all_to_all(of_chip, CHIP, 0, 0)
    mine = jnp.sum(arrived.astype(f32), axis=0)
    theirs = lax.ppermute(mine, "c", swap)
    begin = lax.dynamic_slice_in_dim(indiv_factors, chip * BS, BS, 0)
    (sent,) = call(indiv_moments, [S, V, V, V, V], [((PAY_I, R), f32, V)])(
        meta, mine, theirs, begin, scales
    )
    sent = jnp.broadcast_to(sent.astype(f16)[None], (ROWS, PAY_I, R))
    here = lax.all_to_all(sent, CHIP, 0, 0)
    there = lax.ppermute(here, "c", swap)
    lines = here[:, BS, :BS].astype(f32)
    (moments,) = call(chip_moments, [V], [row])(lines)
    nexts = [lax.ppermute(moments, "x", ring(k)) for k in (1, 2, 3)]
    (shares,) = call(indiv_shares, [S] + [V] * 5, [((ROWS, BS), f32, V)])(
        meta, lines, moments, *nexts
    )
    change = (
        shares[:, 0].reshape(ROWS, 1, 1) * here[:, :BS].astype(f32)
        + shares[:, 1].reshape(ROWS, 1, 1) * there[:, :BS].astype(f32)
    )
    indiv_new = indiv_factors.reshape(ROWS, BS, R) + change
    return variant_new, indiv_new.reshape(ROWS * BS, R)


def solution(mesh):
    grid = np.asarray(mesh.devices).reshape(4, 4, 2, 4)
    inner = Mesh(grid, ALL)
    return jax.shard_map(
        on_device,
        mesh=inner,
        in_specs=(
            P("x", None),
            P(GEN, None),
            P(GEN, "x", None, None, None),
            P(GEN, "x", None),
            P(GEN, "x", None),
            P(GEN, "x"),
        ),
        out_specs=(P(GEN, None), P("x", None)),
        check_vma=False,
    )
```

```python
import jax
import jax.numpy as jnp
import numpy as np
from jax import lax
from jax.experimental import pallas as pl
from jax.experimental.pallas import tpu as pltpu
from jax.sharding import Mesh
from jax.sharding import PartitionSpec as P

BS = 128
R = 256
NB = 64
ROWS = 16
COLS = 8
smooth_weight = 32.0
ridge_weight = 1.0
f32, bf16, f16 = jnp.float32, jnp.bfloat16, jnp.float16
ALL = ("z", "y", "c", "x")
GEN = ("z", "y", "c")
CHIP = ("z", "y")
PAY_V = 2 * BS + 2 * BS + 8
PAY_I = BS + 8
VMEM_LIMIT = 16 * 1024 * 1024


def row_col():
    rows = lax.broadcasted_iota(jnp.int32, (BS, BS), 0)
    cols = lax.broadcasted_iota(jnp.int32, (BS, BS), 1)
    return rows, cols


def pack(gram):
    rows, cols = row_col()
    upper = gram[:BS, :BS]
    lower = gram[BS:, BS:]
    mixed = jnp.where(rows <= cols, upper, lower)
    diag = jnp.sum(jnp.where(rows == cols, lower, 0.0), axis=0, keepdims=True)
    return mixed, gram[:BS, BS:], diag


def unpack(mixed, cross, diag):
    rows, cols = row_col()
    turned = mixed.T
    upper = jnp.where(rows <= cols, mixed, turned)
    lower = jnp.where(rows > cols, mixed, jnp.where(rows < cols, turned, diag))
    top = jnp.concatenate([upper, cross], axis=1)
    bottom = jnp.concatenate([cross.T, lower], axis=1)
    return jnp.concatenate([top, bottom], axis=0)


def split(matrix):
    high = matrix.astype(bf16)
    return high, (matrix - high.astype(f32)).astype(bf16)


def times(values, high, low):
    rounded = values.astype(bf16)
    return jnp.dot(rounded, high, preferred_element_type=f32) + jnp.dot(
        rounded, low, preferred_element_type=f32
    )


def scatter(row_of, col_of, live, tiles, dense, mask=None):
    def four(step, carry):
        for k in range(4):
            s = jnp.minimum(step * 4 + k, live - 1)
            row, col = row_of(s), col_of(s)
            rows = pl.ds(pl.multiple_of(row * BS, BS), BS)
            cols = pl.ds(pl.multiple_of(col * BS, BS), BS)
            dense[rows, cols] = tiles[s]
            if mask is not None:
                mask[row * COLS + col] = 1.0
        return carry

    lax.fori_loop(0, (live + 3) // 4, four, 0)


def fill(ids, tiles, dense):
    scatter(lambda s: ids[s], lambda s: ids[NB + s], ids[2 * NB], tiles, dense)


def variant_sums(
    meta, live, rows_hbm, cols_hbm, tiles_hbm, factors_hbm, start_hbm,
    own, far, mask, upward, downward,
    tiles, factors, dense, turned, rounded, grams, diags, ids, sides, rims, sems,
):
    me = meta[0]
    plan = [
        pltpu.make_async_copy(rows_hbm.at[0], ids.at[0], sems.at[5]),
        pltpu.make_async_copy(cols_hbm.at[0], ids.at[1], sems.at[6]),
    ]
    for c in range(COLS):
        first = c * BS if c % 2 == 0 else (c + 1) * BS - 8
        plan.append(
            pltpu.make_async_copy(
                start_hbm.at[pl.ds(first, 8), :], sides.at[pl.ds(8 * c, 8), :], sems.at[7 + c]
            )
        )
    for load in plan:
        load.start()
    quarter = ROWS * BS // 4
    loads = [
        pltpu.make_async_copy(
            factors_hbm.at[pl.ds(k * quarter, quarter), :],
            factors.at[pl.ds(k * quarter, quarter), :],
            sems.at[k],
        )
        for k in range(4)
    ]
    load_tiles = pltpu.make_async_copy(tiles_hbm.at[0, 0], tiles, sems.at[4])
    for load in loads:
        load.start()
    load_tiles.start()
    dense[...] = jnp.zeros_like(dense)
    for cell in range(ROWS * COLS):
        mask[cell] = 0.0
    for r in range(ROWS):
        if r % 4 == 0:
            loads[r // 4].wait()
        block = factors[r * BS : (r + 1) * BS, :]
        rounded[r * BS : (r + 1) * BS, :] = block.astype(bf16)
        turned[:, r * BS : (r + 1) * BS] = block.T.astype(bf16)
        gram = jnp.dot(
            turned[:, r * BS : (r + 1) * BS],
            rounded[r * BS : (r + 1) * BS, :],
            preferred_element_type=f32,
        )
        mixed, cross, diag = pack(gram)
        grams[r, :, :BS] = mixed
        grams[r, :, BS:] = cross
        diags[r : r + 1, :] = diag
    for load in plan:
        load.wait()
    load_tiles.wait()
    scatter(lambda s: ids[0, 0, s], lambda s: ids[1, 0, s], live[0, 0], tiles, dense, mask)
    zero = jnp.zeros((8, R), f32)
    for k in range(4):
        part = lax.rem(me + k, 4)
        out = own if k == 0 else far.at[k - 1]
        cols = pl.ds(pl.multiple_of(part * 2 * BS, 2 * BS), 2 * BS)
        data = jnp.dot(turned[...], dense[:, cols], preferred_element_type=f32)
        out[2 * BS : 4 * BS, :] = data
        rims[pl.ds(2 * part, 1), :] = data[:, :BS].T[0:1, :]
        rims[pl.ds(2 * part + 1, 1), :] = data[:, BS:].T[BS - 1 : BS, :]
        out[4 * BS :, :] = zero
        for j in range(2):
            weights = [mask[r * COLS + part * 2 + j] for r in range(ROWS)]
            for piece in range(4):
                rows = slice(piece * 32, (piece + 1) * 32)
                total = weights[0] * grams[0, rows, :]
                for r in range(1, ROWS):
                    total += weights[r] * grams[r, rows, :]
                out[j * BS + piece * 32 : j * BS + (piece + 1) * 32, :] = total
            total = weights[0] * diags[0:1, :]
            for r in range(1, ROWS):
                total += weights[r] * diags[r : r + 1, :]
            out[4 * BS + j : 4 * BS + j + 1, :BS] = total
    edges = [sides[8 * c + (0 if c % 2 == 0 else 7) : 8 * c + (1 if c % 2 == 0 else 8), :] for c in range(COLS)]
    met = jnp.dot(
        jnp.concatenate(edges, axis=0).astype(bf16), turned[...], preferred_element_type=f32
    )
    lines = lax.broadcasted_iota(jnp.int32, (COLS, BS), 0)
    live_cells = []
    for r in range(ROWS):
        cells = jnp.zeros((COLS, BS), f32)
        for c in range(COLS):
            cells = jnp.where(lines == c, mask[r * COLS + c], cells)
        live_cells.append(cells)
    high, low = split(met * jnp.concatenate(live_cells, axis=1))
    rims[...] -= jnp.dot(high, rounded[...], preferred_element_type=f32) + jnp.dot(
        low, rounded[...], preferred_element_type=f32
    )
    for k in range(4):
        part = lax.rem(me + k, 4)
        out = own if k == 0 else far.at[k - 1]
        out[4 * BS + 2 : 4 * BS + 3, :] = rims[pl.ds(jnp.maximum(2 * part - 1, 0), 1), :]
        out[4 * BS + 3 : 4 * BS + 4, :] = rims[pl.ds(jnp.minimum(2 * part + 2, COLS - 1), 1), :]
    upward[...] = jnp.concatenate(
        [sides[8 * COLS - 2 : 8 * COLS, :], rims[COLS - 1 : COLS, :], jnp.zeros((5, R), f32)], axis=0
    )
    downward[...] = jnp.concatenate(
        [sides[0:2, :], rims[0:1, :], jnp.zeros((5, R), f32)], axis=0
    )


def band_of(values, before, after, ext):
    n = values.shape[0]
    ext[7:8, :] = before
    ext[8 : 8 + n, :] = values
    ext[8 + n : 9 + n, :] = after
    return 2.0 * values - ext[7 : 7 + n, :] - ext[9 : 9 + n, :]


def as_row(values):
    lanes = lax.broadcasted_iota(jnp.int32, (8, BS), 1)
    row = jnp.zeros((8, BS), f32)
    for k, value in enumerate(values):
        row = jnp.where(lanes == k, value, row)
    return row


def total_of(values):
    return jnp.sum(jnp.sum(values, axis=0, keepdims=True), axis=1, keepdims=True)


def largest(values):
    return jnp.max(jnp.max(jnp.abs(values), axis=0, keepdims=True), axis=1, keepdims=True)


def curve_of(rr, ra, aa, aaa):
    first = rr / ra
    rr_next = rr - 2.0 * first * ra + first * first * aa
    ratio = rr_next / rr
    curve = (
        (1.0 + ratio) * (1.0 + ratio) * ra
        - 2.0 * (1.0 + ratio) * first * aa
        + first * first * aaa
    )
    second = rr_next / curve
    return first + second * (1.0 + ratio), second * first, rr_next, curve


def variant_moments(
    meta, total, start, near0, near1, near2, near3, sent, table, g_high, g_low, ext
):
    part, has_before, has_after = meta[0], meta[1], meta[2]
    n = 2 * BS
    first_row = pl.multiple_of(part * n, n)
    mine = start[pl.ds(first_row, n), :]
    before8 = start[pl.ds(pl.multiple_of(jnp.maximum(first_row - 8, 0), 8), 8), :]
    after8 = start[pl.ds(pl.multiple_of(jnp.minimum(first_row + n, 4 * n - 8), 8), 8), :]
    at_low, at_high = part == 0, part == 3
    before = jnp.where(at_low, near0[1:2, :], before8[7:8, :])
    before2 = jnp.where(at_low, near0[0:1, :], before8[6:7, :])
    after = jnp.where(at_high, near0[8:9, :], after8[0:1, :])
    after2 = jnp.where(at_high, near0[9:10, :], after8[1:2, :])
    banded = band_of(mine, before, after, ext)
    data = total[2 * BS : 4 * BS, :].T
    pieces = []
    for k in range(2):
        gram = unpack(
            total[k * BS : (k + 1) * BS, :BS],
            total[k * BS : (k + 1) * BS, BS:],
            total[4 * BS + k : 4 * BS + k + 1, :BS],
        )
        g_high[k], g_low[k] = split(gram)
        rows = slice(k * BS, (k + 1) * BS)
        pieces.append(
            data[rows]
            - times(mine[rows], g_high[k], g_low[k])
            - ridge_weight * mine[rows]
            - smooth_weight * banded[rows]
        )
    value = jnp.concatenate(pieces, axis=0)
    low = near0[2:3, :] + near1[2:3, :] + near2[2:3, :] + near3[2:3, :]
    high = near0[10:11, :] + near1[10:11, :] + near2[10:11, :] + near3[10:11, :]
    low = jnp.where(at_low, low, total[4 * BS + 2 : 4 * BS + 3, :])
    high = jnp.where(at_high, high, total[4 * BS + 3 : 4 * BS + 4, :])
    low = low - ridge_weight * before - smooth_weight * (2.0 * before - before2 - mine[0:1, :])
    high = high - ridge_weight * after - smooth_weight * (2.0 * after - after2 - mine[n - 1 : n, :])
    zero = jnp.zeros((1, R), f32)
    low = jnp.where(has_before == 1, low, zero)
    high = jnp.where(has_after == 1, high, zero)

    def operator(values, banded):
        data = [times(values[k * BS : (k + 1) * BS], g_high[k], g_low[k]) for k in range(2)]
        return jnp.concatenate(data, axis=0) + ridge_weight * values + smooth_weight * banded

    first = operator(value, band_of(value, low, high, ext))
    second = operator(first, band_of(first, zero, zero, ext))
    rr, ra = total_of(value * value), total_of(value * first)
    aa, aaa = total_of(first * first), total_of(first * second)
    near, far, rr_next, curve = curve_of(rr, ra, aa, aaa)
    good = (ra > 0.0) & (rr_next > 1e-3 * rr) & (curve > 0.0) & (far > 0.0)
    on_start = jnp.where(good, 1.0, 0.0)
    near = jnp.where(good, near, 0.0)
    far = jnp.where(good, far, -1.0)
    guess = on_start * mine + near * value - far * first
    peak_value, peak_guess = largest(value), largest(guess)
    unit_value = jnp.maximum(peak_value, 1e-30) / 16384.0
    unit_guess = jnp.maximum(peak_guess, 1e-30) / 16384.0
    sent[0] = value / unit_value
    sent[1] = guess / unit_guess
    line = as_row(
        [rr, ra, aa, aaa, peak_value, largest(first), on_start, near, far, unit_value, unit_guess]
    )
    five = jnp.concatenate(
        [
            line[0:1, :],
            first[0:1, :BS],
            first[0:1, BS:],
            first[n - 1 : n, :BS],
            first[n - 1 : n, BS:],
        ],
        axis=0,
    )
    forty = jnp.concatenate([five] * 8, axis=0)
    for k in range(table.shape[0] // 40):
        table[40 * k : 40 * (k + 1), :] = forty


def new_variants(
    meta, ids, table, start, pieces, tiles_hbm, new_hbm, rounded, scales, dense, new, tiles, sems
):
    me, core, slab = meta[0], meta[1], meta[2]
    load = pltpu.make_async_copy(tiles_hbm.at[0, 0], tiles, sems.at[4])
    load.start()

    @pl.when(core == 1)
    def _():
        dense[...] = jnp.zeros_like(dense)

    parts = table.shape[0] // 5
    lines = table[pl.ds(0, parts, stride=5), :]
    sums = jnp.sum(lines, axis=0, keepdims=True)
    peaks = jnp.max(lines, axis=0, keepdims=True)
    across = sum(
        table[pl.ds(3 + half, parts - 1, stride=5), :] * table[pl.ds(6 + half, parts - 1, stride=5), :]
        for half in range(2)
    )
    rr, ra, aa, aaa = (sums[:, k : k + 1] for k in range(4))
    on_resid, on_applied, _, _ = curve_of(rr, ra, aa, aaa - 2.0 * smooth_weight * total_of(across))
    n = 2 * BS
    keeps = []
    for k in range(4):
        owner = lax.rem(me - k + 4, 4)
        rows = pl.ds(pl.multiple_of(owner * n, n), n)
        line = table[pl.ds((slab * 4 + owner) * 5, 1), :]
        on_start, near, far, unit_value, unit_guess = (line[:, j : j + 1] for j in range(6, 11))
        share = on_applied / far
        value = (
            (1.0 - share * on_start) * start[rows, :]
            + ((on_resid - share * near) * unit_value) * pieces[k, 0]
            + (share * unit_guess) * pieces[k, 1]
        )
        new[rows, :] = value
        rounded[rows, :] = value.astype(bf16)
        keep = pltpu.make_async_copy(new.at[rows, :], new_hbm.at[rows, :], sems.at[k])
        keep.start()
        keeps.append(keep)
    top = jnp.abs(on_resid) * peaks[:, 4:5] + jnp.abs(on_applied) * peaks[:, 5:6] + 1.5
    scale_e = 30000.0 / (2.0 * 6.0 * COLS * BS * top)
    scale_h = 30000.0 / (2.0 * COLS * BS * top * top)
    scales[...] = as_row([scale_e, scale_h, 1.0 / scale_e, 1.0 / scale_h])
    load.wait()

    @pl.when(core == 1)
    def _():
        fill(ids, tiles, dense)

    for keep in keeps:
        keep.wait()


def tile_sums(scale, dense, rounded, pay):
    for r in range(ROWS):
        product = jnp.dot(
            dense[r * BS : (r + 1) * BS, :], rounded[...], preferred_element_type=f32
        )
        pay[r, :BS, :] = scale * product
        pay[r, BS:, :] = jnp.zeros((PAY_I - BS, R), f32)


def gram_sums(scale, mask, rounded, pay, grams, diags):
    for c in range(COLS):
        block = rounded[c * BS : (c + 1) * BS, :]
        turned = block.astype(f32).T.astype(bf16)
        gram = scale * jnp.dot(turned, block, preferred_element_type=f32)
        mixed, cross, diag = pack(gram)
        grams[c, :, :BS] = mixed
        grams[c, :, BS:] = cross
        diags[c : c + 1, :] = diag
    lines = lax.broadcasted_iota(jnp.int32, (PAY_I - BS, R), 0)
    for r in range(ROWS):
        weights = [mask[r * COLS + c] for c in range(COLS)]
        for piece in range(4):
            rows = slice(piece * 32, (piece + 1) * 32)
            total = weights[0] * grams[0, rows, :]
            for c in range(1, COLS):
                total += weights[c] * grams[c, rows, :]
            pay[r, rows, :] = total
        total = weights[0] * diags[0:1, :]
        for c in range(1, COLS):
            total += weights[c] * diags[c : c + 1, :]
        row = jnp.concatenate([total, jnp.zeros((1, BS), f32)], axis=1)
        pay[r, BS:, :] = jnp.where(lines == 0, row, 0.0)


def sums_to_send(meta, mask, scales, dense, rounded, pay, grams, diags):
    @pl.when(meta[1] == 1)
    def _():
        tile_sums(scales[0:1, 0:1], dense, rounded, pay)

    @pl.when(meta[1] == 0)
    def _():
        gram_sums(scales[0:1, 1:2], mask, rounded, pay, grams, diags)


def sums_to_keep(meta, ids, mask, scales, rounded, tiles, pay, dense, grams, diags):
    @pl.when(meta[1] == 0)
    def _():
        dense[...] = jnp.zeros_like(dense)
        fill(ids, tiles.at[0, 0], dense)
        tile_sums(scales[0:1, 0:1], dense, rounded, pay)

    @pl.when(meta[1] == 1)
    def _():
        gram_sums(scales[0:1, 1:2], mask, rounded, pay, grams, diags)


def exponent_of(peak):
    return jnp.clip(jnp.ceil(jnp.log2(jnp.maximum(peak, 1e-30))), -100.0, 100.0)


def pieces_of(value):
    high = value.astype(bf16).astype(f32)
    rest = (value - high) * 256.0
    middle = rest.astype(bf16).astype(f32)
    return [high, middle, (rest - middle) * 256.0]


def indiv_moments(meta, mine, theirs, start, scales, sent):
    core = meta[1]
    own, far = mine[...], theirs[...]
    data = jnp.where(core == 0, own, far) * scales[0:1, 2:3]
    packed = jnp.where(core == 0, far, own) * scales[0:1, 3:4]
    high, low = split(unpack(packed[:BS, :BS], packed[:BS, BS:], packed[BS : BS + 1, :BS]))
    begin = start[...]
    value = data[:BS, :] - times(begin, high, low) - ridge_weight * begin
    first = times(value, high, low) + ridge_weight * value
    second = times(first, high, low) + ridge_weight * first
    powers = [exponent_of(largest(array)) for array in (value, first, second)]
    value, first, second = (
        array * jnp.exp2(-power) for array, power in zip((value, first, second), powers)
    )
    moments = [
        total_of(value * value),
        total_of(value * first),
        total_of(first * first),
        total_of(first * second),
    ]
    sent[:BS, :] = jnp.where(core == 0, value, first) * 16384.0
    row = as_row([part for moment in moments for part in pieces_of(moment)] + powers)
    sent[BS:, :] = jnp.concatenate([row, row], axis=1)


def chip_moments(lines, moments):
    def moment(k, power):
        parts = [lines[:, 3 * k + j : 3 * k + j + 1] for j in range(3)]
        value = parts[0] + parts[1] * (1.0 / 256.0) + parts[2] * (1.0 / 65536.0)
        return jnp.sum(value * power, axis=0, keepdims=True)

    one, two, three = (jnp.exp2(lines[:, j : j + 1]) for j in (12, 13, 14))
    moments[...] = as_row(
        [
            moment(0, one * one),
            moment(1, one * two),
            moment(2, two * two),
            moment(3, two * three),
        ]
    )


def indiv_shares(meta, lines, own, next1, next2, next3, shares):
    sums = own[0:1, :] + next1[0:1, :] + next2[0:1, :] + next3[0:1, :]
    on_resid, on_applied, _, _ = curve_of(*(sums[:, k : k + 1] for k in range(4)))
    of_resid = on_resid * jnp.exp2(lines[:, 12:13]) * (1.0 / 16384.0)
    of_applied = -on_applied * jnp.exp2(lines[:, 13:14]) * (1.0 / 16384.0)
    core = meta[1]
    lanes = lax.broadcasted_iota(jnp.int32, (ROWS, BS), 1)
    here = jnp.where(core == 0, of_resid, of_applied)
    there = jnp.where(core == 0, of_applied, of_resid)
    shares[...] = jnp.where(lanes == 0, here, there)


def ring(step):
    return [(k, (k + step) % 4) for k in range(4)]


def call(kernel, ins, outs, scratch=(), nbytes=1 << 20):
    def placed(shape, dtype, space):
        if space == pltpu.SMEM:
            return jax.ShapeDtypeStruct(shape, dtype)
        return space(shape, dtype)

    def run(*operands):
        operands = [
            pltpu.with_memory_space_constraint(x, pltpu.HBM) if space == pltpu.HBM else x
            for x, space in zip(operands, ins)
        ]
        return pl.pallas_call(
            kernel,
            out_shape=tuple(placed(*out) for out in outs),
            in_specs=[pl.BlockSpec(memory_space=space) for space in ins],
            out_specs=tuple(pl.BlockSpec(memory_space=out[2]) for out in outs),
            scratch_shapes=list(scratch),
            compiler_params=pltpu.CompilerParams(vmem_limit_bytes=VMEM_LIMIT),
            cost_estimate=pl.CostEstimate(flops=0, bytes_accessed=nbytes, transcendentals=0),
        )(*operands)

    return run


def on_device(indiv_factors, variant_factors, dosage_tiles, block_rows, block_cols, live_blocks):
    S, V, H = pltpu.SMEM, pltpu.VMEM, pltpu.HBM
    me = lax.axis_index("x")
    core = lax.axis_index("c")
    chip = lax.axis_index(CHIP)
    slab = lax.axis_index(GEN)
    slabs = 32
    swap = [(0, 1), (1, 0)]
    meta = jnp.stack([me, core, slab]).astype(jnp.int32)
    ids = jnp.concatenate([block_rows[0, 0], block_cols[0, 0], live_blocks[0]])

    big = pltpu.VMEM((NB, BS, BS), bf16)
    flags = ((ROWS * COLS,), f32, S)
    edge = ((8, R), f32, V)
    own, far, mask, upward, downward = call(
        variant_sums,
        [S, S, H, H, H, H, H],
        [((PAY_V, R), f32, V), ((3, PAY_V, R), f32, V), flags, edge, edge],
        [
            big,
            pltpu.VMEM((ROWS * BS, R), f32),
            pltpu.VMEM((ROWS * BS, COLS * BS), bf16),
            pltpu.VMEM((R, ROWS * BS), bf16),
            pltpu.VMEM((ROWS * BS, R), bf16),
            pltpu.VMEM((ROWS, BS, R), f32),
            pltpu.VMEM((ROWS, BS), f32),
            pltpu.SMEM((2, 1, NB), jnp.int32),
            pltpu.VMEM((8 * COLS, R), f32),
            pltpu.VMEM((COLS, R), f32),
            pltpu.SemaphoreType.DMA((7 + COLS,)),
        ],
        20 << 20,
    )(meta, live_blocks, block_rows, block_cols, dosage_tiles, indiv_factors, variant_factors)
    far = far.astype(f16)
    got = [lax.ppermute(far[k - 1], "x", ring(k)) for k in (1, 2, 3)]
    low = lax.ppermute(upward, GEN, [(k, k + 1) for k in range(slabs - 1)])
    high = lax.ppermute(downward, GEN, [(k + 1, k) for k in range(slabs - 1)])
    total = own + got[0].astype(f32) + got[1].astype(f32) + got[2].astype(f32)
    near = jnp.concatenate([low, high], axis=0)
    nears = [near] + [lax.ppermute(near, "x", ring(k)) for k in (1, 2, 3)]
    position = slab * 4 + me
    meta_line = jnp.stack([me, position > 0, position < 4 * slabs - 1]).astype(jnp.int32)
    row = ((8, BS), f32, V)
    sent, table = call(
        variant_moments,
        [S] + [V] * 6,
        [((2, 2 * BS, R), f32, V), ((4 * slabs * 5, BS), f32, V)],
        [
            pltpu.VMEM((2, R, R), bf16),
            pltpu.VMEM((2, R, R), bf16),
            pltpu.VMEM((2 * BS + 16, R), f32),
        ],
    )(meta_line, total, variant_factors, *nears)
    sent = sent.astype(f16)
    pieces = jnp.stack([sent] + [lax.ppermute(sent, "x", ring(k)) for k in (1, 2, 3)])
    pieces = pieces.astype(f32)
    table = lax.all_to_all(
        table.reshape(4 * slabs * 5, 1, BS), ALL, 0, 0, tiled=True
    ).reshape(4 * slabs * 5, BS)

    whole = ((ROWS * BS, COLS * BS), bf16, V)
    variant_new, rounded, scales, dense = call(
        new_variants,
        [S, S, V, V, V, H],
        [((COLS * BS, R), f32, H), ((COLS * BS, R), bf16, V), row, whole],
        [pltpu.VMEM((COLS * BS, R), f32), big, pltpu.SemaphoreType.DMA((5,))],
    )(meta, ids, table, variant_factors, pieces, dosage_tiles)
    sums = ((ROWS, PAY_I, R), f32, V)
    scratch = [pltpu.VMEM((COLS, BS, R), f32), pltpu.VMEM((COLS, BS), f32)]
    (pay,) = call(sums_to_send, [S, S, V, V, V], [sums], scratch)(
        meta, mask, scales, dense, rounded
    )
    from_other = lax.ppermute(pay.astype(f16), "c", swap)
    (pay,) = call(
        sums_to_keep,
        [S, S, S, V, V, V],
        [sums],
        [pltpu.VMEM((ROWS * BS, COLS * BS), bf16), *scratch],
        8 << 20,
    )(meta, ids, mask, scales, rounded, dosage_tiles)
    of_chip = (pay + from_other.astype(f32)).astype(f16)
    arrived = lax.all_to_all(of_chip, CHIP, 0, 0)
    mine = jnp.sum(arrived.astype(f32), axis=0)
    theirs = lax.ppermute(mine, "c", swap)
    begin = lax.dynamic_slice_in_dim(indiv_factors, chip * BS, BS, 0)
    (sent,) = call(indiv_moments, [S, V, V, V, V], [((PAY_I, R), f32, V)])(
        meta, mine, theirs, begin, scales
    )
    sent = jnp.broadcast_to(sent.astype(f16)[None], (ROWS, PAY_I, R))
    here = lax.all_to_all(sent, CHIP, 0, 0)
    there = lax.ppermute(here, "c", swap)
    lines = here[:, BS, :BS].astype(f32)
    (moments,) = call(chip_moments, [V], [row])(lines)
    nexts = [lax.ppermute(moments, "x", ring(k)) for k in (1, 2, 3)]
    (shares,) = call(indiv_shares, [S] + [V] * 5, [((ROWS, BS), f32, V)])(
        meta, lines, moments, *nexts
    )
    change = (
        shares[:, 0].reshape(ROWS, 1, 1) * here[:, :BS].astype(f32)
        + shares[:, 1].reshape(ROWS, 1, 1) * there[:, :BS].astype(f32)
    )
    indiv_new = indiv_factors.reshape(ROWS, BS, R) + change
    return variant_new, indiv_new.reshape(ROWS * BS, R)


def solution(mesh):
    grid = np.asarray(mesh.devices).reshape(4, 4, 2, 4)
    inner = Mesh(grid, ALL)
    return jax.shard_map(
        on_device,
        mesh=inner,
        in_specs=(
            P("x", None),
            P(GEN, None),
            P(GEN, "x", None, None, None),
            P(GEN, "x", None),
            P(GEN, "x", None),
            P(GEN, "x"),
        ),
        out_specs=(P(GEN, None), P("x", None)),
        check_vma=False,
    )
```

```python
import jax
import jax.numpy as jnp
import numpy as np
from jax import lax
from jax.experimental import pallas as pl
from jax.experimental.pallas import tpu as pltpu
from jax.sharding import Mesh
from jax.sharding import PartitionSpec as P

BS = 128
R = 256
NB = 64
ROWS = 16
COLS = 8
smooth_weight = 32.0
ridge_weight = 1.0
f32, bf16, f16 = jnp.float32, jnp.bfloat16, jnp.float16
ALL = ("z", "y", "c", "x")
GEN = ("z", "y", "c")
CHIP = ("z", "y")
PAY_V = 2 * BS + 2 * BS + 8
PAY_I = BS + 8
VMEM_LIMIT = 16 * 1024 * 1024


def row_col():
    rows = lax.broadcasted_iota(jnp.int32, (BS, BS), 0)
    cols = lax.broadcasted_iota(jnp.int32, (BS, BS), 1)
    return rows, cols


def pack(gram):
    rows, cols = row_col()
    upper = gram[:BS, :BS]
    lower = gram[BS:, BS:]
    mixed = jnp.where(rows <= cols, upper, lower)
    diag = jnp.sum(jnp.where(rows == cols, lower, 0.0), axis=0, keepdims=True)
    return mixed, gram[:BS, BS:], diag


def unpack(mixed, cross, diag):
    rows, cols = row_col()
    turned = mixed.T
    upper = jnp.where(rows <= cols, mixed, turned)
    lower = jnp.where(rows > cols, mixed, jnp.where(rows < cols, turned, diag))
    top = jnp.concatenate([upper, cross], axis=1)
    bottom = jnp.concatenate([cross.T, lower], axis=1)
    return jnp.concatenate([top, bottom], axis=0)


def split(matrix):
    high = matrix.astype(bf16)
    return high, (matrix - high.astype(f32)).astype(bf16)


def times(values, high, low):
    rounded = values.astype(bf16)
    return jnp.dot(rounded, high, preferred_element_type=f32) + jnp.dot(
        rounded, low, preferred_element_type=f32
    )


def scatter(row_of, col_of, live, tiles, dense, mask=None, begin=0, end=NB):
    def four(step, carry):
        for k in range(4):
            s = jnp.minimum(step * 4 + k, live - 1)
            row, col = row_of(s), col_of(s)
            rows = pl.ds(pl.multiple_of(row * BS, BS), BS)
            cols = pl.ds(pl.multiple_of(col * BS, BS), BS)
            dense[rows, cols] = tiles[s]
            if mask is not None:
                mask[row * COLS + col] = 1.0
        return carry

    lax.fori_loop(begin // 4, jnp.minimum((live + 3) // 4, end // 4), four, 0)


def fill(ids, tiles, dense, **bounds):
    scatter(lambda s: ids[s], lambda s: ids[NB + s], ids[2 * NB], tiles, dense, **bounds)


def variant_sums(
    meta, live, rows_hbm, cols_hbm, tiles_hbm, factors_hbm, start_hbm,
    own, far, mask, upward, downward,
    tiles, factors, dense, turned, rounded, grams, diags, ids, sides, rims, sems,
):
    me = meta[0]
    plan = [
        pltpu.make_async_copy(rows_hbm.at[0], ids.at[0], sems.at[5]),
        pltpu.make_async_copy(cols_hbm.at[0], ids.at[1], sems.at[6]),
    ]
    for c in range(COLS):
        first = c * BS if c % 2 == 0 else (c + 1) * BS - 8
        plan.append(
            pltpu.make_async_copy(
                start_hbm.at[pl.ds(first, 8), :], sides.at[pl.ds(8 * c, 8), :], sems.at[7 + c]
            )
        )
    for load in plan:
        load.start()
    quarter = ROWS * BS // 4
    loads = [
        pltpu.make_async_copy(
            factors_hbm.at[pl.ds(k * quarter, quarter), :],
            factors.at[pl.ds(k * quarter, quarter), :],
            sems.at[k],
        )
        for k in range(4)
    ]
    load_tiles = pltpu.make_async_copy(tiles_hbm.at[0, 0], tiles, sems.at[4])
    for load in loads:
        load.start()
    load_tiles.start()
    dense[...] = jnp.zeros_like(dense)
    for cell in range(ROWS * COLS):
        mask[cell] = 0.0
    for r in range(ROWS):
        if r % 4 == 0:
            loads[r // 4].wait()
        block = factors[r * BS : (r + 1) * BS, :]
        rounded[r * BS : (r + 1) * BS, :] = block.astype(bf16)
        turned[:, r * BS : (r + 1) * BS] = block.T.astype(bf16)
        gram = jnp.dot(
            turned[:, r * BS : (r + 1) * BS],
            rounded[r * BS : (r + 1) * BS, :],
            preferred_element_type=f32,
        )
        mixed, cross, diag = pack(gram)
        grams[r, :, :BS] = mixed
        grams[r, :, BS:] = cross
        diags[r : r + 1, :] = diag
    for load in plan:
        load.wait()
    load_tiles.wait()
    scatter(lambda s: ids[0, 0, s], lambda s: ids[1, 0, s], live[0, 0], tiles, dense, mask)
    zero = jnp.zeros((8, R), f32)
    for k in range(4):
        part = lax.rem(me + k, 4)
        out = own if k == 0 else far.at[k - 1]
        cols = pl.ds(pl.multiple_of(part * 2 * BS, 2 * BS), 2 * BS)
        data = jnp.dot(turned[...], dense[:, cols], preferred_element_type=f32)
        out[2 * BS : 4 * BS, :] = data
        rims[pl.ds(2 * part, 1), :] = data[:, :BS].T[0:1, :]
        rims[pl.ds(2 * part + 1, 1), :] = data[:, BS:].T[BS - 1 : BS, :]
        out[4 * BS :, :] = zero
        for j in range(2):
            weights = [mask[r * COLS + part * 2 + j] for r in range(ROWS)]
            for piece in range(4):
                rows = slice(piece * 32, (piece + 1) * 32)
                total = weights[0] * grams[0, rows, :]
                for r in range(1, ROWS):
                    total += weights[r] * grams[r, rows, :]
                out[j * BS + piece * 32 : j * BS + (piece + 1) * 32, :] = total
            total = weights[0] * diags[0:1, :]
            for r in range(1, ROWS):
                total += weights[r] * diags[r : r + 1, :]
            out[4 * BS + j : 4 * BS + j + 1, :BS] = total
    edges = [sides[8 * c + (0 if c % 2 == 0 else 7) : 8 * c + (1 if c % 2 == 0 else 8), :] for c in range(COLS)]
    met = jnp.dot(
        jnp.concatenate(edges, axis=0).astype(bf16), turned[...], preferred_element_type=f32
    )
    lines = lax.broadcasted_iota(jnp.int32, (COLS, BS), 0)
    live_cells = []
    for r in range(ROWS):
        cells = jnp.zeros((COLS, BS), f32)
        for c in range(COLS):
            cells = jnp.where(lines == c, mask[r * COLS + c], cells)
        live_cells.append(cells)
    high, low = split(met * jnp.concatenate(live_cells, axis=1))
    rims[...] -= jnp.dot(high, rounded[...], preferred_element_type=f32) + jnp.dot(
        low, rounded[...], preferred_element_type=f32
    )
    for k in range(4):
        part = lax.rem(me + k, 4)
        out = own if k == 0 else far.at[k - 1]
        out[4 * BS + 2 : 4 * BS + 3, :] = rims[pl.ds(jnp.maximum(2 * part - 1, 0), 1), :]
        out[4 * BS + 3 : 4 * BS + 4, :] = rims[pl.ds(jnp.minimum(2 * part + 2, COLS - 1), 1), :]
    upward[...] = jnp.concatenate(
        [sides[8 * COLS - 2 : 8 * COLS, :], rims[COLS - 1 : COLS, :], jnp.zeros((5, R), f32)], axis=0
    )
    downward[...] = jnp.concatenate(
        [sides[0:2, :], rims[0:1, :], jnp.zeros((5, R), f32)], axis=0
    )


def band_of(values, before, after, ext):
    n = values.shape[0]
    ext[7:8, :] = before
    ext[8 : 8 + n, :] = values
    ext[8 + n : 9 + n, :] = after
    return 2.0 * values - ext[7 : 7 + n, :] - ext[9 : 9 + n, :]


def as_row(values):
    lanes = lax.broadcasted_iota(jnp.int32, (8, BS), 1)
    row = jnp.zeros((8, BS), f32)
    for k, value in enumerate(values):
        row = jnp.where(lanes == k, value, row)
    return row


def total_of(values):
    return jnp.sum(jnp.sum(values, axis=0, keepdims=True), axis=1, keepdims=True)


def largest(values):
    return jnp.max(jnp.max(jnp.abs(values), axis=0, keepdims=True), axis=1, keepdims=True)


def curve_of(rr, ra, aa, aaa):
    first = rr / ra
    rr_next = rr - 2.0 * first * ra + first * first * aa
    ratio = rr_next / rr
    curve = (
        (1.0 + ratio) * (1.0 + ratio) * ra
        - 2.0 * (1.0 + ratio) * first * aa
        + first * first * aaa
    )
    second = rr_next / curve
    return first + second * (1.0 + ratio), second * first, rr_next, curve


def variant_moments(
    meta, total, start, near0, near1, near2, near3, sent, table, g_high, g_low, ext
):
    part, has_before, has_after = meta[0], meta[1], meta[2]
    n = 2 * BS
    first_row = pl.multiple_of(part * n, n)
    mine = start[pl.ds(first_row, n), :]
    before8 = start[pl.ds(pl.multiple_of(jnp.maximum(first_row - 8, 0), 8), 8), :]
    after8 = start[pl.ds(pl.multiple_of(jnp.minimum(first_row + n, 4 * n - 8), 8), 8), :]
    at_low, at_high = part == 0, part == 3
    before = jnp.where(at_low, near0[1:2, :], before8[7:8, :])
    before2 = jnp.where(at_low, near0[0:1, :], before8[6:7, :])
    after = jnp.where(at_high, near0[8:9, :], after8[0:1, :])
    after2 = jnp.where(at_high, near0[9:10, :], after8[1:2, :])
    banded = band_of(mine, before, after, ext)
    data = total[2 * BS : 4 * BS, :].T
    pieces = []
    for k in range(2):
        gram = unpack(
            total[k * BS : (k + 1) * BS, :BS],
            total[k * BS : (k + 1) * BS, BS:],
            total[4 * BS + k : 4 * BS + k + 1, :BS],
        )
        g_high[k], g_low[k] = split(gram)
        rows = slice(k * BS, (k + 1) * BS)
        pieces.append(
            data[rows]
            - times(mine[rows], g_high[k], g_low[k])
            - ridge_weight * mine[rows]
            - smooth_weight * banded[rows]
        )
    value = jnp.concatenate(pieces, axis=0)
    low = near0[2:3, :] + near1[2:3, :] + near2[2:3, :] + near3[2:3, :]
    high = near0[10:11, :] + near1[10:11, :] + near2[10:11, :] + near3[10:11, :]
    low = jnp.where(at_low, low, total[4 * BS + 2 : 4 * BS + 3, :])
    high = jnp.where(at_high, high, total[4 * BS + 3 : 4 * BS + 4, :])
    low = low - ridge_weight * before - smooth_weight * (2.0 * before - before2 - mine[0:1, :])
    high = high - ridge_weight * after - smooth_weight * (2.0 * after - after2 - mine[n - 1 : n, :])
    zero = jnp.zeros((1, R), f32)
    low = jnp.where(has_before == 1, low, zero)
    high = jnp.where(has_after == 1, high, zero)

    def operator(values, banded):
        data = [times(values[k * BS : (k + 1) * BS], g_high[k], g_low[k]) for k in range(2)]
        return jnp.concatenate(data, axis=0) + ridge_weight * values + smooth_weight * banded

    first = operator(value, band_of(value, low, high, ext))
    second = operator(first, band_of(first, zero, zero, ext))
    rr, ra = total_of(value * value), total_of(value * first)
    aa, aaa = total_of(first * first), total_of(first * second)
    near, far, rr_next, curve = curve_of(rr, ra, aa, aaa)
    good = (ra > 0.0) & (rr_next > 1e-3 * rr) & (curve > 0.0) & (far > 0.0)
    on_start = jnp.where(good, 1.0, 0.0)
    near = jnp.where(good, near, 0.0)
    far = jnp.where(good, far, -1.0)
    guess = on_start * mine + near * value - far * first
    peak_value, peak_guess = largest(value), largest(guess)
    unit_value = jnp.maximum(peak_value, 1e-30) / 16384.0
    unit_guess = jnp.maximum(peak_guess, 1e-30) / 16384.0
    sent[0] = value / unit_value
    sent[1] = guess / unit_guess
    line = as_row(
        [rr, ra, aa, aaa, peak_value, largest(first), on_start, near, far, unit_value, unit_guess]
    )
    five = jnp.concatenate(
        [
            line[0:1, :],
            first[0:1, :BS],
            first[0:1, BS:],
            first[n - 1 : n, :BS],
            first[n - 1 : n, BS:],
        ],
        axis=0,
    )
    forty = jnp.concatenate([five] * 8, axis=0)
    for k in range(table.shape[0] // 40):
        table[40 * k : 40 * (k + 1), :] = forty


def new_variants(
    meta, ids, table, start, pieces, tiles_hbm, new, rounded, scales, dense, tiles, sem
):
    me, core, slab = meta[0], meta[1], meta[2]
    load = pltpu.make_async_copy(tiles_hbm.at[0, 0], tiles, sem)
    load.start()

    @pl.when(core == 1)
    def _():
        dense[...] = jnp.zeros_like(dense)

    parts = table.shape[0] // 5
    lines = table[pl.ds(0, parts, stride=5), :]
    sums = jnp.sum(lines, axis=0, keepdims=True)
    peaks = jnp.max(lines, axis=0, keepdims=True)
    across = sum(
        table[pl.ds(3 + half, parts - 1, stride=5), :] * table[pl.ds(6 + half, parts - 1, stride=5), :]
        for half in range(2)
    )
    rr, ra, aa, aaa = (sums[:, k : k + 1] for k in range(4))
    on_resid, on_applied, _, _ = curve_of(rr, ra, aa, aaa - 2.0 * smooth_weight * total_of(across))
    n = 2 * BS
    for k in range(4):
        owner = lax.rem(me - k + 4, 4)
        rows = pl.ds(pl.multiple_of(owner * n, n), n)
        line = table[pl.ds((slab * 4 + owner) * 5, 1), :]
        on_start, near, far, unit_value, unit_guess = (line[:, j : j + 1] for j in range(6, 11))
        share = on_applied / far
        value = (
            (1.0 - share * on_start) * start[rows, :]
            + ((on_resid - share * near) * unit_value) * pieces[k, 0]
            + (share * unit_guess) * pieces[k, 1]
        )
        new[rows, :] = value
        rounded[rows, :] = value.astype(bf16)
    top = jnp.abs(on_resid) * peaks[:, 4:5] + jnp.abs(on_applied) * peaks[:, 5:6] + 1.5
    scale_e = 30000.0 / (2.0 * 6.0 * COLS * BS * top)
    scale_h = 30000.0 / (2.0 * COLS * BS * top * top)
    scales[...] = as_row([scale_e, scale_h, 1.0 / scale_e, 1.0 / scale_h])
    load.wait()

    @pl.when(core == 1)
    def _():
        fill(ids, tiles, dense)


def tile_sums(scale, dense, rounded, pay):
    for r in range(ROWS):
        product = jnp.dot(
            dense[r * BS : (r + 1) * BS, :], rounded[...], preferred_element_type=f32
        )
        pay[r, :BS, :] = scale * product
        pay[r, BS:, :] = jnp.zeros((PAY_I - BS, R), f32)


def gram_sums(scale, mask, rounded, pay, grams, diags):
    for c in range(COLS):
        block = rounded[c * BS : (c + 1) * BS, :]
        turned = block.astype(f32).T.astype(bf16)
        gram = scale * jnp.dot(turned, block, preferred_element_type=f32)
        mixed, cross, diag = pack(gram)
        grams[c, :, :BS] = mixed
        grams[c, :, BS:] = cross
        diags[c : c + 1, :] = diag
    lines = lax.broadcasted_iota(jnp.int32, (PAY_I - BS, R), 0)
    for r in range(ROWS):
        weights = [mask[r * COLS + c] for c in range(COLS)]
        for piece in range(4):
            rows = slice(piece * 32, (piece + 1) * 32)
            total = weights[0] * grams[0, rows, :]
            for c in range(1, COLS):
                total += weights[c] * grams[c, rows, :]
            pay[r, rows, :] = total
        total = weights[0] * diags[0:1, :]
        for c in range(1, COLS):
            total += weights[c] * diags[c : c + 1, :]
        row = jnp.concatenate([total, jnp.zeros((1, BS), f32)], axis=1)
        pay[r, BS:, :] = jnp.where(lines == 0, row, 0.0)


def sums_to_send(meta, mask, scales, dense, rounded, new, pay, new_hbm, grams, diags, sem):
    keep = pltpu.make_async_copy(new, new_hbm, sem)
    keep.start()

    @pl.when(meta[1] == 1)
    def _():
        tile_sums(scales[0:1, 0:1], dense, rounded, pay)

    @pl.when(meta[1] == 0)
    def _():
        gram_sums(scales[0:1, 1:2], mask, rounded, pay, grams, diags)

    keep.wait()


def sums_to_keep(meta, ids, mask, scales, rounded, tiles_hbm, pay, dense, tiles, grams, diags, sems):
    @pl.when(meta[1] == 0)
    def _():
        quarter = NB // 4
        loads = [
            pltpu.make_async_copy(
                tiles_hbm.at[0, 0, pl.ds(k * quarter, quarter)],
                tiles.at[pl.ds(k * quarter, quarter)],
                sems.at[k],
            )
            for k in range(4)
        ]
        for load in loads:
            load.start()
        dense[...] = jnp.zeros_like(dense)
        for k, load in enumerate(loads):
            load.wait()
            fill(ids, tiles, dense, begin=k * quarter, end=(k + 1) * quarter)
        tile_sums(scales[0:1, 0:1], dense, rounded, pay)

    @pl.when(meta[1] == 1)
    def _():
        gram_sums(scales[0:1, 1:2], mask, rounded, pay, grams, diags)


def exponent_of(peak):
    return jnp.clip(jnp.ceil(jnp.log2(jnp.maximum(peak, 1e-30))), -100.0, 100.0)


def pieces_of(value):
    high = value.astype(bf16).astype(f32)
    rest = (value - high) * 256.0
    middle = rest.astype(bf16).astype(f32)
    return [high, middle, (rest - middle) * 256.0]


def indiv_moments(meta, mine, theirs, start, scales, sent):
    core = meta[1]
    own, far = mine[...], theirs[...]
    data = jnp.where(core == 0, own, far) * scales[0:1, 2:3]
    packed = jnp.where(core == 0, far, own) * scales[0:1, 3:4]
    high, low = split(unpack(packed[:BS, :BS], packed[:BS, BS:], packed[BS : BS + 1, :BS]))
    begin = start[...]
    value = data[:BS, :] - times(begin, high, low) - ridge_weight * begin
    first = times(value, high, low) + ridge_weight * value
    second = times(first, high, low) + ridge_weight * first
    powers = [exponent_of(largest(array)) for array in (value, first, second)]
    value, first, second = (
        array * jnp.exp2(-power) for array, power in zip((value, first, second), powers)
    )
    moments = [
        total_of(value * value),
        total_of(value * first),
        total_of(first * first),
        total_of(first * second),
    ]
    sent[:BS, :] = jnp.where(core == 0, value, first) * 16384.0
    row = as_row([part for moment in moments for part in pieces_of(moment)] + powers)
    sent[BS:, :] = jnp.concatenate([row, row], axis=1)


def chip_moments(lines, moments):
    def moment(k, power):
        parts = [lines[:, 3 * k + j : 3 * k + j + 1] for j in range(3)]
        value = parts[0] + parts[1] * (1.0 / 256.0) + parts[2] * (1.0 / 65536.0)
        return jnp.sum(value * power, axis=0, keepdims=True)

    one, two, three = (jnp.exp2(lines[:, j : j + 1]) for j in (12, 13, 14))
    moments[...] = as_row(
        [
            moment(0, one * one),
            moment(1, one * two),
            moment(2, two * two),
            moment(3, two * three),
        ]
    )


def indiv_shares(meta, lines, own, next1, next2, next3, shares):
    sums = own[0:1, :] + next1[0:1, :] + next2[0:1, :] + next3[0:1, :]
    on_resid, on_applied, _, _ = curve_of(*(sums[:, k : k + 1] for k in range(4)))
    of_resid = on_resid * jnp.exp2(lines[:, 12:13]) * (1.0 / 16384.0)
    of_applied = -on_applied * jnp.exp2(lines[:, 13:14]) * (1.0 / 16384.0)
    core = meta[1]
    lanes = lax.broadcasted_iota(jnp.int32, (ROWS, BS), 1)
    here = jnp.where(core == 0, of_resid, of_applied)
    there = jnp.where(core == 0, of_applied, of_resid)
    shares[...] = jnp.where(lanes == 0, here, there)


def ring(step):
    return [(k, (k + step) % 4) for k in range(4)]


def call(kernel, ins, outs, scratch=(), nbytes=1 << 20):
    def placed(shape, dtype, space):
        if space == pltpu.SMEM:
            return jax.ShapeDtypeStruct(shape, dtype)
        return space(shape, dtype)

    def run(*operands):
        operands = [
            pltpu.with_memory_space_constraint(x, pltpu.HBM) if space == pltpu.HBM else x
            for x, space in zip(operands, ins)
        ]
        return pl.pallas_call(
            kernel,
            out_shape=tuple(placed(*out) for out in outs),
            in_specs=[pl.BlockSpec(memory_space=space) for space in ins],
            out_specs=tuple(pl.BlockSpec(memory_space=out[2]) for out in outs),
            scratch_shapes=list(scratch),
            compiler_params=pltpu.CompilerParams(vmem_limit_bytes=VMEM_LIMIT),
            cost_estimate=pl.CostEstimate(flops=0, bytes_accessed=nbytes, transcendentals=0),
        )(*operands)

    return run


def on_device(indiv_factors, variant_factors, dosage_tiles, block_rows, block_cols, live_blocks):
    S, V, H = pltpu.SMEM, pltpu.VMEM, pltpu.HBM
    me = lax.axis_index("x")
    core = lax.axis_index("c")
    chip = lax.axis_index(CHIP)
    slab = lax.axis_index(GEN)
    slabs = 32
    swap = [(0, 1), (1, 0)]
    meta = jnp.stack([me, core, slab]).astype(jnp.int32)
    ids = jnp.concatenate([block_rows[0, 0], block_cols[0, 0], live_blocks[0]])

    big = pltpu.VMEM((NB, BS, BS), bf16)
    flags = ((ROWS * COLS,), f32, S)
    edge = ((8, R), f32, V)
    own, far, mask, upward, downward = call(
        variant_sums,
        [S, S, H, H, H, H, H],
        [((PAY_V, R), f32, V), ((3, PAY_V, R), f32, V), flags, edge, edge],
        [
            big,
            pltpu.VMEM((ROWS * BS, R), f32),
            pltpu.VMEM((ROWS * BS, COLS * BS), bf16),
            pltpu.VMEM((R, ROWS * BS), bf16),
            pltpu.VMEM((ROWS * BS, R), bf16),
            pltpu.VMEM((ROWS, BS, R), f32),
            pltpu.VMEM((ROWS, BS), f32),
            pltpu.SMEM((2, 1, NB), jnp.int32),
            pltpu.VMEM((8 * COLS, R), f32),
            pltpu.VMEM((COLS, R), f32),
            pltpu.SemaphoreType.DMA((7 + COLS,)),
        ],
        20 << 20,
    )(meta, live_blocks, block_rows, block_cols, dosage_tiles, indiv_factors, variant_factors)
    far = far.astype(f16)
    got = [lax.ppermute(far[k - 1], "x", ring(k)) for k in (1, 2, 3)]
    low = lax.ppermute(upward, GEN, [(k, k + 1) for k in range(slabs - 1)])
    high = lax.ppermute(downward, GEN, [(k + 1, k) for k in range(slabs - 1)])
    total = own + got[0].astype(f32) + got[1].astype(f32) + got[2].astype(f32)
    near = jnp.concatenate([low, high], axis=0)
    nears = [near] + [lax.ppermute(near, "x", ring(k)) for k in (1, 2, 3)]
    position = slab * 4 + me
    meta_line = jnp.stack([me, position > 0, position < 4 * slabs - 1]).astype(jnp.int32)
    row = ((8, BS), f32, V)
    sent, table = call(
        variant_moments,
        [S] + [V] * 6,
        [((2, 2 * BS, R), f32, V), ((4 * slabs * 5, BS), f32, V)],
        [
            pltpu.VMEM((2, R, R), bf16),
            pltpu.VMEM((2, R, R), bf16),
            pltpu.VMEM((2 * BS + 16, R), f32),
        ],
    )(meta_line, total, variant_factors, *nears)
    sent = sent.astype(f16)
    pieces = jnp.stack([sent] + [lax.ppermute(sent, "x", ring(k)) for k in (1, 2, 3)])
    pieces = pieces.astype(f32)
    table = lax.all_to_all(
        table.reshape(4 * slabs * 5, 1, BS), ALL, 0, 0, tiled=True
    ).reshape(4 * slabs * 5, BS)

    whole = ((ROWS * BS, COLS * BS), bf16, V)
    new, rounded, scales, dense = call(
        new_variants,
        [S, S, V, V, V, H],
        [((COLS * BS, R), f32, V), ((COLS * BS, R), bf16, V), row, whole],
        [big, pltpu.SemaphoreType.DMA],
    )(meta, ids, table, variant_factors, pieces, dosage_tiles)
    sums = ((ROWS, PAY_I, R), f32, V)
    scratch = [pltpu.VMEM((COLS, BS, R), f32), pltpu.VMEM((COLS, BS), f32)]
    pay, variant_new = call(
        sums_to_send,
        [S, S, V, V, V, V],
        [sums, ((COLS * BS, R), f32, H)],
        scratch + [pltpu.SemaphoreType.DMA],
    )(meta, mask, scales, dense, rounded, new)
    from_other = lax.ppermute(pay.astype(f16), "c", swap)
    (pay,) = call(
        sums_to_keep,
        [S, S, S, V, V, H],
        [sums],
        [
            pltpu.VMEM((ROWS * BS, COLS * BS), bf16),
            big,
            *scratch,
            pltpu.SemaphoreType.DMA((4,)),
        ],
        8 << 20,
    )(meta, ids, mask, scales, rounded, dosage_tiles)
    of_chip = (pay + from_other.astype(f32)).astype(f16)
    arrived = lax.all_to_all(of_chip, CHIP, 0, 0)
    mine = jnp.sum(arrived.astype(f32), axis=0)
    theirs = lax.ppermute(mine, "c", swap)
    begin = lax.dynamic_slice_in_dim(indiv_factors, chip * BS, BS, 0)
    (sent,) = call(indiv_moments, [S, V, V, V, V], [((PAY_I, R), f32, V)])(
        meta, mine, theirs, begin, scales
    )
    sent = jnp.broadcast_to(sent.astype(f16)[None], (ROWS, PAY_I, R))
    here = lax.all_to_all(sent, CHIP, 0, 0)
    there = lax.ppermute(here, "c", swap)
    lines = here[:, BS, :BS].astype(f32)
    (moments,) = call(chip_moments, [V], [row])(lines)
    nexts = [lax.ppermute(moments, "x", ring(k)) for k in (1, 2, 3)]
    (shares,) = call(indiv_shares, [S] + [V] * 5, [((ROWS, BS), f32, V)])(
        meta, lines, moments, *nexts
    )
    change = (
        shares[:, 0].reshape(ROWS, 1, 1) * here[:, :BS].astype(f32)
        + shares[:, 1].reshape(ROWS, 1, 1) * there[:, :BS].astype(f32)
    )
    indiv_new = indiv_factors.reshape(ROWS, BS, R) + change
    return variant_new, indiv_new.reshape(ROWS * BS, R)


def solution(mesh):
    grid = np.asarray(mesh.devices).reshape(4, 4, 2, 4)
    inner = Mesh(grid, ALL)
    return jax.shard_map(
        on_device,
        mesh=inner,
        in_specs=(
            P("x", None),
            P(GEN, None),
            P(GEN, "x", None, None, None),
            P(GEN, "x", None),
            P(GEN, "x", None),
            P(GEN, "x"),
        ),
        out_specs=(P(GEN, None), P("x", None)),
        check_vma=False,
    )
```

```python
import jax
import jax.numpy as jnp
import numpy as np
from jax import lax
from jax.experimental import pallas as pl
from jax.experimental.pallas import tpu as pltpu
from jax.sharding import Mesh
from jax.sharding import PartitionSpec as P

BS = 128
R = 256
NB = 64
ROWS = 16
COLS = 8
smooth_weight = 32.0
ridge_weight = 1.0
damping = 2.0**-12
resid_unit = 64.0
f32, bf16, f16 = jnp.float32, jnp.bfloat16, jnp.float16
ALL = ("z", "y", "c", "x")
GEN = ("z", "y", "c")
CHIP = ("z", "y")
PAY_V = 2 * BS + 2 * BS + 8
PAY_I = BS + 8
VMEM_LIMIT = 16 * 1024 * 1024


def row_col():
    rows = lax.broadcasted_iota(jnp.int32, (BS, BS), 0)
    cols = lax.broadcasted_iota(jnp.int32, (BS, BS), 1)
    return rows, cols


def pack(gram):
    rows, cols = row_col()
    upper = gram[:BS, :BS]
    lower = gram[BS:, BS:]
    mixed = jnp.where(rows <= cols, upper, lower)
    diag = jnp.sum(jnp.where(rows == cols, lower, 0.0), axis=0, keepdims=True)
    return mixed, gram[:BS, BS:], diag


def unpack(mixed, cross, diag):
    rows, cols = row_col()
    turned = mixed.T
    upper = jnp.where(rows <= cols, mixed, turned)
    lower = jnp.where(rows > cols, mixed, jnp.where(rows < cols, turned, diag))
    top = jnp.concatenate([upper, cross], axis=1)
    bottom = jnp.concatenate([cross.T, lower], axis=1)
    return jnp.concatenate([top, bottom], axis=0)


def split(matrix):
    high = matrix.astype(bf16)
    return high, (matrix - high.astype(f32)).astype(bf16)


def times(values, high, low):
    rounded = values.astype(bf16)
    return jnp.dot(rounded, high, preferred_element_type=f32) + jnp.dot(
        rounded, low, preferred_element_type=f32
    )


def scatter(row_of, col_of, live, tiles, dense, mask=None, begin=0, end=NB):
    def four(step, carry):
        for k in range(4):
            s = jnp.minimum(step * 4 + k, live - 1)
            row, col = row_of(s), col_of(s)
            rows = pl.ds(pl.multiple_of(row * BS, BS), BS)
            cols = pl.ds(pl.multiple_of(col * BS, BS), BS)
            dense[rows, cols] = tiles[s]
            if mask is not None:
                mask[row * COLS + col] = 1.0
        return carry

    lax.fori_loop(begin // 4, jnp.minimum((live + 3) // 4, end // 4), four, 0)


def fill(ids, tiles, dense, **bounds):
    scatter(lambda s: ids[s], lambda s: ids[NB + s], ids[2 * NB], tiles, dense, **bounds)


def variant_sums(
    meta, live, rows_hbm, cols_hbm, tiles_hbm, factors_hbm, start_hbm,
    own, far, mask, upward, downward,
    tiles, factors, dense, turned, rounded, grams, diags, ids, sides, rims, sems,
):
    me = meta[0]
    plan = [
        pltpu.make_async_copy(rows_hbm.at[0], ids.at[0], sems.at[5]),
        pltpu.make_async_copy(cols_hbm.at[0], ids.at[1], sems.at[6]),
    ]
    for c in range(COLS):
        first = c * BS if c % 2 == 0 else (c + 1) * BS - 8
        plan.append(
            pltpu.make_async_copy(
                start_hbm.at[pl.ds(first, 8), :], sides.at[pl.ds(8 * c, 8), :], sems.at[7 + c]
            )
        )
    for load in plan:
        load.start()
    quarter = ROWS * BS // 4
    loads = [
        pltpu.make_async_copy(
            factors_hbm.at[pl.ds(k * quarter, quarter), :],
            factors.at[pl.ds(k * quarter, quarter), :],
            sems.at[k],
        )
        for k in range(4)
    ]
    load_tiles = pltpu.make_async_copy(tiles_hbm.at[0, 0], tiles, sems.at[4])
    for load in loads:
        load.start()
    load_tiles.start()
    dense[...] = jnp.zeros_like(dense)
    for cell in range(ROWS * COLS):
        mask[cell] = 0.0
    for r in range(ROWS):
        if r % 4 == 0:
            loads[r // 4].wait()
        block = factors[r * BS : (r + 1) * BS, :]
        rounded[r * BS : (r + 1) * BS, :] = block.astype(bf16)
        turned[:, r * BS : (r + 1) * BS] = block.T.astype(bf16)
        gram = jnp.dot(
            turned[:, r * BS : (r + 1) * BS],
            rounded[r * BS : (r + 1) * BS, :],
            preferred_element_type=f32,
        )
        mixed, cross, diag = pack(gram)
        grams[r, :, :BS] = mixed
        grams[r, :, BS:] = cross
        diags[r : r + 1, :] = diag
    for load in plan:
        load.wait()
    load_tiles.wait()
    scatter(lambda s: ids[0, 0, s], lambda s: ids[1, 0, s], live[0, 0], tiles, dense, mask)
    zero = jnp.zeros((8, R), f32)
    for k in range(4):
        part = lax.rem(me + k, 4)
        out = own if k == 0 else far.at[k - 1]
        cols = pl.ds(pl.multiple_of(part * 2 * BS, 2 * BS), 2 * BS)
        data = jnp.dot(turned[...], dense[:, cols], preferred_element_type=f32)
        out[2 * BS : 4 * BS, :] = data
        rims[pl.ds(2 * part, 1), :] = data[:, :BS].T[0:1, :]
        rims[pl.ds(2 * part + 1, 1), :] = data[:, BS:].T[BS - 1 : BS, :]
        out[4 * BS :, :] = zero
        for j in range(2):
            weights = [mask[r * COLS + part * 2 + j] for r in range(ROWS)]
            for piece in range(4):
                rows = slice(piece * 32, (piece + 1) * 32)
                total = weights[0] * grams[0, rows, :]
                for r in range(1, ROWS):
                    total += weights[r] * grams[r, rows, :]
                out[j * BS + piece * 32 : j * BS + (piece + 1) * 32, :] = total
            total = weights[0] * diags[0:1, :]
            for r in range(1, ROWS):
                total += weights[r] * diags[r : r + 1, :]
            out[4 * BS + j : 4 * BS + j + 1, :BS] = total
    edges = [sides[8 * c + (0 if c % 2 == 0 else 7) : 8 * c + (1 if c % 2 == 0 else 8), :] for c in range(COLS)]
    met = jnp.dot(
        jnp.concatenate(edges, axis=0).astype(bf16), turned[...], preferred_element_type=f32
    )
    lines = lax.broadcasted_iota(jnp.int32, (COLS, BS), 0)
    live_cells = []
    for r in range(ROWS):
        cells = jnp.zeros((COLS, BS), f32)
        for c in range(COLS):
            cells = jnp.where(lines == c, mask[r * COLS + c], cells)
        live_cells.append(cells)
    high, low = split(met * jnp.concatenate(live_cells, axis=1))
    rims[...] -= jnp.dot(high, rounded[...], preferred_element_type=f32) + jnp.dot(
        low, rounded[...], preferred_element_type=f32
    )
    for k in range(4):
        part = lax.rem(me + k, 4)
        out = own if k == 0 else far.at[k - 1]
        before = rims[pl.ds(jnp.maximum(2 * part - 1, 0), 1), :]
        after = rims[pl.ds(jnp.minimum(2 * part + 2, COLS - 1), 1), :]
        out[4 * BS + 2 : 4 * BS + 3, :] = before * (1.0 / resid_unit)
        out[4 * BS + 3 : 4 * BS + 4, :] = after * (1.0 / resid_unit)
    upward[...] = jnp.concatenate(
        [sides[8 * COLS - 2 : 8 * COLS, :], rims[COLS - 1 : COLS, :], jnp.zeros((5, R), f32)], axis=0
    )
    downward[...] = jnp.concatenate(
        [sides[0:2, :], rims[0:1, :], jnp.zeros((5, R), f32)], axis=0
    )


def band_of(values, before, after, ext):
    n = values.shape[0]
    ext[7:8, :] = before
    ext[8 : 8 + n, :] = values
    ext[8 + n : 9 + n, :] = after
    return 2.0 * values - ext[7 : 7 + n, :] - ext[9 : 9 + n, :]


def as_row(values):
    lanes = lax.broadcasted_iota(jnp.int32, (8, BS), 1)
    row = jnp.zeros((8, BS), f32)
    for k, value in enumerate(values):
        row = jnp.where(lanes == k, value, row)
    return row


def total_of(values):
    return jnp.sum(jnp.sum(values, axis=0, keepdims=True), axis=1, keepdims=True)


def largest(values):
    return jnp.max(jnp.max(jnp.abs(values), axis=0, keepdims=True), axis=1, keepdims=True)


def curve_of(rr, ra, aa, aaa):
    first = rr / ra
    rr_next = rr - 2.0 * first * ra + first * first * aa
    ratio = rr_next / rr
    curve = (
        (1.0 + ratio) * (1.0 + ratio) * ra
        - 2.0 * (1.0 + ratio) * first * aa
        + first * first * aaa
    )
    second = jnp.where((rr_next > 2e-6 * rr) & (curve > 0.0), rr_next / curve, 0.0)
    return damping * (first + second * (1.0 + ratio)), damping * second * first, rr_next, curve


def variant_moments(
    meta, total, start, near0, near1, near2, near3, sent, table, g_high, g_low, ext
):
    part, has_before, has_after = meta[0], meta[1], meta[2]
    n = 2 * BS
    first_row = pl.multiple_of(part * n, n)
    mine = start[pl.ds(first_row, n), :]
    before8 = start[pl.ds(pl.multiple_of(jnp.maximum(first_row - 8, 0), 8), 8), :]
    after8 = start[pl.ds(pl.multiple_of(jnp.minimum(first_row + n, 4 * n - 8), 8), 8), :]
    at_low, at_high = part == 0, part == 3
    before = jnp.where(at_low, near0[1:2, :], before8[7:8, :])
    before2 = jnp.where(at_low, near0[0:1, :], before8[6:7, :])
    after = jnp.where(at_high, near0[8:9, :], after8[0:1, :])
    after2 = jnp.where(at_high, near0[9:10, :], after8[1:2, :])
    banded = band_of(mine, before, after, ext)
    data = total[2 * BS : 4 * BS, :].T
    pieces = []
    for k in range(2):
        gram = unpack(
            total[k * BS : (k + 1) * BS, :BS],
            total[k * BS : (k + 1) * BS, BS:],
            total[4 * BS + k : 4 * BS + k + 1, :BS],
        )
        g_high[k], g_low[k] = split(gram)
        rows = slice(k * BS, (k + 1) * BS)
        pieces.append(
            data[rows]
            - times(mine[rows], g_high[k], g_low[k])
            - ridge_weight * mine[rows]
            - smooth_weight * banded[rows]
        )
    value = jnp.concatenate(pieces, axis=0)
    low = near0[2:3, :] + near1[2:3, :] + near2[2:3, :] + near3[2:3, :]
    high = near0[10:11, :] + near1[10:11, :] + near2[10:11, :] + near3[10:11, :]
    low = jnp.where(at_low, low, resid_unit * total[4 * BS + 2 : 4 * BS + 3, :])
    high = jnp.where(at_high, high, resid_unit * total[4 * BS + 3 : 4 * BS + 4, :])
    low = low - ridge_weight * before - smooth_weight * (2.0 * before - before2 - mine[0:1, :])
    high = high - ridge_weight * after - smooth_weight * (2.0 * after - after2 - mine[n - 1 : n, :])
    zero = jnp.zeros((1, R), f32)
    low = jnp.where(has_before == 1, low, zero)
    high = jnp.where(has_after == 1, high, zero)

    def operator(values, banded):
        data = [times(values[k * BS : (k + 1) * BS], g_high[k], g_low[k]) for k in range(2)]
        return jnp.concatenate(data, axis=0) + ridge_weight * values + smooth_weight * banded

    first = damping * operator(value, band_of(value, low, high, ext))
    second = damping * operator(first, band_of(first, zero, zero, ext))
    rr, ra = total_of(value * value), total_of(value * first)
    aa, aaa = total_of(first * first), total_of(first * second)
    near, far, rr_next, curve = curve_of(rr, ra, aa, aaa)
    good = (ra > 0.0) & (rr_next > 1e-3 * rr) & (curve > 0.0) & (far > 0.0)
    on_start = jnp.where(good, 1.0, 0.0)
    near = jnp.where(good, near, 0.0)
    far = jnp.where(good, far, -1.0)
    guess = on_start * mine + near * value - far * first
    peak_value, peak_guess = largest(value), largest(guess)
    unit_value = jnp.maximum(peak_value, 1e-30) / 16384.0
    unit_guess = jnp.maximum(peak_guess, 1e-30) / 16384.0
    sent[0] = value / unit_value
    sent[1] = guess / unit_guess
    line = as_row(
        [rr, ra, aa, aaa, peak_value, largest(first), on_start, near, far, unit_value, unit_guess]
    )
    five = jnp.concatenate(
        [
            line[0:1, :],
            first[0:1, :BS],
            first[0:1, BS:],
            first[n - 1 : n, :BS],
            first[n - 1 : n, BS:],
        ],
        axis=0,
    )
    forty = jnp.concatenate([five] * 8, axis=0)
    for k in range(table.shape[0] // 40):
        table[40 * k : 40 * (k + 1), :] = forty


def new_variants(
    meta, ids, table, start, pieces, tiles_hbm, new, rounded, scales, dense, tiles, sem
):
    me, core, slab = meta[0], meta[1], meta[2]
    load = pltpu.make_async_copy(tiles_hbm.at[0, 0], tiles, sem)
    load.start()

    @pl.when(core == 1)
    def _():
        dense[...] = jnp.zeros_like(dense)

    parts = table.shape[0] // 5
    lines = table[pl.ds(0, parts, stride=5), :]
    sums = jnp.sum(lines, axis=0, keepdims=True)
    peaks = jnp.max(lines, axis=0, keepdims=True)
    across = sum(
        table[pl.ds(3 + half, parts - 1, stride=5), :] * table[pl.ds(6 + half, parts - 1, stride=5), :]
        for half in range(2)
    )
    rr, ra, aa, aaa = (sums[:, k : k + 1] for k in range(4))
    on_resid, on_applied, _, _ = curve_of(rr, ra, aa, aaa - 2.0 * damping * smooth_weight * total_of(across))
    n = 2 * BS
    for k in range(4):
        owner = lax.rem(me - k + 4, 4)
        rows = pl.ds(pl.multiple_of(owner * n, n), n)
        line = table[pl.ds((slab * 4 + owner) * 5, 1), :]
        on_start, near, far, unit_value, unit_guess = (line[:, j : j + 1] for j in range(6, 11))
        share = on_applied / far
        value = (
            (1.0 - share * on_start) * start[rows, :]
            + ((on_resid - share * near) * unit_value) * pieces[k, 0]
            + (share * unit_guess) * pieces[k, 1]
        )
        new[rows, :] = value
        rounded[rows, :] = value.astype(bf16)
    top = jnp.abs(on_resid) * peaks[:, 4:5] + jnp.abs(on_applied) * peaks[:, 5:6] + 1.5
    scale_e = 30000.0 / (2.0 * 6.0 * COLS * BS * top)
    scale_h = 30000.0 / (2.0 * COLS * BS * top * top)
    scales[...] = as_row([scale_e, scale_h, 1.0 / scale_e, 1.0 / scale_h])
    load.wait()

    @pl.when(core == 1)
    def _():
        fill(ids, tiles, dense)


def tile_sums(scale, dense, rounded, pay):
    for r in range(ROWS):
        product = jnp.dot(
            dense[r * BS : (r + 1) * BS, :], rounded[...], preferred_element_type=f32
        )
        pay[r, :BS, :] = scale * product
        pay[r, BS:, :] = jnp.zeros((PAY_I - BS, R), f32)


def gram_sums(scale, mask, rounded, pay, grams, diags):
    for c in range(COLS):
        block = rounded[c * BS : (c + 1) * BS, :]
        turned = block.astype(f32).T.astype(bf16)
        gram = scale * jnp.dot(turned, block, preferred_element_type=f32)
        mixed, cross, diag = pack(gram)
        grams[c, :, :BS] = mixed
        grams[c, :, BS:] = cross
        diags[c : c + 1, :] = diag
    lines = lax.broadcasted_iota(jnp.int32, (PAY_I - BS, R), 0)
    for r in range(ROWS):
        weights = [mask[r * COLS + c] for c in range(COLS)]
        for piece in range(4):
            rows = slice(piece * 32, (piece + 1) * 32)
            total = weights[0] * grams[0, rows, :]
            for c in range(1, COLS):
                total += weights[c] * grams[c, rows, :]
            pay[r, rows, :] = total
        total = weights[0] * diags[0:1, :]
        for c in range(1, COLS):
            total += weights[c] * diags[c : c + 1, :]
        row = jnp.concatenate([total, jnp.zeros((1, BS), f32)], axis=1)
        pay[r, BS:, :] = jnp.where(lines == 0, row, 0.0)


def sums_to_send(meta, mask, scales, dense, rounded, new, pay, new_hbm, grams, diags, sem):
    keep = pltpu.make_async_copy(new, new_hbm, sem)
    keep.start()

    @pl.when(meta[1] == 1)
    def _():
        tile_sums(scales[0:1, 0:1], dense, rounded, pay)

    @pl.when(meta[1] == 0)
    def _():
        gram_sums(scales[0:1, 1:2], mask, rounded, pay, grams, diags)

    keep.wait()


def sums_to_keep(meta, ids, mask, scales, rounded, tiles_hbm, pay, dense, tiles, grams, diags, sems):
    @pl.when(meta[1] == 0)
    def _():
        quarter = NB // 4
        loads = [
            pltpu.make_async_copy(
                tiles_hbm.at[0, 0, pl.ds(k * quarter, quarter)],
                tiles.at[pl.ds(k * quarter, quarter)],
                sems.at[k],
            )
            for k in range(4)
        ]
        for load in loads:
            load.start()
        dense[...] = jnp.zeros_like(dense)
        for k, load in enumerate(loads):
            load.wait()
            fill(ids, tiles, dense, begin=k * quarter, end=(k + 1) * quarter)
        tile_sums(scales[0:1, 0:1], dense, rounded, pay)

    @pl.when(meta[1] == 1)
    def _():
        gram_sums(scales[0:1, 1:2], mask, rounded, pay, grams, diags)


def exponent_of(peak):
    return jnp.clip(jnp.ceil(jnp.log2(jnp.maximum(peak, 1e-30))), -100.0, 100.0)


def pieces_of(value):
    high = value.astype(bf16).astype(f32)
    rest = (value - high) * 256.0
    middle = rest.astype(bf16).astype(f32)
    return [high, middle, (rest - middle) * 256.0]


def indiv_moments(meta, mine, theirs, start, scales, sent):
    core = meta[1]
    own, far = mine[...], theirs[...]
    data = jnp.where(core == 0, own, far) * scales[0:1, 2:3]
    packed = jnp.where(core == 0, far, own) * scales[0:1, 3:4]
    high, low = split(unpack(packed[:BS, :BS], packed[:BS, BS:], packed[BS : BS + 1, :BS]))
    begin = start[...]
    value = data[:BS, :] - times(begin, high, low) - ridge_weight * begin
    first = times(value, high, low) + ridge_weight * value
    second = times(first, high, low) + ridge_weight * first
    powers = [exponent_of(largest(array)) for array in (value, first, second)]
    value, first, second = (
        array * jnp.exp2(-power) for array, power in zip((value, first, second), powers)
    )
    moments = [
        total_of(value * value),
        total_of(value * first),
        total_of(first * first),
        total_of(first * second),
    ]
    sent[:BS, :] = jnp.where(core == 0, value, first) * 16384.0
    row = as_row([part for moment in moments for part in pieces_of(moment)] + powers)
    sent[BS:, :] = jnp.concatenate([row, row], axis=1)


def chip_moments(lines, moments):
    def moment(k, power):
        parts = [lines[:, 3 * k + j : 3 * k + j + 1] for j in range(3)]
        value = parts[0] + parts[1] * (1.0 / 256.0) + parts[2] * (1.0 / 65536.0)
        return jnp.sum(value * power, axis=0, keepdims=True)

    one, two, three = (jnp.exp2(lines[:, j : j + 1]) for j in (12, 13, 14))
    two, three = damping * two, damping * damping * three
    moments[...] = as_row(
        [
            moment(0, one * one),
            moment(1, one * two),
            moment(2, two * two),
            moment(3, two * three),
        ]
    )


def indiv_shares(meta, lines, own, next1, next2, next3, shares):
    sums = own[0:1, :] + next1[0:1, :] + next2[0:1, :] + next3[0:1, :]
    on_resid, on_applied, _, _ = curve_of(*(sums[:, k : k + 1] for k in range(4)))
    of_resid = on_resid * jnp.exp2(lines[:, 12:13]) * (1.0 / 16384.0)
    of_applied = -on_applied * jnp.exp2(lines[:, 13:14]) * (damping / 16384.0)
    core = meta[1]
    lanes = lax.broadcasted_iota(jnp.int32, (ROWS, BS), 1)
    here = jnp.where(core == 0, of_resid, of_applied)
    there = jnp.where(core == 0, of_applied, of_resid)
    shares[...] = jnp.where(lanes == 0, here, there)


def ring(step):
    return [(k, (k + step) % 4) for k in range(4)]


def call(kernel, ins, outs, scratch=(), nbytes=1 << 20):
    def placed(shape, dtype, space):
        if space == pltpu.SMEM:
            return jax.ShapeDtypeStruct(shape, dtype)
        return space(shape, dtype)

    def run(*operands):
        operands = [
            pltpu.with_memory_space_constraint(x, pltpu.HBM) if space == pltpu.HBM else x
            for x, space in zip(operands, ins)
        ]
        return pl.pallas_call(
            kernel,
            out_shape=tuple(placed(*out) for out in outs),
            in_specs=[pl.BlockSpec(memory_space=space) for space in ins],
            out_specs=tuple(pl.BlockSpec(memory_space=out[2]) for out in outs),
            scratch_shapes=list(scratch),
            compiler_params=pltpu.CompilerParams(vmem_limit_bytes=VMEM_LIMIT),
            cost_estimate=pl.CostEstimate(flops=0, bytes_accessed=nbytes, transcendentals=0),
        )(*operands)

    return run


def on_device(indiv_factors, variant_factors, dosage_tiles, block_rows, block_cols, live_blocks):
    S, V, H = pltpu.SMEM, pltpu.VMEM, pltpu.HBM
    me = lax.axis_index("x")
    core = lax.axis_index("c")
    chip = lax.axis_index(CHIP)
    slab = lax.axis_index(GEN)
    slabs = 32
    swap = [(0, 1), (1, 0)]
    meta = jnp.stack([me, core, slab]).astype(jnp.int32)
    ids = jnp.concatenate([block_rows[0, 0], block_cols[0, 0], live_blocks[0]])

    big = pltpu.VMEM((NB, BS, BS), bf16)
    flags = ((ROWS * COLS,), f32, S)
    edge = ((8, R), f32, V)
    own, far, mask, upward, downward = call(
        variant_sums,
        [S, S, H, H, H, H, H],
        [((PAY_V, R), f32, V), ((3, PAY_V, R), f32, V), flags, edge, edge],
        [
            big,
            pltpu.VMEM((ROWS * BS, R), f32),
            pltpu.VMEM((ROWS * BS, COLS * BS), bf16),
            pltpu.VMEM((R, ROWS * BS), bf16),
            pltpu.VMEM((ROWS * BS, R), bf16),
            pltpu.VMEM((ROWS, BS, R), f32),
            pltpu.VMEM((ROWS, BS), f32),
            pltpu.SMEM((2, 1, NB), jnp.int32),
            pltpu.VMEM((8 * COLS, R), f32),
            pltpu.VMEM((COLS, R), f32),
            pltpu.SemaphoreType.DMA((7 + COLS,)),
        ],
        20 << 20,
    )(meta, live_blocks, block_rows, block_cols, dosage_tiles, indiv_factors, variant_factors)
    far = far.astype(f16)
    got = [lax.ppermute(far[k - 1], "x", ring(k)) for k in (1, 2, 3)]
    low = lax.ppermute(upward, GEN, [(k, k + 1) for k in range(slabs - 1)])
    high = lax.ppermute(downward, GEN, [(k + 1, k) for k in range(slabs - 1)])
    total = own + got[0].astype(f32) + got[1].astype(f32) + got[2].astype(f32)
    near = jnp.concatenate([low, high], axis=0)
    nears = [near] + [lax.ppermute(near, "x", ring(k)) for k in (1, 2, 3)]
    position = slab * 4 + me
    meta_line = jnp.stack([me, position > 0, position < 4 * slabs - 1]).astype(jnp.int32)
    row = ((8, BS), f32, V)
    sent, table = call(
        variant_moments,
        [S] + [V] * 6,
        [((2, 2 * BS, R), f32, V), ((4 * slabs * 5, BS), f32, V)],
        [
            pltpu.VMEM((2, R, R), bf16),
            pltpu.VMEM((2, R, R), bf16),
            pltpu.VMEM((2 * BS + 16, R), f32),
        ],
    )(meta_line, total, variant_factors, *nears)
    sent = sent.astype(f16)
    pieces = jnp.stack([sent] + [lax.ppermute(sent, "x", ring(k)) for k in (1, 2, 3)])
    pieces = pieces.astype(f32)
    table = lax.all_to_all(
        table.reshape(4 * slabs * 5, 1, BS), ALL, 0, 0, tiled=True
    ).reshape(4 * slabs * 5, BS)

    whole = ((ROWS * BS, COLS * BS), bf16, V)
    new, rounded, scales, dense = call(
        new_variants,
        [S, S, V, V, V, H],
        [((COLS * BS, R), f32, V), ((COLS * BS, R), bf16, V), row, whole],
        [big, pltpu.SemaphoreType.DMA],
    )(meta, ids, table, variant_factors, pieces, dosage_tiles)
    sums = ((ROWS, PAY_I, R), f32, V)
    scratch = [pltpu.VMEM((COLS, BS, R), f32), pltpu.VMEM((COLS, BS), f32)]
    pay, variant_new = call(
        sums_to_send,
        [S, S, V, V, V, V],
        [sums, ((COLS * BS, R), f32, H)],
        scratch + [pltpu.SemaphoreType.DMA],
    )(meta, mask, scales, dense, rounded, new)
    from_other = lax.ppermute(pay.astype(f16), "c", swap)
    (pay,) = call(
        sums_to_keep,
        [S, S, S, V, V, H],
        [sums],
        [
            pltpu.VMEM((ROWS * BS, COLS * BS), bf16),
            big,
            *scratch,
            pltpu.SemaphoreType.DMA((4,)),
        ],
        8 << 20,
    )(meta, ids, mask, scales, rounded, dosage_tiles)
    of_chip = (pay + from_other.astype(f32)).astype(f16)
    arrived = lax.all_to_all(of_chip, CHIP, 0, 0)
    mine = jnp.sum(arrived.astype(f32), axis=0)
    theirs = lax.ppermute(mine, "c", swap)
    begin = lax.dynamic_slice_in_dim(indiv_factors, chip * BS, BS, 0)
    (sent,) = call(indiv_moments, [S, V, V, V, V], [((PAY_I, R), f32, V)])(
        meta, mine, theirs, begin, scales
    )
    sent = jnp.broadcast_to(sent.astype(f16)[None], (ROWS, PAY_I, R))
    here = lax.all_to_all(sent, CHIP, 0, 0)
    there = lax.ppermute(here, "c", swap)
    lines = here[:, BS, :BS].astype(f32)
    (moments,) = call(chip_moments, [V], [row])(lines)
    nexts = [lax.ppermute(moments, "x", ring(k)) for k in (1, 2, 3)]
    (shares,) = call(indiv_shares, [S] + [V] * 5, [((ROWS, BS), f32, V)])(
        meta, lines, moments, *nexts
    )
    change = (
        shares[:, 0].reshape(ROWS, 1, 1) * here[:, :BS].astype(f32)
        + shares[:, 1].reshape(ROWS, 1, 1) * there[:, :BS].astype(f32)
    )
    indiv_new = indiv_factors.reshape(ROWS, BS, R) + change
    return variant_new, indiv_new.reshape(ROWS * BS, R)


def solution(mesh):
    grid = np.asarray(mesh.devices).reshape(4, 4, 2, 4)
    inner = Mesh(grid, ALL)
    return jax.shard_map(
        on_device,
        mesh=inner,
        in_specs=(
            P("x", None),
            P(GEN, None),
            P(GEN, "x", None, None, None),
            P(GEN, "x", None),
            P(GEN, "x", None),
            P(GEN, "x"),
        ),
        out_specs=(P(GEN, None), P("x", None)),
        check_vma=False,
    )
```

```python
import jax
import jax.numpy as jnp
import numpy as np
from jax import lax
from jax.experimental import pallas as pl
from jax.experimental.pallas import tpu as pltpu
from jax.sharding import Mesh
from jax.sharding import PartitionSpec as P

BS = 128
R = 256
NB = 64
ROWS = 16
COLS = 8
smooth_weight = 32.0
ridge_weight = 1.0
damping = 2.0**-12
resid_unit = 64.0
f32, bf16, f16 = jnp.float32, jnp.bfloat16, jnp.float16
ALL = ("z", "y", "c", "x")
GEN = ("z", "y", "c")
CHIP = ("z", "y")
PAY_V = 2 * BS + 2 * BS + 8
PAY_I = BS + 8
PAY_H = 2 * BS + 8
VMEM_LIMIT = 16 * 1024 * 1024


def row_col():
    rows = lax.broadcasted_iota(jnp.int32, (BS, BS), 0)
    cols = lax.broadcasted_iota(jnp.int32, (BS, BS), 1)
    return rows, cols


def pack(gram):
    rows, cols = row_col()
    upper = gram[:BS, :BS]
    lower = gram[BS:, BS:]
    mixed = jnp.where(rows <= cols, upper, lower)
    diag = jnp.sum(jnp.where(rows == cols, lower, 0.0), axis=0, keepdims=True)
    return mixed, gram[:BS, BS:], diag


def unpack(mixed, cross, diag):
    rows, cols = row_col()
    turned = mixed.T
    upper = jnp.where(rows <= cols, mixed, turned)
    lower = jnp.where(rows > cols, mixed, jnp.where(rows < cols, turned, diag))
    top = jnp.concatenate([upper, cross], axis=1)
    bottom = jnp.concatenate([cross.T, lower], axis=1)
    return jnp.concatenate([top, bottom], axis=0)


def split(matrix):
    high = matrix.astype(bf16)
    return high, (matrix - high.astype(f32)).astype(bf16)


def times(values, high, low):
    rounded = values.astype(bf16)
    return jnp.dot(rounded, high, preferred_element_type=f32) + jnp.dot(
        rounded, low, preferred_element_type=f32
    )


def scatter(row_of, col_of, live, tiles, dense, mask=None, begin=0, end=NB):
    def four(step, carry):
        for k in range(4):
            s = jnp.minimum(step * 4 + k, live - 1)
            row, col = row_of(s), col_of(s)
            rows = pl.ds(pl.multiple_of(row * BS, BS), BS)
            cols = pl.ds(pl.multiple_of(col * BS, BS), BS)
            dense[rows, cols] = tiles[s]
            if mask is not None:
                mask[row * COLS + col] = 1.0
        return carry

    lax.fori_loop(begin // 4, jnp.minimum((live + 3) // 4, end // 4), four, 0)


def fill(ids, tiles, dense, **bounds):
    scatter(lambda s: ids[s], lambda s: ids[NB + s], ids[2 * NB], tiles, dense, **bounds)


def variant_sums(
    meta, live, rows_hbm, cols_hbm, tiles_hbm, factors_hbm, start_hbm,
    own, far, mask, upward, downward,
    tiles, factors, dense, turned, rounded, grams, diags, ids, sides, rims, sems,
):
    me = meta[0]
    plan = [
        pltpu.make_async_copy(rows_hbm.at[0], ids.at[0], sems.at[5]),
        pltpu.make_async_copy(cols_hbm.at[0], ids.at[1], sems.at[6]),
    ]
    for c in range(COLS):
        first = c * BS if c % 2 == 0 else (c + 1) * BS - 8
        plan.append(
            pltpu.make_async_copy(
                start_hbm.at[pl.ds(first, 8), :], sides.at[pl.ds(8 * c, 8), :], sems.at[7 + c]
            )
        )
    for load in plan:
        load.start()
    quarter = ROWS * BS // 4
    loads = [
        pltpu.make_async_copy(
            factors_hbm.at[pl.ds(k * quarter, quarter), :],
            factors.at[pl.ds(k * quarter, quarter), :],
            sems.at[k],
        )
        for k in range(4)
    ]
    load_tiles = pltpu.make_async_copy(tiles_hbm.at[0, 0], tiles, sems.at[4])
    for load in loads:
        load.start()
    load_tiles.start()
    dense[...] = jnp.zeros_like(dense)
    for cell in range(ROWS * COLS):
        mask[cell] = 0.0
    for r in range(ROWS):
        if r % 4 == 0:
            loads[r // 4].wait()
        block = factors[r * BS : (r + 1) * BS, :]
        rounded[r * BS : (r + 1) * BS, :] = block.astype(bf16)
        turned[:, r * BS : (r + 1) * BS] = block.T.astype(bf16)
        gram = jnp.dot(
            turned[:, r * BS : (r + 1) * BS],
            rounded[r * BS : (r + 1) * BS, :],
            preferred_element_type=f32,
        )
        mixed, cross, diag = pack(gram)
        grams[r, :, :BS] = mixed
        grams[r, :, BS:] = cross
        diags[r : r + 1, :] = diag
    for load in plan:
        load.wait()
    load_tiles.wait()
    scatter(lambda s: ids[0, 0, s], lambda s: ids[1, 0, s], live[0, 0], tiles, dense, mask)
    zero = jnp.zeros((8, R), f32)
    for k in range(4):
        part = lax.rem(me + k, 4)
        out = own if k == 0 else far.at[k - 1]
        cols = pl.ds(pl.multiple_of(part * 2 * BS, 2 * BS), 2 * BS)
        data = jnp.dot(turned[...], dense[:, cols], preferred_element_type=f32)
        out[2 * BS : 4 * BS, :] = data
        rims[pl.ds(2 * part, 1), :] = data[:, :BS].T[0:1, :]
        rims[pl.ds(2 * part + 1, 1), :] = data[:, BS:].T[BS - 1 : BS, :]
        out[4 * BS :, :] = zero
        for j in range(2):
            weights = [mask[r * COLS + part * 2 + j] for r in range(ROWS)]
            for piece in range(4):
                rows = slice(piece * 32, (piece + 1) * 32)
                total = weights[0] * grams[0, rows, :]
                for r in range(1, ROWS):
                    total += weights[r] * grams[r, rows, :]
                out[j * BS + piece * 32 : j * BS + (piece + 1) * 32, :] = total
            total = weights[0] * diags[0:1, :]
            for r in range(1, ROWS):
                total += weights[r] * diags[r : r + 1, :]
            out[4 * BS + j : 4 * BS + j + 1, :BS] = total
    edges = [sides[8 * c + (0 if c % 2 == 0 else 7) : 8 * c + (1 if c % 2 == 0 else 8), :] for c in range(COLS)]
    met = jnp.dot(
        jnp.concatenate(edges, axis=0).astype(bf16), turned[...], preferred_element_type=f32
    )
    lines = lax.broadcasted_iota(jnp.int32, (COLS, BS), 0)
    live_cells = []
    for r in range(ROWS):
        cells = jnp.zeros((COLS, BS), f32)
        for c in range(COLS):
            cells = jnp.where(lines == c, mask[r * COLS + c], cells)
        live_cells.append(cells)
    high, low = split(met * jnp.concatenate(live_cells, axis=1))
    rims[...] -= jnp.dot(high, rounded[...], preferred_element_type=f32) + jnp.dot(
        low, rounded[...], preferred_element_type=f32
    )
    for k in range(4):
        part = lax.rem(me + k, 4)
        out = own if k == 0 else far.at[k - 1]
        before = rims[pl.ds(jnp.maximum(2 * part - 1, 0), 1), :]
        after = rims[pl.ds(jnp.minimum(2 * part + 2, COLS - 1), 1), :]
        out[4 * BS + 2 : 4 * BS + 3, :] = before * (1.0 / resid_unit)
        out[4 * BS + 3 : 4 * BS + 4, :] = after * (1.0 / resid_unit)
    upward[...] = jnp.concatenate(
        [sides[8 * COLS - 2 : 8 * COLS, :], rims[COLS - 1 : COLS, :], jnp.zeros((5, R), f32)], axis=0
    )
    downward[...] = jnp.concatenate(
        [sides[0:2, :], rims[0:1, :], jnp.zeros((5, R), f32)], axis=0
    )


def band_of(values, before, after, ext):
    n = values.shape[0]
    ext[7:8, :] = before
    ext[8 : 8 + n, :] = values
    ext[8 + n : 9 + n, :] = after
    return 2.0 * values - ext[7 : 7 + n, :] - ext[9 : 9 + n, :]


def as_row(values):
    lanes = lax.broadcasted_iota(jnp.int32, (8, BS), 1)
    row = jnp.zeros((8, BS), f32)
    for k, value in enumerate(values):
        row = jnp.where(lanes == k, value, row)
    return row


def total_of(values):
    return jnp.sum(jnp.sum(values, axis=0, keepdims=True), axis=1, keepdims=True)


def largest(values):
    return jnp.max(jnp.max(jnp.abs(values), axis=0, keepdims=True), axis=1, keepdims=True)


def curve_of(rr, ra, aa, aaa):
    first = rr / ra
    rr_next = rr - 2.0 * first * ra + first * first * aa
    ratio = rr_next / rr
    curve = (
        (1.0 + ratio) * (1.0 + ratio) * ra
        - 2.0 * (1.0 + ratio) * first * aa
        + first * first * aaa
    )
    second = jnp.where((rr_next > 2e-6 * rr) & (curve > 0.0), rr_next / curve, 0.0)
    return damping * (first + second * (1.0 + ratio)), damping * second * first, rr_next, curve


def variant_moments(
    meta, total, start, near0, near1, near2, near3, sent, table, g_high, g_low, ext
):
    part, has_before, has_after = meta[0], meta[1], meta[2]
    n = 2 * BS
    first_row = pl.multiple_of(part * n, n)
    mine = start[pl.ds(first_row, n), :]
    before8 = start[pl.ds(pl.multiple_of(jnp.maximum(first_row - 8, 0), 8), 8), :]
    after8 = start[pl.ds(pl.multiple_of(jnp.minimum(first_row + n, 4 * n - 8), 8), 8), :]
    at_low, at_high = part == 0, part == 3
    before = jnp.where(at_low, near0[1:2, :], before8[7:8, :])
    before2 = jnp.where(at_low, near0[0:1, :], before8[6:7, :])
    after = jnp.where(at_high, near0[8:9, :], after8[0:1, :])
    after2 = jnp.where(at_high, near0[9:10, :], after8[1:2, :])
    banded = band_of(mine, before, after, ext)
    data = total[2 * BS : 4 * BS, :].T
    pieces = []
    for k in range(2):
        gram = unpack(
            total[k * BS : (k + 1) * BS, :BS],
            total[k * BS : (k + 1) * BS, BS:],
            total[4 * BS + k : 4 * BS + k + 1, :BS],
        )
        g_high[k], g_low[k] = split(gram)
        rows = slice(k * BS, (k + 1) * BS)
        pieces.append(
            data[rows]
            - times(mine[rows], g_high[k], g_low[k])
            - ridge_weight * mine[rows]
            - smooth_weight * banded[rows]
        )
    value = jnp.concatenate(pieces, axis=0)
    low = near0[2:3, :] + near1[2:3, :] + near2[2:3, :] + near3[2:3, :]
    high = near0[10:11, :] + near1[10:11, :] + near2[10:11, :] + near3[10:11, :]
    low = jnp.where(at_low, low, resid_unit * total[4 * BS + 2 : 4 * BS + 3, :])
    high = jnp.where(at_high, high, resid_unit * total[4 * BS + 3 : 4 * BS + 4, :])
    low = low - ridge_weight * before - smooth_weight * (2.0 * before - before2 - mine[0:1, :])
    high = high - ridge_weight * after - smooth_weight * (2.0 * after - after2 - mine[n - 1 : n, :])
    zero = jnp.zeros((1, R), f32)
    low = jnp.where(has_before == 1, low, zero)
    high = jnp.where(has_after == 1, high, zero)

    def operator(values, banded):
        data = [times(values[k * BS : (k + 1) * BS], g_high[k], g_low[k]) for k in range(2)]
        return jnp.concatenate(data, axis=0) + ridge_weight * values + smooth_weight * banded

    first = damping * operator(value, band_of(value, low, high, ext))
    second = damping * operator(first, band_of(first, zero, zero, ext))
    rr, ra = total_of(value * value), total_of(value * first)
    aa, aaa = total_of(first * first), total_of(first * second)
    near, far, rr_next, curve = curve_of(rr, ra, aa, aaa)
    good = (ra > 0.0) & (rr_next > 1e-3 * rr) & (curve > 0.0) & (far > 0.0)
    on_start = jnp.where(good, 1.0, 0.0)
    near = jnp.where(good, near, 0.0)
    far = jnp.where(good, far, -1.0)
    guess = on_start * mine + near * value - far * first
    peak_value, peak_guess = largest(value), largest(guess)
    unit_value = jnp.maximum(peak_value, 1e-30) / 16384.0
    unit_guess = jnp.maximum(peak_guess, 1e-30) / 16384.0
    sent[0] = value / unit_value
    sent[1] = guess / unit_guess
    line = as_row(
        [rr, ra, aa, aaa, peak_value, largest(first), on_start, near, far, unit_value, unit_guess]
    )
    five = jnp.concatenate(
        [
            line[0:1, :],
            first[0:1, :BS],
            first[0:1, BS:],
            first[n - 1 : n, :BS],
            first[n - 1 : n, BS:],
        ],
        axis=0,
    )
    forty = jnp.concatenate([five] * 8, axis=0)
    for k in range(table.shape[0] // 40):
        table[40 * k : 40 * (k + 1), :] = forty


def new_variants(
    meta, ids, table, start, pieces, tiles_hbm, new, rounded, scales, dense, tiles, sem
):
    me, core, slab = meta[0], meta[1], meta[2]
    load = pltpu.make_async_copy(tiles_hbm.at[0, 0], tiles, sem)
    load.start()

    @pl.when(core == 1)
    def _():
        dense[...] = jnp.zeros_like(dense)

    parts = table.shape[0] // 5
    lines = table[pl.ds(0, parts, stride=5), :]
    sums = jnp.sum(lines, axis=0, keepdims=True)
    peaks = jnp.max(lines, axis=0, keepdims=True)
    across = sum(
        table[pl.ds(3 + half, parts - 1, stride=5), :] * table[pl.ds(6 + half, parts - 1, stride=5), :]
        for half in range(2)
    )
    rr, ra, aa, aaa = (sums[:, k : k + 1] for k in range(4))
    on_resid, on_applied, _, _ = curve_of(rr, ra, aa, aaa - 2.0 * damping * smooth_weight * total_of(across))
    n = 2 * BS
    for k in range(4):
        owner = lax.rem(me - k + 4, 4)
        rows = pl.ds(pl.multiple_of(owner * n, n), n)
        line = table[pl.ds((slab * 4 + owner) * 5, 1), :]
        on_start, near, far, unit_value, unit_guess = (line[:, j : j + 1] for j in range(6, 11))
        share = on_applied / far
        value = (
            (1.0 - share * on_start) * start[rows, :]
            + ((on_resid - share * near) * unit_value) * pieces[k, 0]
            + (share * unit_guess) * pieces[k, 1]
        )
        new[rows, :] = value
        rounded[rows, :] = value.astype(bf16)
    top = jnp.abs(on_resid) * peaks[:, 4:5] + jnp.abs(on_applied) * peaks[:, 5:6] + 1.5
    scale_e = 30000.0 / (2.0 * 6.0 * COLS * BS * top)
    scale_h = 30000.0 / (2.0 * COLS * BS * top * top)
    scales[...] = as_row([scale_e, scale_h, 1.0 / scale_e, 1.0 / scale_h])
    load.wait()

    @pl.when(core == 1)
    def _():
        fill(ids, tiles, dense)


def tile_sums(scale, dense, rounded, pay):
    for r in range(ROWS):
        product = jnp.dot(
            dense[r * BS : (r + 1) * BS, :], rounded[...], preferred_element_type=f32
        )
        pay[r, :BS, :] = scale * product[:, :BS]
        pay[r, BS : 2 * BS, :] = scale * product[:, BS:]
        pay[r, 2 * BS :, :] = jnp.zeros((PAY_H - 2 * BS, BS), f32)


def gram_sums(scale, mask, rounded, pay, grams, diags):
    for c in range(COLS):
        block = rounded[c * BS : (c + 1) * BS, :]
        turned = block.astype(f32).T.astype(bf16)
        gram = scale * jnp.dot(turned, block, preferred_element_type=f32)
        mixed, cross, diag = pack(gram)
        grams[c, :, :BS] = mixed
        grams[c, :, BS:] = cross
        diags[c : c + 1, :] = diag
    lines = lax.broadcasted_iota(jnp.int32, (PAY_H - 2 * BS, BS), 0)
    for r in range(ROWS):
        weights = [mask[r * COLS + c] for c in range(COLS)]
        for piece in range(4):
            rows = slice(piece * 32, (piece + 1) * 32)
            total = weights[0] * grams[0, rows, :]
            for c in range(1, COLS):
                total += weights[c] * grams[c, rows, :]
            pay[r, rows, :] = total[:, :BS]
            pay[r, BS + piece * 32 : BS + (piece + 1) * 32, :] = total[:, BS:]
        total = weights[0] * diags[0:1, :]
        for c in range(1, COLS):
            total += weights[c] * diags[c : c + 1, :]
        pay[r, 2 * BS :, :] = jnp.where(lines == 0, total, 0.0)


def sums_to_send(meta, mask, scales, dense, rounded, new, pay, new_hbm, grams, diags, sem):
    keep = pltpu.make_async_copy(new, new_hbm, sem)
    keep.start()

    @pl.when(meta[1] == 1)
    def _():
        tile_sums(scales[0:1, 0:1], dense, rounded, pay)

    @pl.when(meta[1] == 0)
    def _():
        gram_sums(scales[0:1, 1:2], mask, rounded, pay, grams, diags)

    keep.wait()


def sums_to_keep(meta, ids, mask, scales, rounded, tiles_hbm, pay, dense, tiles, grams, diags, sems):
    @pl.when(meta[1] == 0)
    def _():
        quarter = NB // 4
        loads = [
            pltpu.make_async_copy(
                tiles_hbm.at[0, 0, pl.ds(k * quarter, quarter)],
                tiles.at[pl.ds(k * quarter, quarter)],
                sems.at[k],
            )
            for k in range(4)
        ]
        for load in loads:
            load.start()
        dense[...] = jnp.zeros_like(dense)
        for k, load in enumerate(loads):
            load.wait()
            fill(ids, tiles, dense, begin=k * quarter, end=(k + 1) * quarter)
        tile_sums(scales[0:1, 0:1], dense, rounded, pay)

    @pl.when(meta[1] == 1)
    def _():
        gram_sums(scales[0:1, 1:2], mask, rounded, pay, grams, diags)


def exponent_of(peak):
    return jnp.clip(jnp.ceil(jnp.log2(jnp.maximum(peak, 1e-30))), -100.0, 100.0)


def pieces_of(value):
    high = value.astype(bf16).astype(f32)
    rest = (value - high) * 256.0
    middle = rest.astype(bf16).astype(f32)
    return [high, middle, (rest - middle) * 256.0]


def indiv_moments(meta, mine, theirs, start, scales, sent):
    core = meta[1]
    own, far = mine[...], theirs[...]
    data = jnp.where(core == 0, own, far) * scales[0:1, 2:3]
    packed = jnp.where(core == 0, far, own) * scales[0:1, 3:4]
    high, low = split(unpack(packed[:BS], packed[BS : 2 * BS], packed[2 * BS : 2 * BS + 1]))
    begin = start[...]
    data = jnp.concatenate([data[:BS], data[BS : 2 * BS]], axis=1)
    value = data - times(begin, high, low) - ridge_weight * begin
    first = times(value, high, low) + ridge_weight * value
    second = times(first, high, low) + ridge_weight * first
    powers = [exponent_of(largest(array)) for array in (value, first, second)]
    value, first, second = (
        array * jnp.exp2(-power) for array, power in zip((value, first, second), powers)
    )
    moments = [
        total_of(value * value),
        total_of(value * first),
        total_of(first * first),
        total_of(first * second),
    ]
    sent[:BS, :] = jnp.where(core == 0, value, first) * 16384.0
    row = as_row([part for moment in moments for part in pieces_of(moment)] + powers)
    sent[BS:, :] = jnp.concatenate([row, row], axis=1)


def chip_moments(lines, moments):
    def moment(k, power):
        parts = [lines[:, 3 * k + j : 3 * k + j + 1] for j in range(3)]
        value = parts[0] + parts[1] * (1.0 / 256.0) + parts[2] * (1.0 / 65536.0)
        return jnp.sum(value * power, axis=0, keepdims=True)

    one, two, three = (jnp.exp2(lines[:, j : j + 1]) for j in (12, 13, 14))
    two, three = damping * two, damping * damping * three
    moments[...] = as_row(
        [
            moment(0, one * one),
            moment(1, one * two),
            moment(2, two * two),
            moment(3, two * three),
        ]
    )


def indiv_shares(meta, lines, own, next1, next2, next3, shares):
    sums = own[0:1, :] + next1[0:1, :] + next2[0:1, :] + next3[0:1, :]
    on_resid, on_applied, _, _ = curve_of(*(sums[:, k : k + 1] for k in range(4)))
    of_resid = on_resid * jnp.exp2(lines[:, 12:13]) * (1.0 / 16384.0)
    of_applied = -on_applied * jnp.exp2(lines[:, 13:14]) * (damping / 16384.0)
    core = meta[1]
    lanes = lax.broadcasted_iota(jnp.int32, (ROWS, BS), 1)
    here = jnp.where(core == 0, of_resid, of_applied)
    there = jnp.where(core == 0, of_applied, of_resid)
    shares[...] = jnp.where(lanes == 0, here, there)


def ring(step):
    return [(k, (k + step) % 4) for k in range(4)]


def call(kernel, ins, outs, scratch=(), nbytes=1 << 20):
    def placed(shape, dtype, space):
        if space == pltpu.SMEM:
            return jax.ShapeDtypeStruct(shape, dtype)
        return space(shape, dtype)

    def run(*operands):
        operands = [
            pltpu.with_memory_space_constraint(x, pltpu.HBM) if space == pltpu.HBM else x
            for x, space in zip(operands, ins)
        ]
        return pl.pallas_call(
            kernel,
            out_shape=tuple(placed(*out) for out in outs),
            in_specs=[pl.BlockSpec(memory_space=space) for space in ins],
            out_specs=tuple(pl.BlockSpec(memory_space=out[2]) for out in outs),
            scratch_shapes=list(scratch),
            compiler_params=pltpu.CompilerParams(vmem_limit_bytes=VMEM_LIMIT),
            cost_estimate=pl.CostEstimate(flops=0, bytes_accessed=nbytes, transcendentals=0),
        )(*operands)

    return run


def on_device(indiv_factors, variant_factors, dosage_tiles, block_rows, block_cols, live_blocks):
    S, V, H = pltpu.SMEM, pltpu.VMEM, pltpu.HBM
    me = lax.axis_index("x")
    core = lax.axis_index("c")
    chip = lax.axis_index(CHIP)
    slab = lax.axis_index(GEN)
    slabs = 32
    swap = [(0, 1), (1, 0)]
    meta = jnp.stack([me, core, slab]).astype(jnp.int32)
    ids = jnp.concatenate([block_rows[0, 0], block_cols[0, 0], live_blocks[0]])

    big = pltpu.VMEM((NB, BS, BS), bf16)
    flags = ((ROWS * COLS,), f32, S)
    edge = ((8, R), f32, V)
    own, far, mask, upward, downward = call(
        variant_sums,
        [S, S, H, H, H, H, H],
        [((PAY_V, R), f32, V), ((3, PAY_V, R), f32, V), flags, edge, edge],
        [
            big,
            pltpu.VMEM((ROWS * BS, R), f32),
            pltpu.VMEM((ROWS * BS, COLS * BS), bf16),
            pltpu.VMEM((R, ROWS * BS), bf16),
            pltpu.VMEM((ROWS * BS, R), bf16),
            pltpu.VMEM((ROWS, BS, R), f32),
            pltpu.VMEM((ROWS, BS), f32),
            pltpu.SMEM((2, 1, NB), jnp.int32),
            pltpu.VMEM((8 * COLS, R), f32),
            pltpu.VMEM((COLS, R), f32),
            pltpu.SemaphoreType.DMA((7 + COLS,)),
        ],
        20 << 20,
    )(meta, live_blocks, block_rows, block_cols, dosage_tiles, indiv_factors, variant_factors)
    far = far.astype(f16)
    got = [lax.ppermute(far[k - 1], "x", ring(k)) for k in (1, 2, 3)]
    low = lax.ppermute(upward, GEN, [(k, k + 1) for k in range(slabs - 1)])
    high = lax.ppermute(downward, GEN, [(k + 1, k) for k in range(slabs - 1)])
    total = own + got[0].astype(f32) + got[1].astype(f32) + got[2].astype(f32)
    near = jnp.concatenate([low, high], axis=0)
    nears = [near] + [lax.ppermute(near, "x", ring(k)) for k in (1, 2, 3)]
    position = slab * 4 + me
    meta_line = jnp.stack([me, position > 0, position < 4 * slabs - 1]).astype(jnp.int32)
    row = ((8, BS), f32, V)
    sent, table = call(
        variant_moments,
        [S] + [V] * 6,
        [((2, 2 * BS, R), f32, V), ((4 * slabs * 5, BS), f32, V)],
        [
            pltpu.VMEM((2, R, R), bf16),
            pltpu.VMEM((2, R, R), bf16),
            pltpu.VMEM((2 * BS + 16, R), f32),
        ],
    )(meta_line, total, variant_factors, *nears)
    sent = sent.astype(f16)
    pieces = jnp.stack([sent] + [lax.ppermute(sent, "x", ring(k)) for k in (1, 2, 3)])
    pieces = pieces.astype(f32)
    table = lax.all_to_all(
        table.reshape(4 * slabs * 5, 1, BS), ALL, 0, 0, tiled=True
    ).reshape(4 * slabs * 5, BS)

    whole = ((ROWS * BS, COLS * BS), bf16, V)
    new, rounded, scales, dense = call(
        new_variants,
        [S, S, V, V, V, H],
        [((COLS * BS, R), f32, V), ((COLS * BS, R), bf16, V), row, whole],
        [big, pltpu.SemaphoreType.DMA],
    )(meta, ids, table, variant_factors, pieces, dosage_tiles)
    sums = ((ROWS, PAY_H, BS), f32, V)
    scratch = [pltpu.VMEM((COLS, BS, R), f32), pltpu.VMEM((COLS, BS), f32)]
    pay, variant_new = call(
        sums_to_send,
        [S, S, V, V, V, V],
        [sums, ((COLS * BS, R), f32, H)],
        scratch + [pltpu.SemaphoreType.DMA],
    )(meta, mask, scales, dense, rounded, new)
    from_other = lax.ppermute(pay.astype(f16), "c", swap)
    (pay,) = call(
        sums_to_keep,
        [S, S, S, V, V, H],
        [sums],
        [
            pltpu.VMEM((ROWS * BS, COLS * BS), bf16),
            big,
            *scratch,
            pltpu.SemaphoreType.DMA((4,)),
        ],
        8 << 20,
    )(meta, ids, mask, scales, rounded, dosage_tiles)
    of_chip = (pay + from_other.astype(f32)).astype(f16)
    arrived = lax.all_to_all(of_chip, CHIP, 0, 0)
    mine = jnp.sum(arrived.astype(f32), axis=0)
    theirs = lax.ppermute(mine, "c", swap)
    begin = lax.dynamic_slice_in_dim(indiv_factors, chip * BS, BS, 0)
    (sent,) = call(indiv_moments, [S, V, V, V, V], [((PAY_I, R), f32, V)])(
        meta, mine, theirs, begin, scales
    )
    sent = jnp.broadcast_to(sent.astype(f16)[None], (ROWS, PAY_I, R))
    here = lax.all_to_all(sent, CHIP, 0, 0)
    there = lax.ppermute(here, "c", swap)
    lines = here[:, BS, :BS].astype(f32)
    (moments,) = call(chip_moments, [V], [row])(lines)
    nexts = [lax.ppermute(moments, "x", ring(k)) for k in (1, 2, 3)]
    (shares,) = call(indiv_shares, [S] + [V] * 5, [((ROWS, BS), f32, V)])(
        meta, lines, moments, *nexts
    )
    change = (
        shares[:, 0].reshape(ROWS, 1, 1) * here[:, :BS].astype(f32)
        + shares[:, 1].reshape(ROWS, 1, 1) * there[:, :BS].astype(f32)
    )
    indiv_new = indiv_factors.reshape(ROWS, BS, R) + change
    return variant_new, indiv_new.reshape(ROWS * BS, R)


def solution(mesh):
    grid = np.asarray(mesh.devices).reshape(4, 4, 2, 4)
    inner = Mesh(grid, ALL)
    return jax.shard_map(
        on_device,
        mesh=inner,
        in_specs=(
            P("x", None),
            P(GEN, None),
            P(GEN, "x", None, None, None),
            P(GEN, "x", None),
            P(GEN, "x", None),
            P(GEN, "x"),
        ),
        out_specs=(P(GEN, None), P("x", None)),
        check_vma=False,
    )
```

```python
import jax
import jax.numpy as jnp
import numpy as np
from jax import lax
from jax.experimental import pallas as pl
from jax.experimental.pallas import tpu as pltpu
from jax.sharding import Mesh
from jax.sharding import PartitionSpec as P

BS = 128
R = 256
NB = 64
ROWS = 16
COLS = 8
smooth_weight = 32.0
ridge_weight = 1.0
damping = 2.0**-12
resid_unit = 64.0
f32, bf16, f16 = jnp.float32, jnp.bfloat16, jnp.float16
ALL = ("z", "y", "c", "x")
GEN = ("z", "y", "c")
CHIP = ("z", "y")
PAY_V = 2 * BS + 2 * BS + 8
PAY_I = BS + 8
PAY_H = 2 * BS + 8
VMEM_LIMIT = 16 * 1024 * 1024


def row_col():
    rows = lax.broadcasted_iota(jnp.int32, (BS, BS), 0)
    cols = lax.broadcasted_iota(jnp.int32, (BS, BS), 1)
    return rows, cols


def pack(gram):
    rows, cols = row_col()
    upper = gram[:BS, :BS]
    lower = gram[BS:, BS:]
    mixed = jnp.where(rows <= cols, upper, lower)
    diag = jnp.sum(jnp.where(rows == cols, lower, 0.0), axis=0, keepdims=True)
    return mixed, gram[:BS, BS:], diag


def unpack(mixed, cross, diag):
    rows, cols = row_col()
    turned = mixed.T
    upper = jnp.where(rows <= cols, mixed, turned)
    lower = jnp.where(rows > cols, mixed, jnp.where(rows < cols, turned, diag))
    top = jnp.concatenate([upper, cross], axis=1)
    bottom = jnp.concatenate([cross.T, lower], axis=1)
    return jnp.concatenate([top, bottom], axis=0)


def split(matrix):
    high = matrix.astype(bf16)
    return high, (matrix - high.astype(f32)).astype(bf16)


def times(values, high, low):
    rounded = values.astype(bf16)
    return jnp.dot(rounded, high, preferred_element_type=f32) + jnp.dot(
        rounded, low, preferred_element_type=f32
    )


def scatter(row_of, col_of, live, tiles, dense, mask=None, begin=0, end=NB):
    def four(step, carry):
        for k in range(4):
            s = jnp.minimum(step * 4 + k, live - 1)
            row, col = row_of(s), col_of(s)
            rows = pl.ds(pl.multiple_of(row * BS, BS), BS)
            cols = pl.ds(pl.multiple_of(col * BS, BS), BS)
            dense[rows, cols] = tiles[s]
            if mask is not None:
                mask[row * COLS + col] = 1.0
        return carry

    lax.fori_loop(begin // 4, jnp.minimum((live + 3) // 4, end // 4), four, 0)


def fill(ids, tiles, dense, **bounds):
    scatter(lambda s: ids[s], lambda s: ids[NB + s], ids[2 * NB], tiles, dense, **bounds)


def variant_sums(
    meta, live, rows_hbm, cols_hbm, tiles_hbm, factors_hbm, start_hbm,
    own, far, mask, upward, downward,
    tiles, factors, dense, turned, rounded, grams, diags, ids, sides, rims, sems,
):
    me = meta[0]
    plan = [
        pltpu.make_async_copy(rows_hbm.at[0], ids.at[0], sems.at[5]),
        pltpu.make_async_copy(cols_hbm.at[0], ids.at[1], sems.at[6]),
    ]
    for c in range(COLS):
        first = c * BS if c % 2 == 0 else (c + 1) * BS - 8
        plan.append(
            pltpu.make_async_copy(
                start_hbm.at[pl.ds(first, 8), :], sides.at[pl.ds(8 * c, 8), :], sems.at[7 + c]
            )
        )
    for load in plan:
        load.start()
    quarter = ROWS * BS // 4
    loads = [
        pltpu.make_async_copy(
            factors_hbm.at[pl.ds(k * quarter, quarter), :],
            factors.at[pl.ds(k * quarter, quarter), :],
            sems.at[k],
        )
        for k in range(4)
    ]
    load_tiles = pltpu.make_async_copy(tiles_hbm.at[0, 0], tiles, sems.at[4])
    for load in loads:
        load.start()
    load_tiles.start()
    dense[...] = jnp.zeros_like(dense)
    for cell in range(ROWS * COLS):
        mask[cell] = 0.0
    for r in range(ROWS):
        if r % 4 == 0:
            loads[r // 4].wait()
        block = factors[r * BS : (r + 1) * BS, :]
        rounded[r * BS : (r + 1) * BS, :] = block.astype(bf16)
        turned[:, r * BS : (r + 1) * BS] = block.T.astype(bf16)
        gram = jnp.dot(
            turned[:, r * BS : (r + 1) * BS],
            rounded[r * BS : (r + 1) * BS, :],
            preferred_element_type=f32,
        )
        mixed, cross, diag = pack(gram)
        grams[r, :, :BS] = mixed
        grams[r, :, BS:] = cross
        diags[r : r + 1, :] = diag
    for load in plan:
        load.wait()
    load_tiles.wait()
    scatter(lambda s: ids[0, 0, s], lambda s: ids[1, 0, s], live[0, 0], tiles, dense, mask)
    zero = jnp.zeros((8, R), f32)
    for k in range(4):
        part = lax.rem(me + k, 4)
        out = own if k == 0 else far.at[k - 1]
        cols = pl.ds(pl.multiple_of(part * 2 * BS, 2 * BS), 2 * BS)
        data = jnp.dot(turned[...], dense[:, cols], preferred_element_type=f32)
        out[2 * BS : 4 * BS, :] = data
        rims[pl.ds(2 * part, 1), :] = data[:, :BS].T[0:1, :]
        rims[pl.ds(2 * part + 1, 1), :] = data[:, BS:].T[BS - 1 : BS, :]
        out[4 * BS :, :] = zero
        for j in range(2):
            weights = [mask[r * COLS + part * 2 + j] for r in range(ROWS)]
            for piece in range(4):
                rows = slice(piece * 32, (piece + 1) * 32)
                total = weights[0] * grams[0, rows, :]
                for r in range(1, ROWS):
                    total += weights[r] * grams[r, rows, :]
                out[j * BS + piece * 32 : j * BS + (piece + 1) * 32, :] = total
            total = weights[0] * diags[0:1, :]
            for r in range(1, ROWS):
                total += weights[r] * diags[r : r + 1, :]
            out[4 * BS + j : 4 * BS + j + 1, :BS] = total
    edges = [sides[8 * c + (0 if c % 2 == 0 else 7) : 8 * c + (1 if c % 2 == 0 else 8), :] for c in range(COLS)]
    met = jnp.dot(
        jnp.concatenate(edges, axis=0).astype(bf16), turned[...], preferred_element_type=f32
    )
    lines = lax.broadcasted_iota(jnp.int32, (COLS, BS), 0)
    live_cells = []
    for r in range(ROWS):
        cells = jnp.zeros((COLS, BS), f32)
        for c in range(COLS):
            cells = jnp.where(lines == c, mask[r * COLS + c], cells)
        live_cells.append(cells)
    high, low = split(met * jnp.concatenate(live_cells, axis=1))
    rims[...] -= jnp.dot(high, rounded[...], preferred_element_type=f32) + jnp.dot(
        low, rounded[...], preferred_element_type=f32
    )
    for k in range(4):
        part = lax.rem(me + k, 4)
        out = own if k == 0 else far.at[k - 1]
        before = rims[pl.ds(jnp.maximum(2 * part - 1, 0), 1), :]
        after = rims[pl.ds(jnp.minimum(2 * part + 2, COLS - 1), 1), :]
        out[4 * BS + 2 : 4 * BS + 3, :] = before * (1.0 / resid_unit)
        out[4 * BS + 3 : 4 * BS + 4, :] = after * (1.0 / resid_unit)
    upward[...] = jnp.concatenate(
        [sides[8 * COLS - 2 : 8 * COLS, :], rims[COLS - 1 : COLS, :], jnp.zeros((5, R), f32)], axis=0
    )
    downward[...] = jnp.concatenate(
        [sides[0:2, :], rims[0:1, :], jnp.zeros((5, R), f32)], axis=0
    )


def band_of(values, before, after, ext):
    n = values.shape[0]
    ext[7:8, :] = before
    ext[8 : 8 + n, :] = values
    ext[8 + n : 9 + n, :] = after
    return 2.0 * values - ext[7 : 7 + n, :] - ext[9 : 9 + n, :]


def as_row(values):
    lanes = lax.broadcasted_iota(jnp.int32, (8, BS), 1)
    row = jnp.zeros((8, BS), f32)
    for k, value in enumerate(values):
        row = jnp.where(lanes == k, value, row)
    return row


def total_of(values):
    return jnp.sum(jnp.sum(values, axis=0, keepdims=True), axis=1, keepdims=True)


def largest(values):
    return jnp.max(jnp.max(jnp.abs(values), axis=0, keepdims=True), axis=1, keepdims=True)


def curve_of(rr, ra, aa, aaa):
    first = rr / ra
    rr_next = rr - 2.0 * first * ra + first * first * aa
    ratio = rr_next / rr
    curve = (
        (1.0 + ratio) * (1.0 + ratio) * ra
        - 2.0 * (1.0 + ratio) * first * aa
        + first * first * aaa
    )
    second = jnp.where((rr_next > 2e-6 * rr) & (curve > 0.0), rr_next / curve, 0.0)
    return damping * (first + second * (1.0 + ratio)), damping * second * first, rr_next, curve


def variant_moments(
    meta, total, start, near0, near1, near2, near3, sent, table, g_high, g_low, ext
):
    part, has_before, has_after = meta[0], meta[1], meta[2]
    n = 2 * BS
    first_row = pl.multiple_of(part * n, n)
    mine = start[pl.ds(first_row, n), :]
    before8 = start[pl.ds(pl.multiple_of(jnp.maximum(first_row - 8, 0), 8), 8), :]
    after8 = start[pl.ds(pl.multiple_of(jnp.minimum(first_row + n, 4 * n - 8), 8), 8), :]
    at_low, at_high = part == 0, part == 3
    before = jnp.where(at_low, near0[1:2, :], before8[7:8, :])
    before2 = jnp.where(at_low, near0[0:1, :], before8[6:7, :])
    after = jnp.where(at_high, near0[8:9, :], after8[0:1, :])
    after2 = jnp.where(at_high, near0[9:10, :], after8[1:2, :])
    banded = band_of(mine, before, after, ext)
    data = total[2 * BS : 4 * BS, :].T
    pieces = []
    for k in range(2):
        gram = unpack(
            total[k * BS : (k + 1) * BS, :BS],
            total[k * BS : (k + 1) * BS, BS:],
            total[4 * BS + k : 4 * BS + k + 1, :BS],
        )
        g_high[k], g_low[k] = split(gram)
        rows = slice(k * BS, (k + 1) * BS)
        pieces.append(
            data[rows]
            - times(mine[rows], g_high[k], g_low[k])
            - ridge_weight * mine[rows]
            - smooth_weight * banded[rows]
        )
    value = jnp.concatenate(pieces, axis=0)
    low = near0[2:3, :] + near1[2:3, :] + near2[2:3, :] + near3[2:3, :]
    high = near0[10:11, :] + near1[10:11, :] + near2[10:11, :] + near3[10:11, :]
    low = jnp.where(at_low, low, resid_unit * total[4 * BS + 2 : 4 * BS + 3, :])
    high = jnp.where(at_high, high, resid_unit * total[4 * BS + 3 : 4 * BS + 4, :])
    low = low - ridge_weight * before - smooth_weight * (2.0 * before - before2 - mine[0:1, :])
    high = high - ridge_weight * after - smooth_weight * (2.0 * after - after2 - mine[n - 1 : n, :])
    zero = jnp.zeros((1, R), f32)
    low = jnp.where(has_before == 1, low, zero)
    high = jnp.where(has_after == 1, high, zero)

    def operator(values, banded):
        data = [times(values[k * BS : (k + 1) * BS], g_high[k], g_low[k]) for k in range(2)]
        return jnp.concatenate(data, axis=0) + ridge_weight * values + smooth_weight * banded

    first = damping * operator(value, band_of(value, low, high, ext))
    second = damping * operator(first, band_of(first, zero, zero, ext))
    rr, ra = total_of(value * value), total_of(value * first)
    aa, aaa = total_of(first * first), total_of(first * second)
    near, far, rr_next, curve = curve_of(rr, ra, aa, aaa)
    good = (ra > 0.0) & (rr_next > 1e-3 * rr) & (curve > 0.0) & (far > 0.0)
    on_start = jnp.where(good, 1.0, 0.0)
    near = jnp.where(good, near, 0.0)
    far = jnp.where(good, far, -1.0)
    guess = on_start * mine + near * value - far * first
    peak_value, peak_guess = largest(value), largest(guess)
    unit_value = jnp.maximum(peak_value, 1e-30) / 16384.0
    unit_guess = jnp.maximum(peak_guess, 1e-30) / 16384.0
    sent[0] = value / unit_value
    sent[1] = guess / unit_guess
    line = as_row(
        [rr, ra, aa, aaa, peak_value, largest(first), on_start, near, far, unit_value, unit_guess]
    )
    five = jnp.concatenate(
        [
            line[0:1, :],
            first[0:1, :BS],
            first[0:1, BS:],
            first[n - 1 : n, :BS],
            first[n - 1 : n, BS:],
        ],
        axis=0,
    )
    forty = jnp.concatenate([five] * 8, axis=0)
    for k in range(table.shape[0] // 40):
        table[40 * k : 40 * (k + 1), :] = forty


def new_variants(
    meta, ids, table, start, pieces, tiles_hbm, new, rounded, scales, dense, tiles, sem
):
    me, core, slab = meta[0], meta[1], meta[2]
    load = pltpu.make_async_copy(tiles_hbm.at[0, 0], tiles, sem)
    load.start()

    @pl.when(core == 1)
    def _():
        dense[...] = jnp.zeros_like(dense)

    parts = table.shape[0] // 5
    lines = table[pl.ds(0, parts, stride=5), :]
    sums = jnp.sum(lines, axis=0, keepdims=True)
    peaks = jnp.max(lines, axis=0, keepdims=True)
    across = sum(
        table[pl.ds(3 + half, parts - 1, stride=5), :] * table[pl.ds(6 + half, parts - 1, stride=5), :]
        for half in range(2)
    )
    rr, ra, aa, aaa = (sums[:, k : k + 1] for k in range(4))
    on_resid, on_applied, _, _ = curve_of(rr, ra, aa, aaa - 2.0 * damping * smooth_weight * total_of(across))
    n = 2 * BS
    for k in range(4):
        owner = lax.rem(me - k + 4, 4)
        rows = pl.ds(pl.multiple_of(owner * n, n), n)
        line = table[pl.ds((slab * 4 + owner) * 5, 1), :]
        on_start, near, far, unit_value, unit_guess = (line[:, j : j + 1] for j in range(6, 11))
        share = on_applied / far
        value = (
            (1.0 - share * on_start) * start[rows, :]
            + ((on_resid - share * near) * unit_value) * pieces[k, 0]
            + (share * unit_guess) * pieces[k, 1]
        )
        new[rows, :] = value
        rounded[rows, :] = value.astype(bf16)
    top = jnp.abs(on_resid) * peaks[:, 4:5] + jnp.abs(on_applied) * peaks[:, 5:6] + 1.5
    scale_e = 30000.0 / (2.0 * 6.0 * COLS * BS * top)
    scale_h = 30000.0 / (2.0 * COLS * BS * top * top)
    scales[...] = as_row([scale_e, scale_h, 1.0 / scale_e, 1.0 / scale_h])
    load.wait()

    @pl.when(core == 1)
    def _():
        fill(ids, tiles, dense)


def tile_sums(scale, dense, rounded, pay):
    for r in range(ROWS):
        product = jnp.dot(
            dense[r * BS : (r + 1) * BS, :], rounded[...], preferred_element_type=f32
        )
        pay[r, :BS, :] = scale * product[:, :BS]
        pay[r, BS : 2 * BS, :] = scale * product[:, BS:]
        pay[r, 2 * BS :, :] = jnp.zeros((PAY_H - 2 * BS, BS), f32)


def gram_sums(scale, mask, rounded, pay, grams, diags):
    for c in range(COLS):
        block = rounded[c * BS : (c + 1) * BS, :]
        turned = block.astype(f32).T.astype(bf16)
        gram = scale * jnp.dot(turned, block, preferred_element_type=f32)
        mixed, cross, diag = pack(gram)
        grams[c, :, :BS] = mixed
        grams[c, :, BS:] = cross
        diags[c : c + 1, :] = diag
    lines = lax.broadcasted_iota(jnp.int32, (PAY_H - 2 * BS, BS), 0)
    for r in range(ROWS):
        weights = [mask[r * COLS + c] for c in range(COLS)]
        for piece in range(4):
            rows = slice(piece * 32, (piece + 1) * 32)
            total = weights[0] * grams[0, rows, :]
            for c in range(1, COLS):
                total += weights[c] * grams[c, rows, :]
            pay[r, rows, :] = total[:, :BS]
            pay[r, BS + piece * 32 : BS + (piece + 1) * 32, :] = total[:, BS:]
        total = weights[0] * diags[0:1, :]
        for c in range(1, COLS):
            total += weights[c] * diags[c : c + 1, :]
        pay[r, 2 * BS :, :] = jnp.where(lines == 0, total, 0.0)


def sums_to_send(meta, mask, scales, dense, rounded, new, pay, new_hbm, grams, diags, sem):
    keep = pltpu.make_async_copy(new, new_hbm, sem)
    keep.start()

    @pl.when(meta[1] == 1)
    def _():
        tile_sums(scales[0:1, 0:1], dense, rounded, pay)

    @pl.when(meta[1] == 0)
    def _():
        gram_sums(scales[0:1, 1:2], mask, rounded, pay, grams, diags)

    keep.wait()


def sums_to_keep(meta, ids, mask, scales, rounded, tiles_hbm, pay, dense, tiles, grams, diags, sems):
    @pl.when(meta[1] == 0)
    def _():
        quarter = NB // 4
        loads = [
            pltpu.make_async_copy(
                tiles_hbm.at[0, 0, pl.ds(k * quarter, quarter)],
                tiles.at[pl.ds(k * quarter, quarter)],
                sems.at[k],
            )
            for k in range(4)
        ]
        for load in loads:
            load.start()
        dense[...] = jnp.zeros_like(dense)
        for k, load in enumerate(loads):
            load.wait()
            fill(ids, tiles, dense, begin=k * quarter, end=(k + 1) * quarter)
        tile_sums(scales[0:1, 0:1], dense, rounded, pay)

    @pl.when(meta[1] == 1)
    def _():
        gram_sums(scales[0:1, 1:2], mask, rounded, pay, grams, diags)


def exponent_of(peak):
    return jnp.clip(jnp.ceil(jnp.log2(jnp.maximum(peak, 1e-30))), -100.0, 100.0)


def pieces_of(value):
    high = value.astype(bf16).astype(f32)
    rest = (value - high) * 256.0
    middle = rest.astype(bf16).astype(f32)
    return [high, middle, (rest - middle) * 256.0]


def indiv_moments(meta, mine, theirs, start, scales, sent):
    core = meta[1]
    own, far = mine[...], theirs[...]
    data = jnp.where(core == 0, own, far) * scales[0:1, 2:3]
    packed = jnp.where(core == 0, far, own) * scales[0:1, 3:4]
    high, low = split(unpack(packed[:BS], packed[BS : 2 * BS], packed[2 * BS : 2 * BS + 1]))
    begin = start[...]
    data = jnp.concatenate([data[:BS], data[BS : 2 * BS]], axis=1)
    value = data - times(begin, high, low) - ridge_weight * begin
    first = times(value, high, low) + ridge_weight * value
    second = times(first, high, low) + ridge_weight * first
    powers = [exponent_of(largest(array)) for array in (value, first, second)]
    value, first, second = (
        array * jnp.exp2(-power) for array, power in zip((value, first, second), powers)
    )
    moments = [
        total_of(value * value),
        total_of(value * first),
        total_of(first * first),
        total_of(first * second),
    ]
    chosen = jnp.where(core == 0, value, first) * 16384.0
    sent[:BS, :] = chosen[:, :BS]
    sent[BS : 2 * BS, :] = chosen[:, BS:]
    row = as_row([part for moment in moments for part in pieces_of(moment)] + powers)
    sent[2 * BS :, :] = row


def chip_moments(lines, moments):
    def moment(k, power):
        parts = [lines[:, 3 * k + j : 3 * k + j + 1] for j in range(3)]
        value = parts[0] + parts[1] * (1.0 / 256.0) + parts[2] * (1.0 / 65536.0)
        return jnp.sum(value * power, axis=0, keepdims=True)

    one, two, three = (jnp.exp2(lines[:, j : j + 1]) for j in (12, 13, 14))
    two, three = damping * two, damping * damping * three
    moments[...] = as_row(
        [
            moment(0, one * one),
            moment(1, one * two),
            moment(2, two * two),
            moment(3, two * three),
        ]
    )


def indiv_shares(meta, lines, own, next1, next2, next3, shares):
    sums = own[0:1, :] + next1[0:1, :] + next2[0:1, :] + next3[0:1, :]
    on_resid, on_applied, _, _ = curve_of(*(sums[:, k : k + 1] for k in range(4)))
    of_resid = on_resid * jnp.exp2(lines[:, 12:13]) * (1.0 / 16384.0)
    of_applied = -on_applied * jnp.exp2(lines[:, 13:14]) * (damping / 16384.0)
    core = meta[1]
    lanes = lax.broadcasted_iota(jnp.int32, (ROWS, BS), 1)
    here = jnp.where(core == 0, of_resid, of_applied)
    there = jnp.where(core == 0, of_applied, of_resid)
    shares[...] = jnp.where(lanes == 0, here, there)


def ring(step):
    return [(k, (k + step) % 4) for k in range(4)]


def call(kernel, ins, outs, scratch=(), nbytes=1 << 20):
    def placed(shape, dtype, space):
        if space == pltpu.SMEM:
            return jax.ShapeDtypeStruct(shape, dtype)
        return space(shape, dtype)

    def run(*operands):
        operands = [
            pltpu.with_memory_space_constraint(x, pltpu.HBM) if space == pltpu.HBM else x
            for x, space in zip(operands, ins)
        ]
        return pl.pallas_call(
            kernel,
            out_shape=tuple(placed(*out) for out in outs),
            in_specs=[pl.BlockSpec(memory_space=space) for space in ins],
            out_specs=tuple(pl.BlockSpec(memory_space=out[2]) for out in outs),
            scratch_shapes=list(scratch),
            compiler_params=pltpu.CompilerParams(vmem_limit_bytes=VMEM_LIMIT),
            cost_estimate=pl.CostEstimate(flops=0, bytes_accessed=nbytes, transcendentals=0),
        )(*operands)

    return run


def on_device(indiv_factors, variant_factors, dosage_tiles, block_rows, block_cols, live_blocks):
    S, V, H = pltpu.SMEM, pltpu.VMEM, pltpu.HBM
    me = lax.axis_index("x")
    core = lax.axis_index("c")
    chip = lax.axis_index(CHIP)
    slab = lax.axis_index(GEN)
    slabs = 32
    swap = [(0, 1), (1, 0)]
    meta = jnp.stack([me, core, slab]).astype(jnp.int32)
    ids = jnp.concatenate([block_rows[0, 0], block_cols[0, 0], live_blocks[0]])

    big = pltpu.VMEM((NB, BS, BS), bf16)
    flags = ((ROWS * COLS,), f32, S)
    edge = ((8, R), f32, V)
    own, far, mask, upward, downward = call(
        variant_sums,
        [S, S, H, H, H, H, H],
        [((PAY_V, R), f32, V), ((3, PAY_V, R), f32, V), flags, edge, edge],
        [
            big,
            pltpu.VMEM((ROWS * BS, R), f32),
            pltpu.VMEM((ROWS * BS, COLS * BS), bf16),
            pltpu.VMEM((R, ROWS * BS), bf16),
            pltpu.VMEM((ROWS * BS, R), bf16),
            pltpu.VMEM((ROWS, BS, R), f32),
            pltpu.VMEM((ROWS, BS), f32),
            pltpu.SMEM((2, 1, NB), jnp.int32),
            pltpu.VMEM((8 * COLS, R), f32),
            pltpu.VMEM((COLS, R), f32),
            pltpu.SemaphoreType.DMA((7 + COLS,)),
        ],
        20 << 20,
    )(meta, live_blocks, block_rows, block_cols, dosage_tiles, indiv_factors, variant_factors)
    far = far.astype(f16)
    got = [lax.ppermute(far[k - 1], "x", ring(k)) for k in (1, 2, 3)]
    low = lax.ppermute(upward, GEN, [(k, k + 1) for k in range(slabs - 1)])
    high = lax.ppermute(downward, GEN, [(k + 1, k) for k in range(slabs - 1)])
    total = own + got[0].astype(f32) + got[1].astype(f32) + got[2].astype(f32)
    near = jnp.concatenate([low, high], axis=0)
    nears = [near] + [lax.ppermute(near, "x", ring(k)) for k in (1, 2, 3)]
    position = slab * 4 + me
    meta_line = jnp.stack([me, position > 0, position < 4 * slabs - 1]).astype(jnp.int32)
    row = ((8, BS), f32, V)
    sent, table = call(
        variant_moments,
        [S] + [V] * 6,
        [((2, 2 * BS, R), f32, V), ((4 * slabs * 5, BS), f32, V)],
        [
            pltpu.VMEM((2, R, R), bf16),
            pltpu.VMEM((2, R, R), bf16),
            pltpu.VMEM((2 * BS + 16, R), f32),
        ],
    )(meta_line, total, variant_factors, *nears)
    sent = sent.astype(f16)
    pieces = jnp.stack([sent] + [lax.ppermute(sent, "x", ring(k)) for k in (1, 2, 3)])
    pieces = pieces.astype(f32)
    table = lax.all_to_all(
        table.reshape(4 * slabs * 5, 1, BS), ALL, 0, 0, tiled=True
    ).reshape(4 * slabs * 5, BS)

    whole = ((ROWS * BS, COLS * BS), bf16, V)
    new, rounded, scales, dense = call(
        new_variants,
        [S, S, V, V, V, H],
        [((COLS * BS, R), f32, V), ((COLS * BS, R), bf16, V), row, whole],
        [big, pltpu.SemaphoreType.DMA],
    )(meta, ids, table, variant_factors, pieces, dosage_tiles)
    sums = ((ROWS, PAY_H, BS), f32, V)
    scratch = [pltpu.VMEM((COLS, BS, R), f32), pltpu.VMEM((COLS, BS), f32)]
    pay, variant_new = call(
        sums_to_send,
        [S, S, V, V, V, V],
        [sums, ((COLS * BS, R), f32, H)],
        scratch + [pltpu.SemaphoreType.DMA],
    )(meta, mask, scales, dense, rounded, new)
    from_other = lax.ppermute(pay.astype(f16), "c", swap)
    (pay,) = call(
        sums_to_keep,
        [S, S, S, V, V, H],
        [sums],
        [
            pltpu.VMEM((ROWS * BS, COLS * BS), bf16),
            big,
            *scratch,
            pltpu.SemaphoreType.DMA((4,)),
        ],
        8 << 20,
    )(meta, ids, mask, scales, rounded, dosage_tiles)
    of_chip = (pay + from_other.astype(f32)).astype(f16)
    arrived = lax.all_to_all(of_chip, CHIP, 0, 0)
    mine = jnp.sum(arrived.astype(f32), axis=0)
    theirs = lax.ppermute(mine, "c", swap)
    begin = lax.dynamic_slice_in_dim(indiv_factors, chip * BS, BS, 0)
    (sent,) = call(indiv_moments, [S, V, V, V, V], [((PAY_H, BS), f32, V)])(
        meta, mine, theirs, begin, scales
    )
    sent = jnp.broadcast_to(sent.astype(f16)[None], (ROWS, PAY_H, BS))
    here = lax.all_to_all(sent, CHIP, 0, 0)
    there = lax.ppermute(here, "c", swap)
    lines = here[:, 2 * BS].astype(f32)
    (moments,) = call(chip_moments, [V], [row])(lines)
    nexts = [lax.ppermute(moments, "x", ring(k)) for k in (1, 2, 3)]
    (shares,) = call(indiv_shares, [S] + [V] * 5, [((ROWS, BS), f32, V)])(
        meta, lines, moments, *nexts
    )
    def halves(array):
        return jnp.concatenate([array[:, :BS], array[:, BS : 2 * BS]], axis=2).astype(f32)

    change = (
        shares[:, 0].reshape(ROWS, 1, 1) * halves(here)
        + shares[:, 1].reshape(ROWS, 1, 1) * halves(there)
    )
    indiv_new = indiv_factors.reshape(ROWS, BS, R) + change
    return variant_new, indiv_new.reshape(ROWS * BS, R)


def solution(mesh):
    grid = np.asarray(mesh.devices).reshape(4, 4, 2, 4)
    inner = Mesh(grid, ALL)
    return jax.shard_map(
        on_device,
        mesh=inner,
        in_specs=(
            P("x", None),
            P(GEN, None),
            P(GEN, "x", None, None, None),
            P(GEN, "x", None),
            P(GEN, "x", None),
            P(GEN, "x"),
        ),
        out_specs=(P(GEN, None), P("x", None)),
        check_vma=False,
    )
```
